32 devices in a mesh: seq: 8 (over y, x, core), ctx: 4 (over z).
Axes of the slice: x: 2, y: 2, z: 4, core: 2. Of those that a mesh axis runs over, the one named last changes fastest.
Arguments:
- tokens: bfloat16 [8192, 1024], P(('seq', 'ctx')), may hold values from -6 to 6
- first_values: bfloat16 [8192, 1024], P(('seq', 'ctx')), may hold values from -6 to 6
- gain_attn: bfloat16 [1024], P(('seq', 'ctx')), may hold values from 0.099609375 to 1.8984375
- w_query: bfloat16 [1024, 1024], P(('seq', 'ctx')), may hold values from -0.1875 to 0.1875
- w_key: bfloat16 [1024, 1024], P(('seq', 'ctx')), may hold values from -0.1875 to 0.1875
- w_value: bfloat16 [1024, 1024], P(('seq', 'ctx')), may hold values from -0.1875 to 0.1875
- w_out: bfloat16 [1024, 1024], P(('seq', 'ctx')), may hold values from -2 to 2
- gain_ffn: bfloat16 [1024], P(('seq', 'ctx')), may hold values from 0.099609375 to 1.8984375
- w_gate: bfloat16 [1024, 2816], P(('seq', 'ctx')), may hold values from -0.1875 to 0.1875
- w_up: bfloat16 [1024, 2816], P(('seq', 'ctx')), may hold values from -0.1875 to 0.1875
- w_down: bfloat16 [2816, 1024], P(('seq', 'ctx')), may hold values from -0.109375 to 0.109375
- segment_start: int32 [8192], P(('seq', 'ctx')), may hold values from 0 to 1023, as said below
- cotangent: bfloat16 [8192, 1024], P(('seq', 'ctx')), may hold values from -6 to 6
Outputs:
- block_out: bfloat16 [8192, 1024], P(('seq', 'ctx'))
- grad_tokens: bfloat16 [8192, 1024], P(('seq', 'ctx'))
- grad_first_values: bfloat16 [8192, 1024], P(('seq', 'ctx'))
- grad_gain_attn: float32 [1024], P(('seq', 'ctx'))
- grad_w_query: float32 [1024, 1024], P(('seq', 'ctx'))
- grad_w_key: float32 [1024, 1024], P(('seq', 'ctx'))
- grad_w_value: float32 [1024, 1024], P(('seq', 'ctx'))
- grad_w_out: float32 [1024, 1024], P(('seq', 'ctx'))
- grad_gain_ffn: float32 [1024], P(('seq', 'ctx'))
- grad_w_gate: float32 [1024, 2816], P(('seq', 'ctx'))
- grad_w_up: float32 [1024, 2816], P(('seq', 'ctx'))
- grad_w_down: float32 [2816, 1024], P(('seq', 'ctx'))
The draws below stay inside these ranges and needn't reach their ends.
Inputs may be any that keep to these rules, and one draw needn't show every extreme that they name: `segment_start`: documents are runs of consecutive tokens inside one sequence; each token holds the place of its document's first token. In every sequence one document begins within the first 128 tokens and ends within the last 128, and the last token of every sequence begins a document of its own.
All inputs are finite; a program needn't handle non-finite values.
Results may differ from the reference program's by a relative error of at most 0.03.
Values may be sent and summed in bfloat16 or wider, within the bound.
A program may use at most 256 MiB of HBM per device.

```python
import jax
import jax.numpy as jnp
from jax import lax

D = 1024
HEADS = 16
HD = 64
FF = 2816
TOK_DEV = 256
SEQ_LEN = 1024
TOKENS = 8192


def draw_segment_start(key, part):
    key = jax.random.fold_in(key, 7)
    first_key, second_key, third_key = jax.random.split(key, 3)
    seq_count = TOKENS // SEQ_LEN
    half_block = max(TOK_DEV // 2, 1)
    begin = jax.random.randint(first_key, (seq_count, 1), 1, half_block + 1)
    finish = jax.random.randint(second_key, (seq_count, 1), SEQ_LEN - half_block, SEQ_LEN)
    position_index = jnp.arange(SEQ_LEN, dtype=jnp.int32)[None, :]
    marks = jax.random.randint(third_key, (seq_count, SEQ_LEN), 0, 48) == 0
    marks = marks & ((position_index < begin) | (position_index > finish))
    marks = marks | (position_index == 0) | (position_index == begin) | (position_index == finish) | (position_index == SEQ_LEN - 1)
    starts = lax.cummax(jnp.where(marks, position_index, 0), axis=1)
    return starts.reshape(-1).astype(jnp.int32)


def block_scale(own_key, shape, cuts, smallest, high):
    gain, own = 1.0, jax.random.fold_in(own_key, 6)
    for dim, blocks in cuts:
        heights = jnp.exp(jax.random.uniform(jax.random.fold_in(own, dim), (blocks,), jnp.float32, smallest / len(cuts), high / len(cuts)))
        gain = gain * jnp.repeat(heights, shape[dim] // blocks).reshape([-1 if axis == dim else 1 for axis in range(len(shape))])
    return gain


def scatter_about(rng, dims, deviation, limit, cuts=(), kind=jnp.bfloat16):
    values = deviation * jax.random.normal(rng, dims, jnp.float32)
    if cuts:
        values = values * block_scale(rng, dims, cuts, -0.22, 0.18)
    return jnp.clip(values, -limit, limit).astype(kind)


def setup_inputs(seed: int = 0) -> dict:
    splits = jax.random.split(jax.random.key(seed), 14)
    return {
        "tokens": scatter_about(splits[0], (TOKENS, D), 1.0, 6.0, ((0, 32),)),
        "first_values": scatter_about(splits[1], (TOKENS, D), 1.0, 6.0, ((0, 32),)),
        "gain_attn": jnp.clip(1.0 + 0.18 * jax.random.normal(splits[2], (D,), jnp.float32), 0.099609375, 1.8984375).astype(jnp.bfloat16),
        "w_query": scatter_about(splits[3], (D, D), D ** -0.5, 0.1875, ((0, 32),)),
        "w_key": scatter_about(splits[4], (D, D), D ** -0.5, 0.1875, ((0, 32),)),
        "w_value": scatter_about(splits[5], (D, D), D ** -0.5, 0.1875, ((0, 32),)),
        "w_out": scatter_about(splits[6], (D, D), (max(1, D * 8 // SEQ_LEN)) ** -0.5, 2.0, ((0, 32),)),
        "gain_ffn": jnp.clip(1.0 + 0.18 * jax.random.normal(splits[7], (D,), jnp.float32), 0.099609375, 1.8984375).astype(jnp.bfloat16),
        "w_gate": scatter_about(splits[8], (D, FF), D ** -0.5, 0.1875, ((0, 32),)),
        "w_up": scatter_about(splits[9], (D, FF), D ** -0.5, 0.1875, ((0, 32),)),
        "w_down": scatter_about(splits[10], (FF, D), FF ** -0.5, 0.109375, ((0, 32),)),
        "segment_start": draw_segment_start(jax.random.fold_in(splits[13], 71), 0),
        "cotangent": scatter_about(splits[12], (TOKENS, D), 1.0, 6.0, ((0, 32),)),
    }


norm_eps = 1e-06
masked_score = -2e+30

@jax.custom_vjp
def low(v):
    return lax.optimization_barrier(v.astype(jnp.bfloat16)).astype(jnp.float32)

@jax.custom_vjp
def low_back(v):
    return v

def low_keep(v):
    return (low(v), None)

def low_pass(kept, grad):
    return (grad,)

def back_keep(v):
    return (v, None)

def back_low(kept, grad):
    return (low(grad),)
low.defvjp(low_keep, low_pass)
low_back.defvjp(back_keep, back_low)

def matmul_high(left, right):
    return jnp.dot(left, right, precision=lax.Precision.HIGHEST, preferred_element_type=jnp.float32)

def rms_scale(features, scale_gain):
    return features * lax.rsqrt(lax.optimization_barrier(jnp.mean(features * features, axis=-1, keepdims=True)) + norm_eps) * scale_gain

def rope_angles(positions, head_size):
    half_size = head_size // 2
    frequency = 10000.0 ** (-(jnp.arange(half_size, dtype=jnp.float32) * 2.0) / head_size)
    angles = positions.astype(jnp.float32)[:, None] * frequency[None, :]
    return jnp.concatenate([angles, angles], axis=-1)

def rotate(features, angles):
    half_size = features.shape[-1] // 2
    turned = jnp.concatenate([-features[..., half_size:], features[..., :half_size]], axis=-1)
    return features * jnp.cos(angles)[:, None, :] + turned * jnp.sin(angles)[:, None, :]

def attend_block(queries, keys_all, values_all, query_start, query_index, key_start, key_index):
    scores = jnp.einsum('qhd,khd->hqk', queries, keys_all, precision=lax.Precision.HIGHEST) * HD ** (-0.5)
    scores = low_back(scores)
    allowed = (query_start[:, None] == key_start[None, :]) & (key_index[None, :] <= query_index[:, None])
    scores = jnp.where(allowed[None], scores, masked_score)
    row_top = lax.optimization_barrier(jnp.max(scores, axis=-1, keepdims=True))
    log_total = row_top + jnp.log(lax.optimization_barrier(jnp.sum(jnp.exp(scores - row_top), axis=-1, keepdims=True)))
    probability = low(jnp.exp(scores - log_total))
    return jnp.einsum('hqk,khd->qhd', probability, values_all, precision=lax.Precision.HIGHEST)

def layer_rows(token_rows, first_rows, start_rows, gain_attn, w_query, w_key, w_value, w_out, gain_ffn, w_gate, w_up, w_down):
    seq_rows = token_rows.shape[0]
    position_index = jnp.arange(seq_rows, dtype=jnp.int32)
    angles = rope_angles(position_index - start_rows, HD)
    normed = low(rms_scale(token_rows, gain_attn))
    queries = low_back(matmul_high(normed, w_query)).reshape(seq_rows, HEADS, HD)
    queries = low_back(low(rotate(queries, angles)))
    keys_rot = low_back(matmul_high(normed, w_key)).reshape(seq_rows, HEADS, HD)
    keys_rot = low_back(low(rotate(keys_rot, angles)))
    values = low_back(low(0.5 * matmul_high(normed, w_value) + 0.5 * first_rows)).reshape(seq_rows, HEADS, HD)
    block_count = seq_rows // TOK_DEV
    query_blocks = queries.reshape(block_count, TOK_DEV, HEADS, HD)
    start_blocks = start_rows.reshape(block_count, TOK_DEV)
    index_blocks = position_index.reshape(block_count, TOK_DEV)

    def one_block(inputs):
        return attend_block(inputs[0], keys_rot, values, inputs[1], inputs[2], start_rows, position_index)
    mixed = lax.map(jax.checkpoint(one_block), (query_blocks, start_blocks, index_blocks))
    attn = low_back(low(mixed.reshape(seq_rows, D)))
    resid = token_rows + low_back(matmul_high(attn, w_out))
    normed_two = low(rms_scale(resid, gain_ffn))
    gate = low_back(matmul_high(normed_two, w_gate))
    up_proj = low_back(matmul_high(normed_two, w_up))
    hidden = low(jax.nn.silu(gate) * up_proj)
    return resid + matmul_high(hidden, w_down)

def reference(tokens, first_values, gain_attn, w_query, w_key, w_value, w_out, gain_ffn, w_gate, w_up, w_down, segment_start, cotangent):
    seq_count = TOKENS // SEQ_LEN
    start_seqs = segment_start.reshape(seq_count, SEQ_LEN)

    def forward(token_rows, first_rows, gain_one, query_weight, key_weight, value_weight, out_weight, gain_two, gate_weight, up_weight, down_weight):

        def one_sequence(carry, inputs):
            result_rows = layer_rows(inputs[0], inputs[1], inputs[2], gain_one, query_weight, key_weight, value_weight, out_weight, gain_two, gate_weight, up_weight, down_weight)
            return (carry, result_rows)
        _, result = lax.scan(jax.checkpoint(one_sequence), jnp.zeros((), jnp.float32), (token_rows.reshape(seq_count, SEQ_LEN, D), first_rows.reshape(seq_count, SEQ_LEN, D), start_seqs))
        return result.reshape(TOKENS, D)
    floats = (tokens.astype(jnp.float32), first_values.astype(jnp.float32), gain_attn.astype(jnp.float32), w_query.astype(jnp.float32), w_key.astype(jnp.float32), w_value.astype(jnp.float32), w_out.astype(jnp.float32), gain_ffn.astype(jnp.float32), w_gate.astype(jnp.float32), w_up.astype(jnp.float32), w_down.astype(jnp.float32))
    block_out, pullback = jax.vjp(forward, *floats)
    grads = pullback(cotangent.astype(jnp.float32))
    return (block_out.astype(jnp.bfloat16), grads[0].astype(jnp.bfloat16), grads[1].astype(jnp.bfloat16), grads[2], grads[3], grads[4], grads[5], grads[6], grads[7], grads[8], grads[9], grads[10])
```

```python
import types

import jax
import jax.numpy as jnp
from jax import lax
from jax.experimental import pallas as pl
from jax.experimental.pallas import tpu as pltpu
from jax.sharding import PartitionSpec as P

HEADS = 16
HD = 64


norm_eps = 1e-06
masked_score = -2e30
start_score = -1e30


def rms_scale(features, scale_gain):
    return (
        features
        * lax.rsqrt(jnp.mean(features * features, axis=-1, keepdims=True) + norm_eps)
        * scale_gain
    )


def rope_angles(positions, head_size):
    half_size = head_size // 2
    frequency = 10000.0 ** (-(jnp.arange(half_size, dtype=jnp.float32) * 2.0) / head_size)
    angles = positions.astype(jnp.float32)[:, None] * frequency[None, :]
    return jnp.concatenate([angles, angles], axis=-1)


def rotate(features, angles):
    half_size = features.shape[-1] // 2
    turned = jnp.concatenate([-features[..., half_size:], features[..., :half_size]], axis=-1)
    return features * jnp.cos(angles)[:, None, :] + turned * jnp.sin(angles)[:, None, :]


def block_size(shard_rows):
    size_guess = shard_rows * max(1, 640 // shard_rows)
    return size_guess


def masked_scores(queries, keys_part, query_index, query_start, key_index, key_start, score_scale):
    scores = (
        jnp.einsum("qhd,khd->hqk", queries, keys_part, preferred_element_type=jnp.float32)
        * score_scale
    )
    allowed = (query_start[:, None] == key_start[None, :]) & (
        key_index[None, :] <= query_index[:, None]
    )
    return jnp.where(allowed[None], scores, masked_score)


def per_device(
    tokens,
    first_values,
    gain_attn,
    w_query,
    w_key,
    w_value,
    w_out,
    gain_ffn,
    w_gate,
    w_up,
    w_down,
    segment_start,
    cotangent,
):
    tok_rows, model_width = tokens.shape
    score_scale = HD ** (-0.5)
    own_weights = (gain_attn, w_query, w_key, w_value, w_out, gain_ffn, w_gate, w_up, w_down)
    full_weights = (
        lax.all_gather(own_weights[0], ("seq", "ctx"), axis=0, tiled=True),
        lax.all_gather(own_weights[1], ("seq", "ctx"), axis=0, tiled=True),
        lax.all_gather(own_weights[2], ("seq", "ctx"), axis=0, tiled=True),
        lax.all_gather(own_weights[3], ("seq", "ctx"), axis=0, tiled=True),
        lax.all_gather(own_weights[4], ("seq", "ctx"), axis=0, tiled=True),
        lax.all_gather(own_weights[5], ("seq", "ctx"), axis=0, tiled=True),
        lax.all_gather(own_weights[6], ("seq", "ctx"), axis=0, tiled=True),
        lax.all_gather(own_weights[7], ("seq", "ctx"), axis=0, tiled=True),
        lax.all_gather(own_weights[8], ("seq", "ctx"), axis=0, tiled=True),
    )
    all_starts = lax.all_gather(segment_start, "ctx", axis=0, tiled=True)
    own_index = lax.axis_index("ctx") * tok_rows + jnp.arange(tok_rows, dtype=jnp.int32)
    angles = rope_angles(own_index - segment_start, HD)
    (
        gain_one,
        query_weight,
        key_weight,
        value_weight,
        out_weight,
        gain_two,
        gate_weight,
        up_weight,
        down_weight,
    ) = full_weights
    token_float = tokens.astype(jnp.float32)
    normed = rms_scale(token_float, gain_one.astype(jnp.float32)).astype(jnp.bfloat16)
    query_raw = jnp.dot(normed, query_weight, preferred_element_type=jnp.float32).reshape(
        tok_rows, HEADS, HD
    )
    key_raw = jnp.dot(normed, key_weight, preferred_element_type=jnp.float32).reshape(
        tok_rows, HEADS, HD
    )
    queries = rotate(query_raw, angles).astype(jnp.bfloat16)
    keys_rot = rotate(key_raw, angles).astype(jnp.bfloat16)
    values = (
        0.5 * jnp.dot(normed, value_weight, preferred_element_type=jnp.float32)
        + 0.5 * first_values.astype(jnp.float32)
    ).astype(jnp.bfloat16)
    values_heads = values.reshape(tok_rows, HEADS, HD)
    keys_flat = keys_rot.reshape(tok_rows, model_width)
    forward_init = (
        jnp.full((HEADS, tok_rows), start_score, jnp.float32),
        jnp.zeros((HEADS, tok_rows), jnp.float32),
        jnp.zeros((HEADS, tok_rows, HD), jnp.float32),
    )
    running = forward_init
    key_piece = lax.all_gather(keys_flat, "ctx", axis=0, tiled=True)
    value_piece = lax.all_gather(values, "ctx", axis=0, tiled=True)
    piece_rows = key_piece.shape[0]
    size_now = block_size(tok_rows)
    block_count = piece_rows // size_now
    key_blocks = key_piece.reshape(block_count, size_now, HEADS, HD)
    value_blocks = value_piece.reshape(block_count, size_now, HEADS, HD)
    block_starts = jnp.arange(block_count, dtype=jnp.int32) * size_now

    def forward_one_block(partial_value, inputs):
        key_block, value_block, block_start = inputs
        key_index = block_start + jnp.arange(size_now, dtype=jnp.int32)
        key_start = lax.dynamic_slice_in_dim(all_starts, block_start, size_now)
        run_max, run_sum, accum_out = partial_value
        scores = masked_scores(
            queries, key_block, own_index, segment_start, key_index, key_start, score_scale
        )
        new_max = jnp.maximum(run_max, jnp.max(scores, axis=-1))
        weights = jnp.exp(scores - new_max[..., None])
        factor = jnp.exp(run_max - new_max)
        new_sum = run_sum * factor + jnp.sum(weights, axis=-1)
        new_accum = accum_out * factor[..., None] + jnp.einsum(
            "hqk,khd->hqd",
            weights.astype(jnp.bfloat16),
            value_block,
            preferred_element_type=jnp.float32,
        )
        partial_value = (new_max, new_sum, new_accum)
        return (partial_value, None)

    running, _ = lax.scan(forward_one_block, running, (key_blocks, value_blocks, block_starts))
    run_max, run_sum, accum_out = running
    attn_heads = accum_out / run_sum[..., None]
    log_total = run_max + jnp.log(run_sum)
    attn_low = attn_heads.transpose(1, 0, 2).reshape(tok_rows, model_width).astype(jnp.bfloat16)
    resid = token_float + jnp.dot(attn_low, out_weight, preferred_element_type=jnp.float32)
    normed_two = rms_scale(resid, gain_two.astype(jnp.float32)).astype(jnp.bfloat16)
    gate = jnp.dot(normed_two, gate_weight, preferred_element_type=jnp.float32)
    up_proj = jnp.dot(normed_two, up_weight, preferred_element_type=jnp.float32)
    hidden = (jax.nn.silu(gate) * up_proj).astype(jnp.bfloat16)
    block_out = (resid + jnp.dot(hidden, down_weight, preferred_element_type=jnp.float32)).astype(
        jnp.bfloat16
    )
    grad_down = jnp.einsum("tf,td->fd", hidden, cotangent, preferred_element_type=jnp.float32)
    d_hidden = jnp.einsum("td,fd->tf", cotangent, down_weight, preferred_element_type=jnp.float32)
    silu_value, silu_back = jax.vjp(jax.nn.silu, gate)
    d_gate = silu_back(d_hidden * up_proj)[0].astype(jnp.bfloat16)
    d_up = (d_hidden * silu_value).astype(jnp.bfloat16)
    grad_gate = jnp.einsum("td,tf->df", normed_two, d_gate, preferred_element_type=jnp.float32)
    grad_up = jnp.einsum("td,tf->df", normed_two, d_up, preferred_element_type=jnp.float32)
    d_normed_two = jnp.einsum(
        "tf,df->td", d_gate, gate_weight, preferred_element_type=jnp.float32
    ) + jnp.einsum("tf,df->td", d_up, up_weight, preferred_element_type=jnp.float32)
    _, norm_two_back = jax.vjp(rms_scale, resid, gain_two.astype(jnp.float32))
    resid_part, grad_gain_two = norm_two_back(d_normed_two)
    d_resid = cotangent.astype(jnp.float32) + resid_part
    d_branch = d_resid.astype(jnp.bfloat16)
    grad_out = jnp.einsum("td,te->de", attn_low, d_branch, preferred_element_type=jnp.float32)
    d_attn = jnp.einsum(
        "te,de->td", d_branch, out_weight, preferred_element_type=jnp.float32
    ).astype(jnp.bfloat16)
    d_attn_heads = d_attn.reshape(tok_rows, HEADS, HD)
    delta_heads = jnp.sum(d_attn_heads.astype(jnp.float32).transpose(1, 0, 2) * attn_heads, axis=-1)
    all_log_total, all_delta = (
        lax.all_gather(log_total.T.astype(jnp.bfloat16), "ctx", axis=0, tiled=True).astype(
            jnp.float32
        ),
        lax.all_gather(delta_heads.T.astype(jnp.bfloat16), "ctx", axis=0, tiled=True).astype(
            jnp.float32
        ),
    )
    d_query_sum = jnp.zeros((tok_rows, HEADS, HD), jnp.float32)
    key_piece = lax.all_gather(keys_flat, "ctx", axis=0, tiled=True)
    value_piece = lax.all_gather(values, "ctx", axis=0, tiled=True)
    piece_rows = key_piece.shape[0]
    query_size_now = block_size(tok_rows)
    block_count = piece_rows // query_size_now
    key_blocks = key_piece.reshape(block_count, query_size_now, HEADS, HD)
    value_blocks = value_piece.reshape(block_count, query_size_now, HEADS, HD)
    block_starts = jnp.arange(block_count, dtype=jnp.int32) * query_size_now

    def query_one_block(partial_value, inputs):
        key_block, value_block, block_start = inputs
        key_index = block_start + jnp.arange(query_size_now, dtype=jnp.int32)
        key_start = lax.dynamic_slice_in_dim(all_starts, block_start, query_size_now)
        scores = masked_scores(
            queries, key_block, own_index, segment_start, key_index, key_start, score_scale
        )
        probability = jnp.exp(scores - log_total[..., None])
        d_prob = jnp.einsum(
            "qhd,khd->hqk", d_attn_heads, value_block, preferred_element_type=jnp.float32
        )
        d_score = (probability * (d_prob - delta_heads[..., None])).astype(jnp.bfloat16)
        partial_value = (
            partial_value
            + jnp.einsum("hqk,khd->qhd", d_score, key_block, preferred_element_type=jnp.float32)
            * score_scale
        )
        return (partial_value, None)

    d_query_sum, _ = lax.scan(
        query_one_block, d_query_sum, (key_blocks, value_blocks, block_starts)
    )
    queries_flat = queries.reshape(tok_rows, model_width)
    key_init = (
        jnp.zeros((tok_rows, HEADS, HD), jnp.float32),
        jnp.zeros((tok_rows, HEADS, HD), jnp.float32),
    )
    sums_now = key_init
    query_piece = lax.all_gather(queries_flat, "ctx", axis=0, tiled=True)
    grad_piece = lax.all_gather(d_attn, "ctx", axis=0, tiled=True)
    piece_rows = query_piece.shape[0]
    key_size_now = block_size(tok_rows)
    block_count = piece_rows // key_size_now
    query_blocks = query_piece.reshape(block_count, key_size_now, HEADS, HD)
    grad_blocks = grad_piece.reshape(block_count, key_size_now, HEADS, HD)
    block_starts = jnp.arange(block_count, dtype=jnp.int32) * key_size_now

    def key_one_block(partial_value, inputs):
        query_block, grad_block, block_start = inputs
        query_index = block_start + jnp.arange(key_size_now, dtype=jnp.int32)
        query_start = lax.dynamic_slice_in_dim(all_starts, block_start, key_size_now)
        block_total = lax.dynamic_slice_in_dim(all_log_total, block_start, key_size_now).T
        block_delta = lax.dynamic_slice_in_dim(all_delta, block_start, key_size_now).T
        d_key_sum, d_value_sum = partial_value
        scores = masked_scores(
            query_block, keys_rot, query_index, query_start, own_index, segment_start, score_scale
        )
        probability = jnp.exp(scores - block_total[..., None])
        d_prob = jnp.einsum(
            "qhd,khd->hqk", grad_block, values_heads, preferred_element_type=jnp.float32
        )
        d_score = (probability * (d_prob - block_delta[..., None])).astype(jnp.bfloat16)
        d_value_sum = d_value_sum + jnp.einsum(
            "hqk,qhd->khd",
            probability.astype(jnp.bfloat16),
            grad_block,
            preferred_element_type=jnp.float32,
        )
        d_key_sum = (
            d_key_sum
            + jnp.einsum("hqk,qhd->khd", d_score, query_block, preferred_element_type=jnp.float32)
            * score_scale
        )
        partial_value = (d_key_sum, d_value_sum)
        return (partial_value, None)

    sums_now, _ = lax.scan(key_one_block, sums_now, (query_blocks, grad_blocks, block_starts))
    d_key_rot, d_values = sums_now

    def rotate_here(features):
        return rotate(features, angles)

    _, rotate_back = jax.vjp(rotate_here, query_raw)
    d_query = (
        rotate_back(d_query_sum.astype(jnp.bfloat16).astype(jnp.float32))[0]
        .astype(jnp.bfloat16)
        .reshape(tok_rows, model_width)
    )
    d_key = (
        rotate_back(d_key_rot.astype(jnp.bfloat16).astype(jnp.float32))[0]
        .astype(jnp.bfloat16)
        .reshape(tok_rows, model_width)
    )
    d_values_low = d_values.astype(jnp.bfloat16).reshape(tok_rows, model_width)
    grad_first = (0.5 * d_values_low.astype(jnp.float32)).astype(jnp.bfloat16)
    grad_query = jnp.einsum("td,te->de", normed, d_query, preferred_element_type=jnp.float32)
    grad_key = jnp.einsum("td,te->de", normed, d_key, preferred_element_type=jnp.float32)
    grad_value = jnp.einsum("td,te->de", normed, grad_first, preferred_element_type=jnp.float32)
    d_normed = jnp.einsum("te,de->td", d_query, query_weight, preferred_element_type=jnp.float32)
    d_normed = d_normed + jnp.einsum(
        "te,de->td", d_key, key_weight, preferred_element_type=jnp.float32
    )
    d_normed = d_normed + jnp.einsum(
        "te,de->td", grad_first, value_weight, preferred_element_type=jnp.float32
    )
    _, norm_one_back = jax.vjp(rms_scale, token_float, gain_one.astype(jnp.float32))
    token_part, grad_gain_one = norm_one_back(d_normed)
    grad_tokens = (d_resid + token_part).astype(jnp.bfloat16)
    reduced = (
        lax.psum_scatter(grad_gain_one, ("seq", "ctx"), scatter_dimension=0, tiled=True),
        lax.psum_scatter(grad_query, ("seq", "ctx"), scatter_dimension=0, tiled=True),
        lax.psum_scatter(grad_key, ("seq", "ctx"), scatter_dimension=0, tiled=True),
        lax.psum_scatter(grad_value, ("seq", "ctx"), scatter_dimension=0, tiled=True),
        lax.psum_scatter(grad_out, ("seq", "ctx"), scatter_dimension=0, tiled=True),
        lax.psum_scatter(grad_gain_two, ("seq", "ctx"), scatter_dimension=0, tiled=True),
        lax.psum_scatter(grad_gate, ("seq", "ctx"), scatter_dimension=0, tiled=True),
        lax.psum_scatter(grad_up, ("seq", "ctx"), scatter_dimension=0, tiled=True),
        lax.psum_scatter(grad_down, ("seq", "ctx"), scatter_dimension=0, tiled=True),
    )
    return (
        block_out,
        grad_tokens,
        grad_first,
        reduced[0],
        reduced[1],
        reduced[2],
        reduced[3],
        reduced[4],
        reduced[5],
        reduced[6],
        reduced[7],
        reduced[8],
    )


BF = jnp.bfloat16
F32 = jnp.float32
MESH_ID = pl.DeviceIdType.MESH
QC = 768
GC = 1536
BLK = 256


def dot_nn(a, b):
    return lax.dot_general(a, b, (((1,), (0,)), ((), ())), preferred_element_type=F32)


def dot_nt(a, b):
    return lax.dot_general(a, b, (((1,), (1,)), ((), ())), preferred_element_type=F32)


def dot_tn(a, b):
    return lax.dot_general(a, b, (((0,), (0,)), ((), ())), preferred_element_type=F32)


N_SEM = 220
VMEM_LIMIT = 64 * 2**20 - 2**18

SCRATCH = dict(
    TOK=((256, 1024), BF),
    STT=((4, 8, 128), F32),
    ST=((1024, 128), F32),
    COS=((1024, 128), F32),
    SIN=((1024, 128), F32),
    FV=((1024, 256), BF),
    COT=((1024, 1024), BF),
    N1=((1024, 1024), BF),
    N2=((1024, 1024), BF),
    DB=((1024, 1024), BF),
    GA=((2, 4, 4, 16, 128), BF),
    GV=((8, 1024), F32),
    WA=((2, 4, 4, 32, QC), BF),
    WO=((2, 4, 32, 1024), BF),
    WG=((2, 4, 4, 32, GC), BF),
    WD=((2, 4, 96, 1024), BF),
    QS=((1024, 256), BF),
    KR=((1024, 256), BF),
    V=((1024, 256), BF),
    O=((1024, 256), BF),
    DA=((1024, 256), BF),
    P0=((4, 256, 256), BF),
    P1=((4, 256, 512), BF),
    P2=((4, 256, 768), BF),
    P3=((4, 256, 1024), BF),
    DQ=((1024, 256), BF),
    DK=((1024, 256), F32),
    DV=((1024, 256), F32),
    DQKV=((1024, QC), BF),
    H=((1024, 768), BF),
    DGU=((1024, GC), BF),
    RES=((256, 1024), F32),
    DRES=((256, 1024), F32),
    SSA=((2, 256, 1024), BF),
    SRA=((2, 256, 1024), BF),
    XSA=((256, 1024), BF),
    XRA=((256, 1024), BF),
    SSB=((2, 256, 1024), BF),
    SRB=((2, 256, 1024), BF),
    XSB=((256, 1024), BF),
    XRB=((256, 1024), BF),
    FF=((2, 256, 1024), F32),
    OUT=((256, 1024), BF),
    GQ=((4, 4, 32, QC), F32),
    GO=((4, 32, 1024), F32),
    GG=((4, 4, 32, GC), F32),
    GD=((4, 96, 1024), F32),
    RYQ=((4, 4, 32, QC), BF),
    RYO=((4, 32, 1024), BF),
    RYG=((4, 4, 32, GC), BF),
    RYD=((4, 96, 1024), BF),
    ZQ=((5, 4, 32, QC), BF),
    ZO=((5, 32, 1024), BF),
    ZG=((5, 4, 32, GC), BF),
    ZD=((5, 96, 1024), BF),
    GGS=((8, 1024), F32),
    GGR=((3, 8, 1024), F32),
    GGY=((8, 1024), F32),
    GGT=((8, 1024), F32),
    GGZ=((4, 8, 1024), F32),
)


def layer_kernel(*refs):
    (tok, fv, cot, stt, gt, sa, sg, wo, wd) = refs[:9]
    (o_block, o_gtok, o_gfv, o_gq, o_gg, o_go, o_gd, o_gain) = refs[9:17]
    R = types.SimpleNamespace(**dict(zip(SCRATCH, refs[17:])))
    ssem, rsem, lsem = refs[17 + len(SCRATCH) :]

    s = lax.axis_index("seq")
    z = lax.axis_index("ctx")
    y = s // 4
    j = s % 4
    x = j // 2
    k = j % 2
    ny = 1 - y
    sib = (4 * y + 2 * x + (1 - k), z)
    xp = (4 * y + 2 * (1 - x) + k, z)
    yp = (4 * ny + j, z)
    home = (4 * y + z, 2 * k + (x + z) % 2)
    away = (4 * y + 2 * ((z + j) % 2) + z // 2, j)
    at_home = (home[0] == s) & (home[1] == z)
    b_me = 2 * k + (x + z) % 2
    b_x = 2 * k + (1 - x + z) % 2
    b_s = 2 * (1 - k) + (x + z) % 2
    b_xs = 2 * (1 - k) + (1 - x + z) % 2

    counter = [0]
    pend = []

    def sems(n=1):
        first = counter[0]
        counter[0] += n
        assert counter[0] <= N_SEM
        return first

    def rows(b):
        return pl.ds(pl.multiple_of(b * BLK, BLK), BLK)

    def rc(src, dst, i, dev, r=None):
        return pltpu.make_async_remote_copy(
            src_ref=src,
            dst_ref=dst,
            send_sem=ssem.at[i],
            recv_sem=rsem.at[i if r is None else r],
            device_id=dev,
            device_id_type=MESH_ID,
        )

    def when(cond, fn):
        if cond is None:
            fn()
        else:
            pl.when(cond)(fn)

    def start(desc, cond=None, keep=True):
        when(cond, desc.start)
        if keep:
            pend.append((cond, desc))

    barrier = pltpu.get_barrier_semaphore()
    me = s * 4 + z

    def greet(i, c):
        t = (me + i) % 32
        pl.semaphore_signal(barrier, inc=1, device_id=(t // 4, t % 4), device_id_type=MESH_ID)
        return c

    lax.fori_loop(1, 32, greet, 0)
    pl.semaphore_wait(barrier, 31)

    i_tok, i_cot, i_st, i_fv = sems(), sems(), sems(4), sems(8)

    def route(src, dst, i, self_cond, dev, r=None):
        when(self_cond, pltpu.make_async_copy(src, dst, rsem.at[i if r is None else r]).start)
        start(rc(src, dst, i, dev, r), jnp.logical_not(self_cond))

    def arrive(like_src, dst, i, self_cond, dev):
        when(self_cond, pltpu.make_async_copy(like_src, dst, rsem.at[i]).wait)
        when(jnp.logical_not(self_cond), rc(dst, dst, i, dev).wait_recv)

    away_self = (away[0] == s) & (away[1] == z)
    own_x = (z + j) % 2
    b_away = z

    def arrivals_tok():
        arrive(tok, R.TOK, i_tok, at_home, home)

    def group_dev(c, jj):
        return (4 * y + c, jj)

    route(tok, R.TOK, i_tok, away_self, away)
    for c in range(4):
        self_c = (j == z) & (j == c)
        route(stt, R.STT.at[z], i_st + c, self_c, group_dev(c, j), i_st + z)

    def spread(src, buf, base, dst_index):
        for c in range(4):
            start(rc(src.at[c], dst_index, base + c, group_dev(c, z), base + j), j != c)

    i_gt, i_sa, i_sg = sems(4), sems(4), sems(4)
    l_copies = []

    def local(src, dst):
        d = pltpu.make_async_copy(src, dst, lsem.at[len(l_copies)])
        l_copies.append(d)
        d.start()
        return d

    loc_gt = local(gt, R.GA.at[y, j, z])
    for c in range(4):
        start(rc(gt, R.GA.at[y, j, z], i_gt + c, group_dev(c, z), i_gt + j), j != c)
    loc_sa = local(sa.at[j], R.WA.at[y, j, z])
    spread(sa, R.WA, i_sa, R.WA.at[y, j, z])
    loc_wo = local(wo, R.WO.at[y, z])
    for c in range(4):
        self_c = (j == z) & (j == c)
        for h in range(2):
            src = fv.at[:, pl.ds(128 * (c + 4 * h), 128)]
            dst = R.FV.at[rows(z), pl.ds(128 * h, 128)]
            route(src, dst, i_fv + 2 * c + h, self_c, group_dev(c, j), i_fv + 2 * z + h)
    loc_sg = local(sg.at[j], R.WG.at[y, j, z])
    spread(sg, R.WG, i_sg, R.WG.at[y, j, z])
    loc_wd = local(wd, R.WD.at[y, z])
    route(cot, R.COT.at[rows(b_away)], i_cot, away_self, away)

    def wait_group(base, dst_of):
        for c in range(4):
            when(j != c, rc(dst_of(c), dst_of(c), base + c, sib).wait_recv)

    class Gather:
        def __init__(self, pieces):
            self.pieces = pieces
            n = len(pieces)
            self.up, self.dn, self.ys = sems(4 * n), sems(4 * n), sems(4 * n)

        def send(self, step):
            zu, zd = z - step, z + step
            cu, cd = zu >= 0, zd <= 3
            for p, piece in enumerate(self.pieces):
                if step < 3:
                    src = piece(y, zu)
                    start(
                        rc(src, src, self.up + 4 * p + zu, (s, z + 1), self.up + 4 * p + zu),
                        cu & (z < 3),
                    )
                    src = piece(y, zd)
                    start(
                        rc(src, src, self.dn + 4 * p + zd, (s, z - 1), self.dn + 4 * p + zd),
                        cd & (z > 0),
                    )
                src = piece(y, zu)
                start(rc(src, src, self.ys + 4 * p + zu, yp), cu)
                if step > 0:
                    src = piece(y, zd)
                    start(rc(src, src, self.ys + 4 * p + zd, yp), cd)

        def recv(self, step):
            zu, zd = z - step, z + step
            for p, piece in enumerate(self.pieces):
                src = piece(y, zu)
                when(zu >= 0, rc(src, src, self.up + 4 * p + zu, (s, z)).wait_recv)
                src = piece(y, zd)
                when(zd <= 3, rc(src, src, self.dn + 4 * p + zd, (s, z)).wait_recv)

        def finish(self):
            for p, piece in enumerate(self.pieces):
                for zz in range(4):
                    src = piece(ny, zz)
                    rc(src, src, self.ys + 4 * p + zz, yp).wait_recv()

    def cols(ref):
        return lambda yy, zz: ref.at[yy, :, zz]

    def rws(ref):
        return lambda yy, zz: ref.at[yy, zz]

    g_gain = Gather([cols(R.GA)])
    g_attn = Gather([cols(R.WA), rws(R.WO)])
    g_ffn = Gather([cols(R.WG), rws(R.WD)])

    loc_gt.wait()
    wait_group(i_gt, lambda c: R.GA.at[y, c, z])
    g_gain.send(0)
    loc_sa.wait()
    loc_wo.wait()
    wait_group(i_sa, lambda c: R.WA.at[y, c, z])
    g_attn.send(0)
    for step in (1, 2, 3):
        g_gain.recv(step)
        g_gain.send(step)
        g_attn.recv(step)
        g_attn.send(step)
    loc_sg.wait()
    loc_wd.wait()
    wait_group(i_sg, lambda c: R.WG.at[y, c, z])
    g_ffn.send(0)
    g_gain.finish()
    gains = jnp.zeros((16, 128), F32)
    for yy in range(2):
        for jj in range(4):
            for zz in range(4):
                gains = gains + R.GA[yy, jj, zz].astype(F32)
    for r in range(8):
        R.GV[0:1, 128 * r : 128 * r + 128] = gains[r : r + 1, :]
        R.GV[1:2, 128 * r : 128 * r + 128] = gains[8 + r : 9 + r, :]

    class Share:
        def __init__(self, buf):
            self.buf = buf
            self.i = sems(3)

        def piece(self, b):
            return self.buf.at[rows(b)]

        def send(self):
            p = self.piece(b_me)
            start(rc(p, p, self.i, xp))
            start(rc(p, p, self.i + 1, sib))

        def forward(self):
            p = self.piece(b_x)
            rc(p, p, self.i, xp).wait_recv()
            start(rc(p, p, self.i + 2, sib))

        def wait_sib(self):
            p = self.piece(b_s)
            rc(p, p, self.i + 1, sib).wait_recv()

        def finish(self):
            p = self.piece(b_xs)
            rc(p, p, self.i + 2, sib).wait_recv()

    arrivals_tok()
    xs = R.TOK[...].astype(F32)
    rs1 = lax.rsqrt(jnp.mean(xs * xs, axis=-1, keepdims=True) + norm_eps)
    R.N1[rows(b_me), :] = (xs * rs1 * R.GV[0:1, :]).astype(BF)
    sh1 = Share(R.N1)
    sh1.send()
    for c in range(4):
        arrive(stt, R.STT.at[c], i_st + c, (j == z) & (c == z), home)
    for b in range(4):
        for r in range(2):
            row = R.STT[b, r : r + 1, :]
            R.ST[256 * b + 128 * r : 256 * b + 128 * r + 128, :] = jnp.transpose(
                jnp.broadcast_to(row, (128, 128))
            )
    lane = lax.broadcasted_iota(jnp.int32, (1, 128), 1)
    low_half = (lane % 64) < 32
    freq = jnp.exp((lane % 32).astype(F32) * (-2.0 / HD * 9.210340371976184))

    def angle_body(b, c):
        pos = (lax.broadcasted_iota(jnp.int32, (BLK, 128), 0) + b * BLK).astype(F32)
        ang = (pos - R.ST[rows(b), :]) * freq
        R.COS[rows(b), :] = jnp.cos(ang)
        R.SIN[rows(b), :] = jnp.where(low_half, -jnp.sin(ang), jnp.sin(ang))
        return c

    lax.fori_loop(0, 4, angle_body, 0)
    sh1.forward()
    g_ffn.recv(1)
    g_ffn.send(1)

    def turn(v):
        return jnp.where(low_half, pltpu.roll(v, 96, 1), pltpu.roll(v, 32, 1))

    for c in range(4):
        self_c = (j == z) & (c == z)
        for h in range(2):
            src = fv.at[:, pl.ds(128 * (j + 4 * h), 128)]
            dst = R.FV.at[rows(c), pl.ds(128 * h, 128)]
            arrive(src, dst, i_fv + 2 * c + h, self_c, home)
    g_attn.finish()
    sh1.wait_sib()
    sh1.finish()

    def qkv_body(b, c):
        raw = dot_nn(R.N1[rows(b), :], R.WA[...].reshape(1024, QC))
        cs, sn = R.COS[rows(b), :], R.SIN[rows(b), :]
        for t in range(2):
            sl = slice(128 * t, 128 * t + 128)
            q = raw[:, sl]
            R.QS[rows(b), sl] = ((q * cs + turn(q) * sn).astype(BF).astype(F32) * 0.125).astype(
                BF
            )
            kk = raw[:, 256 + 128 * t : 384 + 128 * t]
            R.KR[rows(b), sl] = (kk * cs + turn(kk) * sn).astype(BF)
        R.V[rows(b), :] = (
            0.5 * raw[:, 512:768] + 0.5 * R.FV[rows(b), :].astype(F32)
        ).astype(BF)
        return c

    lax.fori_loop(0, 4, qkv_body, 0)
    g_ffn.recv(2)
    g_ffn.send(2)

    PB = [R.P0, R.P1, R.P2, R.P3]

    def head_parts(h):
        pair = pl.ds(pl.multiple_of((h // 2) * 128, 128), 128)
        mine = ((lane // 64) == (h % 2)).astype(F32)
        return pair, mine.astype(BF), mine

    def attn_body(h, c):
        pair, low_mine, mine = head_parts(h)
        for i in range(4):
            n = BLK * (i + 1)
            q = R.QS[BLK * i : n, pair] * low_mine
            sc = dot_nt(q, R.KR[0:n, pair])
            col = lax.broadcasted_iota(jnp.int32, (BLK, n), 1)
            row = lax.broadcasted_iota(jnp.int32, (BLK, n), 0) + BLK * i
            first = R.ST[BLK * i : n, 0:1].astype(jnp.int32)
            sc = jnp.where((col >= first) & (col <= row), sc, masked_score)
            top = jnp.max(sc, axis=-1, keepdims=True)
            e = jnp.exp(sc - top)
            p = (e * (1.0 / jnp.sum(e, axis=-1, keepdims=True))).astype(BF)
            PB[i][h] = p
            o = dot_nn(p, R.V[0:n, pair]) * mine
            R.O[BLK * i : n, pair] += o.astype(BF)
        return c

    R.O[...] = jnp.zeros((1024, 256), BF)
    lax.fori_loop(0, 4, attn_body, 0)
    g_ffn.recv(3)
    g_ffn.send(3)

    class GroupSum:
        def __init__(self, bufs):
            self.ss, self.sr, self.xs, self.xr = bufs
            self.i = sems(3)

        def run(self, fn):
            ff = R.FF
            self.ss[0] = fn(b_xs).astype(BF)
            d0 = rc(self.ss.at[0], self.sr.at[0], self.i, sib)
            d0.start()
            self.ss[1] = fn(b_s).astype(BF)
            d1 = rc(self.ss.at[1], self.sr.at[1], self.i + 1, sib)
            d1.start()
            ff[0] = fn(b_x)
            d0.wait_recv()
            self.xs[...] = (ff[0] + self.sr[0].astype(F32)).astype(BF)
            d2 = rc(self.xs, self.xr, self.i + 2, xp)
            d2.start()
            ff[1] = fn(b_me)
            d1.wait_recv()
            ff[1] = ff[1] + self.sr[1].astype(F32)
            self.descs = (d0, d1, d2)

        def result(self):
            d0, d1, d2 = self.descs
            d2.wait_recv()
            out = R.FF[1] + self.xr[...].astype(F32)
            d0.wait_send()
            d1.wait_send()
            d2.wait_send()
            return out

    set_a = (R.SSA, R.SRA, R.XSA, R.XRA)
    set_b = (R.SSB, R.SRB, R.XSB, R.XRB)
    sum_attn = GroupSum(set_a)
    sum_attn.run(lambda b: dot_nn(R.O[rows(b), :], R.WO[...].reshape(256, 1024)))
    arrive(cot, R.COT.at[rows(b_me)], i_cot, at_home, home)
    sh_cot = Share(R.COT)
    sh_cot.send()
    res = R.TOK[...].astype(F32) + sum_attn.result()
    R.RES[...] = res
    rs2 = lax.rsqrt(jnp.mean(res * res, axis=-1, keepdims=True) + norm_eps)
    R.N2[rows(b_me), :] = (res * rs2 * R.GV[1:2, :]).astype(BF)
    sh2 = Share(R.N2)
    sh2.send()
    sh_cot.forward()
    sh_cot.wait_sib()
    sh_cot.finish()
    g_ffn.finish()
    sh2.forward()
    sh2.wait_sib()
    sh2.finish()

    def ffn_body(b, c):
        gu = dot_nn(R.N2[rows(b), :], R.WG[...].reshape(1024, GC))
        gate, up = gu[:, :768], gu[:, 768:]
        sig = 1.0 / (1.0 + jnp.exp(-gate))
        silu = gate * sig
        R.H[rows(b), :] = (silu * up).astype(BF)
        dh = dot_nt(R.COT[rows(b), :], R.WD[...].reshape(768, 1024))
        R.DGU[rows(b), 0:768] = (dh * up * (sig * (1.0 + gate * (1.0 - sig)))).astype(BF)
        R.DGU[rows(b), 768:1536] = (dh * silu).astype(BF)
        return c

    lax.fori_loop(0, 4, ffn_body, 0)
    sum_dn2 = GroupSum(set_a)
    sum_dn2.run(lambda b: dot_nt(R.DGU[rows(b), :], R.WG[...].reshape(1024, GC)))

    class Reduce:
        def __init__(self, g, ry, zr, is_cols):
            self.g, self.ry, self.zr = g, ry, zr
            self.is_cols = is_cols
            self.iy, self.up, self.dn = sems(), sems(5), sems(5)

        def send_y(self, sy):
            self.sy = sy
            start(rc(sy, self.ry, self.iy, yp))

        def recv_y(self):
            rc(self.ry, self.ry, self.iy, yp).wait_recv()

        def term(self, o, c):
            if self.is_cols:
                return self.g[c, o] + self.ry[c, o].astype(F32)
            return self.g[o] + self.ry[o].astype(F32)

        def slot(self, o, c):
            return self.zr.at[o, c] if self.is_cols else self.zr.at[o]

        def chunks(self):
            return range(4) if self.is_cols else range(1)

        def hop(self, o, upward):
            zr = self.zr
            if upward:
                cond, head, target = z < o, z == 0, (s, z + 1)
                slot_in, slot_out, base = o, o, self.up
            else:
                cond, head, target = z > o, z == 3, (s, z - 1)
                slot_in, base = o, self.dn
                slot_out = jnp.where(z - 1 == o, 4, o)

            def go():
                @pl.when(jnp.logical_not(head))
                def _():
                    rc(zr.at[slot_in], zr.at[slot_in], base + slot_in, (s, z)).wait_recv()
                    for c in self.chunks():
                        self.slot(o, c)[...] = (
                            self.term(o, c) + self.slot(o, c)[...].astype(F32)
                        ).astype(BF)

                @pl.when(head)
                def _():
                    for c in self.chunks():
                        self.slot(o, c)[...] = self.term(o, c).astype(BF)

                rc(zr.at[o], zr.at[slot_out], base + o, target, base + slot_out).start()

            pl.when(cond)(go)
            pend.append((cond, rc(zr.at[o], zr.at[slot_out], base + o, target, base + slot_out)))

        def last(self, put):
            zr = self.zr

            @pl.when(z > 0)
            def _():
                rc(zr.at[z], zr.at[z], self.up + z, (s, z)).wait_recv()

            @pl.when(z == 0)
            def _():
                for c in self.chunks():
                    self.slot(z, c)[...] = jnp.zeros(self.slot(z, c).shape, BF)

            @pl.when(z < 3)
            def _():
                rc(zr.at[4], zr.at[4], self.dn + 4, (s, z)).wait_recv()

            @pl.when(z == 3)
            def _():
                for c in self.chunks():
                    self.slot(4, c)[...] = jnp.zeros(self.slot(4, c).shape, BF)

            for c in self.chunks():
                put(
                    c,
                    self.term(z, c)
                    + self.slot(z, c)[...].astype(F32)
                    + self.slot(4, c)[...].astype(F32),
                )

        def chain(self, put):
            for o_up, o_dn in ((3, 0), (2, 1), (1, 2)):
                self.hop(o_up, True)
                self.hop(o_dn, False)
            self.last(put)

    def half(yy, width):
        return pl.ds(pl.multiple_of(yy * width, width), width)

    def grad_cols(left, right, red, sy):
        width = right.shape[1]
        for yy, keep in ((ny, False), (y, True)):
            for m in range(2):
                a = left[:, pl.ds(pl.multiple_of(yy * 512 + 256 * m, 256), 256)]
                val = dot_tn(a, right[...]).reshape(2, 4, 32, width)
                if keep:
                    red.g[2 * m : 2 * m + 2] = val
                else:
                    sy[2 * m : 2 * m + 2] = val.astype(BF)
            if not keep:
                red.send_y(sy)

    def grad_rows(left, right, red, sy, per):
        for yy, keep in ((ny, False), (y, True)):
            a = left[:, half(yy, 4 * per)]
            val = dot_tn(a, right[...]).reshape(4, per, 1024)
            if keep:
                red.g[...] = val
            else:
                sy[...] = val.astype(BF)
                red.send_y(sy)

    red_g = Reduce(R.GG, R.RYG, R.ZG, True)
    red_d = Reduce(R.GD, R.RYD, R.ZD, False)
    red_o = Reduce(R.GO, R.RYO, R.ZO, False)
    red_q = Reduce(R.GQ, R.RYQ, R.ZQ, True)

    dn2 = sum_dn2.result()
    res = R.RES[...]
    rs2 = lax.rsqrt(jnp.mean(res * res, axis=-1, keepdims=True) + norm_eps)
    xh = res * rs2
    gd = dn2 * R.GV[1:2, :]
    R.GGS[...] = jnp.zeros((8, 1024), F32)
    R.GGS[1:2, :] = jnp.sum(dn2 * xh, axis=0, keepdims=True)
    dres = (
        R.COT[rows(b_me), :].astype(F32)
        + rs2 * (gd - xh * jnp.mean(gd * xh, axis=-1, keepdims=True))
    )
    R.DRES[...] = dres
    R.DB[rows(b_me), :] = dres.astype(BF)
    sh3 = Share(R.DB)
    sh3.send()
    for cond, desc in pend:
        when(cond, desc.wait_send)
    pend.clear()
    sum_out = GroupSum(set_b)
    sum_out.run(lambda b: dot_nn(R.H[rows(b), :], R.WD[...].reshape(768, 1024)))
    R.OUT[...] = (R.RES[...] + sum_out.result()).astype(BF)
    i_out = sems()
    route(R.OUT, o_block, i_out, at_home, home)
    grad_rows(R.H, R.COT, red_d, R.WD.at[0], 96)
    grad_cols(R.N2, R.DGU, red_g, R.WG.at[0])
    sh3.forward()
    sh3.wait_sib()
    sh3.finish()

    def da_body(b, c):
        R.DA[rows(b), :] = dot_nt(R.DB[rows(b), :], R.WO[...].reshape(256, 1024)).astype(
            BF
        )
        return c

    lax.fori_loop(0, 4, da_body, 0)
    grad_rows(R.O, R.DB, red_o, R.WO.at[0], 32)
    red_d.recv_y()
    red_g.recv_y()

    def put_rows(ref):
        def put(c, val):
            ref[...] = val

        return put

    red_d.chain(put_rows(R.GD.at[0]))
    R.DK[...] = jnp.zeros((1024, 256), F32)
    R.DV[...] = jnp.zeros((1024, 256), F32)

    def back_body(h, c):
        pair, low_mine, mine = head_parts(h)
        for i in range(4):
            n = BLK * (i + 1)
            do = R.DA[BLK * i : n, pair] * low_mine
            q = R.QS[BLK * i : n, pair] * low_mine
            dp = dot_nt(do, R.V[0:n, pair])
            pb = PB[i][h]
            p = pb.astype(F32)
            delta = jnp.sum(p * dp, axis=-1, keepdims=True)
            ds = (p * (dp - delta)).astype(BF)
            dq = dot_nn(ds, R.KR[0:n, pair]) * (0.125 * mine)
            R.DQ[BLK * i : n, pair] += dq.astype(BF)
            R.DK[0:n, pair] += dot_tn(ds, q)
            R.DV[0:n, pair] += dot_tn(pb, do)
        return c

    R.DQ[...] = jnp.zeros((1024, 256), BF)
    lax.fori_loop(0, 4, back_body, 0)

    def dqkv_body(b, c):
        cs, sn = R.COS[rows(b), :], R.SIN[rows(b), :]
        for t in range(2):
            sl = slice(128 * t, 128 * t + 128)
            u = R.DQ[rows(b), sl].astype(F32)
            R.DQKV[rows(b), sl] = (u * cs - turn(u) * sn).astype(BF)
            u = R.DK[rows(b), sl].astype(BF).astype(F32)
            R.DQKV[rows(b), 256 + 128 * t : 384 + 128 * t] = (u * cs - turn(u) * sn).astype(BF)
        R.DQKV[rows(b), 512:768] = (
            0.5 * R.DV[rows(b), :].astype(BF).astype(F32)
        ).astype(BF)
        return c

    lax.fori_loop(0, 4, dqkv_body, 0)
    i_gf = sems(8)
    for b in range(4):
        self_b = (j == z) & (z == b)
        for h in range(2):
            src = R.DQKV.at[pl.ds(256 * b, 256), pl.ds(512 + 128 * h, 128)]
            dst = o_gfv.at[:, pl.ds(pl.multiple_of(128 * (j + 4 * h), 128), 128)]
            route(src, dst, i_gf + 2 * b + h, self_b, (4 * y + z, b), i_gf + 2 * j + h)
    sum_dn1 = GroupSum(set_a)
    sum_dn1.run(lambda b: dot_nt(R.DQKV[rows(b), :], R.WA[...].reshape(1024, QC)))
    grad_cols(R.N1, R.DQKV, red_q, R.WA.at[0])

    dn1 = sum_dn1.result()
    xs = R.TOK[...].astype(F32)
    rs1 = lax.rsqrt(jnp.mean(xs * xs, axis=-1, keepdims=True) + norm_eps)
    xh = xs * rs1
    gd = dn1 * R.GV[0:1, :]
    R.GGS[0:1, :] = jnp.sum(dn1 * xh, axis=0, keepdims=True)
    R.XSB[...] = (
        R.DRES[...] + rs1 * (gd - xh * jnp.mean(gd * xh, axis=-1, keepdims=True))
    ).astype(BF)
    i_gtok = sems()
    route(R.XSB, o_gtok, i_gtok, at_home, home)

    i_ggg, i_ggy, i_ggz = sems(4), sems(), sems(4)
    for c in range(4):
        start(
            rc(R.GGS, R.GGR.at[(j - c - 1) % 4], i_ggg + c, group_dev(c, z), i_ggg + j),
            j != c,
        )
    def put_cols(ref):
        def put(c, val):
            ref[c, 0] = val

        return put

    red_g.chain(put_cols(R.GG))
    red_o.recv_y()
    red_q.recv_y()
    for c in range(4):
        slot = R.GGR.at[(c - j - 1) % 4]
        when(j != c, rc(slot, slot, i_ggg + c, sib).wait_recv)
    R.GGT[...] = R.GGS[...] + R.GGR[0] + R.GGR[1] + R.GGR[2]
    start(rc(R.GGT, R.GGY, i_ggy, yp))
    red_o.chain(put_rows(R.GO.at[0]))
    rc(R.GGY, R.GGY, i_ggy, yp).wait_recv()
    R.GGZ[z] = R.GGT[...] + R.GGY[...]
    for c in range(4):
        start(rc(R.GGZ.at[z], R.GGZ.at[z], i_ggz + c, (s, c), i_ggz + z), z != c)
    red_q.chain(put_cols(R.GQ))

    i_rg, i_rq = sems(4), sems(4)
    outs = []

    def hand_back(g, send, out, base):
        for c in range(4):
            send[c] = g[c, 0].astype(BF)
        for c in range(4):
            start(rc(send.at[c], out.at[j], base + c, group_dev(c, z), base + j), j != c)
        d = pltpu.make_async_copy(send.at[j], out.at[j], lsem.at[10 + len(outs)])
        d.start()
        outs.append(d)

    hand_back(R.GG, R.RYG.at[0], o_gg, i_rg)
    hand_back(R.GQ, R.RYQ.at[0], o_gq, i_rq)
    for ref, out in ((R.GO, o_go), (R.GD, o_gd)):
        d = pltpu.make_async_copy(ref.at[0], out, lsem.at[10 + len(outs)])
        d.start()
        outs.append(d)
    for c in range(4):
        when(z != c, rc(R.GGZ.at[c], R.GGZ.at[c], i_ggz + c, (s, z)).wait_recv)
    R.GGY[...] = R.GGZ[0] + R.GGZ[1] + R.GGZ[2] + R.GGZ[3]
    d = pltpu.make_async_copy(R.GGY, o_gain, lsem.at[10 + len(outs)])
    d.start()
    outs.append(d)

    arrive(R.OUT, o_block, i_out, away_self, away)
    arrive(R.XSB, o_gtok, i_gtok, away_self, away)
    for c in range(4):
        self_c = (j == z) & (j == c)
        for h in range(2):
            src = R.DQKV.at[pl.ds(256 * z, 256), pl.ds(512 + 128 * h, 128)]
            dst = o_gfv.at[:, pl.ds(pl.multiple_of(128 * (c + 4 * h), 128), 128)]
            arrive(src, dst, i_gf + 2 * c + h, self_c, home)
    wait_group(i_rg, lambda c: o_gg.at[c])
    wait_group(i_rq, lambda c: o_gq.at[c])
    for d in outs:
        d.wait()
    for cond, desc in pend:
        when(cond, desc.wait_send)


def slot_map():
    r = lax.broadcasted_iota(jnp.int32, (1408, 1536), 0)
    c = lax.broadcasted_iota(jnp.int32, (1408, 1536), 1)
    return ((r // 88 == c // 96) & (r % 88 == c % 96)).astype(BF)


def fast_device(
    tokens,
    first_values,
    gain_attn,
    w_query,
    w_key,
    w_value,
    w_out,
    gain_ffn,
    w_gate,
    w_up,
    w_down,
    segment_start,
    cotangent,
):
    d = lax.axis_index("seq") * 4 + lax.axis_index("ctx")
    place = slot_map()
    sa = jnp.stack([w_query, w_key, w_value]).reshape(3, 32, 2, 4, 128)
    sa = sa.transpose(3, 1, 0, 2, 4).reshape(4, 32, QC)
    gu = jnp.stack([w_gate, w_up]).reshape(128, 1408)
    gu = dot_nn(gu, place).astype(BF).reshape(2, 32, 2, 4, 384)
    sg = gu.transpose(3, 1, 0, 2, 4).reshape(4, 32, GC)
    wd = jnp.pad(w_down, ((0, 8), (0, 0)))

    def spot(g):
        return lax.dynamic_update_slice(jnp.zeros((1024,), BF), g, (32 * d,)).reshape(8, 128)

    gt = jnp.concatenate([spot(gain_attn), spot(gain_ffn)])
    stt = jnp.pad(segment_start.astype(F32).reshape(2, 128), ((0, 6), (0, 0)))
    hbm = pl.BlockSpec(memory_space=pl.ANY)
    outs = pl.pallas_call(
        layer_kernel,
        name="layer",
        out_shape=[
            jax.ShapeDtypeStruct((256, 1024), BF),
            jax.ShapeDtypeStruct((256, 1024), BF),
            jax.ShapeDtypeStruct((256, 1024), BF),
            jax.ShapeDtypeStruct((4, 32, QC), BF),
            jax.ShapeDtypeStruct((4, 32, GC), BF),
            jax.ShapeDtypeStruct((32, 1024), F32),
            jax.ShapeDtypeStruct((96, 1024), F32),
            jax.ShapeDtypeStruct((8, 1024), F32),
        ],
        in_specs=[hbm] * 9,
        out_specs=[hbm] * 8,
        scratch_shapes=[pltpu.VMEM(shape, dtype) for shape, dtype in SCRATCH.values()]
        + [
            pltpu.SemaphoreType.DMA((N_SEM,)),
            pltpu.SemaphoreType.DMA((N_SEM,)),
            pltpu.SemaphoreType.DMA((20,)),
        ],
        compiler_params=pltpu.CompilerParams(
            collective_id=0, has_side_effects=True, vmem_limit_bytes=VMEM_LIMIT
        ),
    )(tokens, first_values, cotangent, stt, gt, sa, sg, w_out, wd)
    block_out, grad_tokens, grad_first, gq, gg, grad_out, gd, gains = outs
    gq = gq.reshape(4, 32, 3, 2, 128).transpose(2, 1, 3, 0, 4).reshape(3, 32, 1024).astype(F32)
    gg = gg.reshape(4, 32, 2, 2, 384).transpose(2, 1, 3, 0, 4).reshape(128, 1536)
    gg = dot_nt(gg, place).reshape(2, 32, 2816)
    own_gains = lax.dynamic_slice(gains, (0, 32 * d), (2, 32))
    return (
        block_out,
        grad_tokens,
        grad_first,
        own_gains[0],
        gq[0],
        gq[1],
        gq[2],
        grad_out,
        own_gains[1],
        gg[0],
        gg[1],
        gd[:88],
    )


def solution(mesh):
    fits = mesh.shape["seq"] == 8 and mesh.shape["ctx"] == 4
    return jax.shard_map(
        fast_device if fits else per_device,
        mesh=mesh,
        in_specs=(
            P(("seq", "ctx"), None),
            P(("seq", "ctx"), None),
            P(("seq", "ctx")),
            P(("seq", "ctx"), None),
            P(("seq", "ctx"), None),
            P(("seq", "ctx"), None),
            P(("seq", "ctx"), None),
            P(("seq", "ctx")),
            P(("seq", "ctx"), None),
            P(("seq", "ctx"), None),
            P(("seq", "ctx"), None),
            P(("seq", "ctx")),
            P(("seq", "ctx"), None),
        ),
        out_specs=(
            P(("seq", "ctx"), None),
            P(("seq", "ctx"), None),
            P(("seq", "ctx"), None),
            P(("seq", "ctx")),
            P(("seq", "ctx"), None),
            P(("seq", "ctx"), None),
            P(("seq", "ctx"), None),
            P(("seq", "ctx"), None),
            P(("seq", "ctx")),
            P(("seq", "ctx"), None),
            P(("seq", "ctx"), None),
            P(("seq", "ctx"), None),
        ),
        check_vma=False,
    )
```

```python
import types

import jax
import jax.numpy as jnp
from jax import lax
from jax.experimental import pallas as pl
from jax.experimental.pallas import tpu as pltpu
from jax.sharding import PartitionSpec as P

HEADS = 16
HD = 64


norm_eps = 1e-06
masked_score = -2e30
start_score = -1e30


def rms_scale(features, scale_gain):
    return (
        features
        * lax.rsqrt(jnp.mean(features * features, axis=-1, keepdims=True) + norm_eps)
        * scale_gain
    )


def rope_angles(positions, head_size):
    half_size = head_size // 2
    frequency = 10000.0 ** (-(jnp.arange(half_size, dtype=jnp.float32) * 2.0) / head_size)
    angles = positions.astype(jnp.float32)[:, None] * frequency[None, :]
    return jnp.concatenate([angles, angles], axis=-1)


def rotate(features, angles):
    half_size = features.shape[-1] // 2
    turned = jnp.concatenate([-features[..., half_size:], features[..., :half_size]], axis=-1)
    return features * jnp.cos(angles)[:, None, :] + turned * jnp.sin(angles)[:, None, :]


def block_size(shard_rows):
    size_guess = shard_rows * max(1, 640 // shard_rows)
    return size_guess


def masked_scores(queries, keys_part, query_index, query_start, key_index, key_start, score_scale):
    scores = (
        jnp.einsum("qhd,khd->hqk", queries, keys_part, preferred_element_type=jnp.float32)
        * score_scale
    )
    allowed = (query_start[:, None] == key_start[None, :]) & (
        key_index[None, :] <= query_index[:, None]
    )
    return jnp.where(allowed[None], scores, masked_score)


def per_device(
    tokens,
    first_values,
    gain_attn,
    w_query,
    w_key,
    w_value,
    w_out,
    gain_ffn,
    w_gate,
    w_up,
    w_down,
    segment_start,
    cotangent,
):
    tok_rows, model_width = tokens.shape
    score_scale = HD ** (-0.5)
    own_weights = (gain_attn, w_query, w_key, w_value, w_out, gain_ffn, w_gate, w_up, w_down)
    full_weights = (
        lax.all_gather(own_weights[0], ("seq", "ctx"), axis=0, tiled=True),
        lax.all_gather(own_weights[1], ("seq", "ctx"), axis=0, tiled=True),
        lax.all_gather(own_weights[2], ("seq", "ctx"), axis=0, tiled=True),
        lax.all_gather(own_weights[3], ("seq", "ctx"), axis=0, tiled=True),
        lax.all_gather(own_weights[4], ("seq", "ctx"), axis=0, tiled=True),
        lax.all_gather(own_weights[5], ("seq", "ctx"), axis=0, tiled=True),
        lax.all_gather(own_weights[6], ("seq", "ctx"), axis=0, tiled=True),
        lax.all_gather(own_weights[7], ("seq", "ctx"), axis=0, tiled=True),
        lax.all_gather(own_weights[8], ("seq", "ctx"), axis=0, tiled=True),
    )
    all_starts = lax.all_gather(segment_start, "ctx", axis=0, tiled=True)
    own_index = lax.axis_index("ctx") * tok_rows + jnp.arange(tok_rows, dtype=jnp.int32)
    angles = rope_angles(own_index - segment_start, HD)
    (
        gain_one,
        query_weight,
        key_weight,
        value_weight,
        out_weight,
        gain_two,
        gate_weight,
        up_weight,
        down_weight,
    ) = full_weights
    token_float = tokens.astype(jnp.float32)
    normed = rms_scale(token_float, gain_one.astype(jnp.float32)).astype(jnp.bfloat16)
    query_raw = jnp.dot(normed, query_weight, preferred_element_type=jnp.float32).reshape(
        tok_rows, HEADS, HD
    )
    key_raw = jnp.dot(normed, key_weight, preferred_element_type=jnp.float32).reshape(
        tok_rows, HEADS, HD
    )
    queries = rotate(query_raw, angles).astype(jnp.bfloat16)
    keys_rot = rotate(key_raw, angles).astype(jnp.bfloat16)
    values = (
        0.5 * jnp.dot(normed, value_weight, preferred_element_type=jnp.float32)
        + 0.5 * first_values.astype(jnp.float32)
    ).astype(jnp.bfloat16)
    values_heads = values.reshape(tok_rows, HEADS, HD)
    keys_flat = keys_rot.reshape(tok_rows, model_width)
    forward_init = (
        jnp.full((HEADS, tok_rows), start_score, jnp.float32),
        jnp.zeros((HEADS, tok_rows), jnp.float32),
        jnp.zeros((HEADS, tok_rows, HD), jnp.float32),
    )
    running = forward_init
    key_piece = lax.all_gather(keys_flat, "ctx", axis=0, tiled=True)
    value_piece = lax.all_gather(values, "ctx", axis=0, tiled=True)
    piece_rows = key_piece.shape[0]
    size_now = block_size(tok_rows)
    block_count = piece_rows // size_now
    key_blocks = key_piece.reshape(block_count, size_now, HEADS, HD)
    value_blocks = value_piece.reshape(block_count, size_now, HEADS, HD)
    block_starts = jnp.arange(block_count, dtype=jnp.int32) * size_now

    def forward_one_block(partial_value, inputs):
        key_block, value_block, block_start = inputs
        key_index = block_start + jnp.arange(size_now, dtype=jnp.int32)
        key_start = lax.dynamic_slice_in_dim(all_starts, block_start, size_now)
        run_max, run_sum, accum_out = partial_value
        scores = masked_scores(
            queries, key_block, own_index, segment_start, key_index, key_start, score_scale
        )
        new_max = jnp.maximum(run_max, jnp.max(scores, axis=-1))
        weights = jnp.exp(scores - new_max[..., None])
        factor = jnp.exp(run_max - new_max)
        new_sum = run_sum * factor + jnp.sum(weights, axis=-1)
        new_accum = accum_out * factor[..., None] + jnp.einsum(
            "hqk,khd->hqd",
            weights.astype(jnp.bfloat16),
            value_block,
            preferred_element_type=jnp.float32,
        )
        partial_value = (new_max, new_sum, new_accum)
        return (partial_value, None)

    running, _ = lax.scan(forward_one_block, running, (key_blocks, value_blocks, block_starts))
    run_max, run_sum, accum_out = running
    attn_heads = accum_out / run_sum[..., None]
    log_total = run_max + jnp.log(run_sum)
    attn_low = attn_heads.transpose(1, 0, 2).reshape(tok_rows, model_width).astype(jnp.bfloat16)
    resid = token_float + jnp.dot(attn_low, out_weight, preferred_element_type=jnp.float32)
    normed_two = rms_scale(resid, gain_two.astype(jnp.float32)).astype(jnp.bfloat16)
    gate = jnp.dot(normed_two, gate_weight, preferred_element_type=jnp.float32)
    up_proj = jnp.dot(normed_two, up_weight, preferred_element_type=jnp.float32)
    hidden = (jax.nn.silu(gate) * up_proj).astype(jnp.bfloat16)
    block_out = (resid + jnp.dot(hidden, down_weight, preferred_element_type=jnp.float32)).astype(
        jnp.bfloat16
    )
    grad_down = jnp.einsum("tf,td->fd", hidden, cotangent, preferred_element_type=jnp.float32)
    d_hidden = jnp.einsum("td,fd->tf", cotangent, down_weight, preferred_element_type=jnp.float32)
    silu_value, silu_back = jax.vjp(jax.nn.silu, gate)
    d_gate = silu_back(d_hidden * up_proj)[0].astype(jnp.bfloat16)
    d_up = (d_hidden * silu_value).astype(jnp.bfloat16)
    grad_gate = jnp.einsum("td,tf->df", normed_two, d_gate, preferred_element_type=jnp.float32)
    grad_up = jnp.einsum("td,tf->df", normed_two, d_up, preferred_element_type=jnp.float32)
    d_normed_two = jnp.einsum(
        "tf,df->td", d_gate, gate_weight, preferred_element_type=jnp.float32
    ) + jnp.einsum("tf,df->td", d_up, up_weight, preferred_element_type=jnp.float32)
    _, norm_two_back = jax.vjp(rms_scale, resid, gain_two.astype(jnp.float32))
    resid_part, grad_gain_two = norm_two_back(d_normed_two)
    d_resid = cotangent.astype(jnp.float32) + resid_part
    d_branch = d_resid.astype(jnp.bfloat16)
    grad_out = jnp.einsum("td,te->de", attn_low, d_branch, preferred_element_type=jnp.float32)
    d_attn = jnp.einsum(
        "te,de->td", d_branch, out_weight, preferred_element_type=jnp.float32
    ).astype(jnp.bfloat16)
    d_attn_heads = d_attn.reshape(tok_rows, HEADS, HD)
    delta_heads = jnp.sum(d_attn_heads.astype(jnp.float32).transpose(1, 0, 2) * attn_heads, axis=-1)
    all_log_total, all_delta = (
        lax.all_gather(log_total.T.astype(jnp.bfloat16), "ctx", axis=0, tiled=True).astype(
            jnp.float32
        ),
        lax.all_gather(delta_heads.T.astype(jnp.bfloat16), "ctx", axis=0, tiled=True).astype(
            jnp.float32
        ),
    )
    d_query_sum = jnp.zeros((tok_rows, HEADS, HD), jnp.float32)
    key_piece = lax.all_gather(keys_flat, "ctx", axis=0, tiled=True)
    value_piece = lax.all_gather(values, "ctx", axis=0, tiled=True)
    piece_rows = key_piece.shape[0]
    query_size_now = block_size(tok_rows)
    block_count = piece_rows // query_size_now
    key_blocks = key_piece.reshape(block_count, query_size_now, HEADS, HD)
    value_blocks = value_piece.reshape(block_count, query_size_now, HEADS, HD)
    block_starts = jnp.arange(block_count, dtype=jnp.int32) * query_size_now

    def query_one_block(partial_value, inputs):
        key_block, value_block, block_start = inputs
        key_index = block_start + jnp.arange(query_size_now, dtype=jnp.int32)
        key_start = lax.dynamic_slice_in_dim(all_starts, block_start, query_size_now)
        scores = masked_scores(
            queries, key_block, own_index, segment_start, key_index, key_start, score_scale
        )
        probability = jnp.exp(scores - log_total[..., None])
        d_prob = jnp.einsum(
            "qhd,khd->hqk", d_attn_heads, value_block, preferred_element_type=jnp.float32
        )
        d_score = (probability * (d_prob - delta_heads[..., None])).astype(jnp.bfloat16)
        partial_value = (
            partial_value
            + jnp.einsum("hqk,khd->qhd", d_score, key_block, preferred_element_type=jnp.float32)
            * score_scale
        )
        return (partial_value, None)

    d_query_sum, _ = lax.scan(
        query_one_block, d_query_sum, (key_blocks, value_blocks, block_starts)
    )
    queries_flat = queries.reshape(tok_rows, model_width)
    key_init = (
        jnp.zeros((tok_rows, HEADS, HD), jnp.float32),
        jnp.zeros((tok_rows, HEADS, HD), jnp.float32),
    )
    sums_now = key_init
    query_piece = lax.all_gather(queries_flat, "ctx", axis=0, tiled=True)
    grad_piece = lax.all_gather(d_attn, "ctx", axis=0, tiled=True)
    piece_rows = query_piece.shape[0]
    key_size_now = block_size(tok_rows)
    block_count = piece_rows // key_size_now
    query_blocks = query_piece.reshape(block_count, key_size_now, HEADS, HD)
    grad_blocks = grad_piece.reshape(block_count, key_size_now, HEADS, HD)
    block_starts = jnp.arange(block_count, dtype=jnp.int32) * key_size_now

    def key_one_block(partial_value, inputs):
        query_block, grad_block, block_start = inputs
        query_index = block_start + jnp.arange(key_size_now, dtype=jnp.int32)
        query_start = lax.dynamic_slice_in_dim(all_starts, block_start, key_size_now)
        block_total = lax.dynamic_slice_in_dim(all_log_total, block_start, key_size_now).T
        block_delta = lax.dynamic_slice_in_dim(all_delta, block_start, key_size_now).T
        d_key_sum, d_value_sum = partial_value
        scores = masked_scores(
            query_block, keys_rot, query_index, query_start, own_index, segment_start, score_scale
        )
        probability = jnp.exp(scores - block_total[..., None])
        d_prob = jnp.einsum(
            "qhd,khd->hqk", grad_block, values_heads, preferred_element_type=jnp.float32
        )
        d_score = (probability * (d_prob - block_delta[..., None])).astype(jnp.bfloat16)
        d_value_sum = d_value_sum + jnp.einsum(
            "hqk,qhd->khd",
            probability.astype(jnp.bfloat16),
            grad_block,
            preferred_element_type=jnp.float32,
        )
        d_key_sum = (
            d_key_sum
            + jnp.einsum("hqk,qhd->khd", d_score, query_block, preferred_element_type=jnp.float32)
            * score_scale
        )
        partial_value = (d_key_sum, d_value_sum)
        return (partial_value, None)

    sums_now, _ = lax.scan(key_one_block, sums_now, (query_blocks, grad_blocks, block_starts))
    d_key_rot, d_values = sums_now

    def rotate_here(features):
        return rotate(features, angles)

    _, rotate_back = jax.vjp(rotate_here, query_raw)
    d_query = (
        rotate_back(d_query_sum.astype(jnp.bfloat16).astype(jnp.float32))[0]
        .astype(jnp.bfloat16)
        .reshape(tok_rows, model_width)
    )
    d_key = (
        rotate_back(d_key_rot.astype(jnp.bfloat16).astype(jnp.float32))[0]
        .astype(jnp.bfloat16)
        .reshape(tok_rows, model_width)
    )
    d_values_low = d_values.astype(jnp.bfloat16).reshape(tok_rows, model_width)
    grad_first = (0.5 * d_values_low.astype(jnp.float32)).astype(jnp.bfloat16)
    grad_query = jnp.einsum("td,te->de", normed, d_query, preferred_element_type=jnp.float32)
    grad_key = jnp.einsum("td,te->de", normed, d_key, preferred_element_type=jnp.float32)
    grad_value = jnp.einsum("td,te->de", normed, grad_first, preferred_element_type=jnp.float32)
    d_normed = jnp.einsum("te,de->td", d_query, query_weight, preferred_element_type=jnp.float32)
    d_normed = d_normed + jnp.einsum(
        "te,de->td", d_key, key_weight, preferred_element_type=jnp.float32
    )
    d_normed = d_normed + jnp.einsum(
        "te,de->td", grad_first, value_weight, preferred_element_type=jnp.float32
    )
    _, norm_one_back = jax.vjp(rms_scale, token_float, gain_one.astype(jnp.float32))
    token_part, grad_gain_one = norm_one_back(d_normed)
    grad_tokens = (d_resid + token_part).astype(jnp.bfloat16)
    reduced = (
        lax.psum_scatter(grad_gain_one, ("seq", "ctx"), scatter_dimension=0, tiled=True),
        lax.psum_scatter(grad_query, ("seq", "ctx"), scatter_dimension=0, tiled=True),
        lax.psum_scatter(grad_key, ("seq", "ctx"), scatter_dimension=0, tiled=True),
        lax.psum_scatter(grad_value, ("seq", "ctx"), scatter_dimension=0, tiled=True),
        lax.psum_scatter(grad_out, ("seq", "ctx"), scatter_dimension=0, tiled=True),
        lax.psum_scatter(grad_gain_two, ("seq", "ctx"), scatter_dimension=0, tiled=True),
        lax.psum_scatter(grad_gate, ("seq", "ctx"), scatter_dimension=0, tiled=True),
        lax.psum_scatter(grad_up, ("seq", "ctx"), scatter_dimension=0, tiled=True),
        lax.psum_scatter(grad_down, ("seq", "ctx"), scatter_dimension=0, tiled=True),
    )
    return (
        block_out,
        grad_tokens,
        grad_first,
        reduced[0],
        reduced[1],
        reduced[2],
        reduced[3],
        reduced[4],
        reduced[5],
        reduced[6],
        reduced[7],
        reduced[8],
    )


BF = jnp.bfloat16
F32 = jnp.float32
MESH_ID = pl.DeviceIdType.MESH
QC = 768
GC = 1536
BLK = 256


def dot_nn(a, b):
    return lax.dot_general(a, b, (((1,), (0,)), ((), ())), preferred_element_type=F32)


def dot_nt(a, b):
    return lax.dot_general(a, b, (((1,), (1,)), ((), ())), preferred_element_type=F32)


def dot_tn(a, b):
    return lax.dot_general(a, b, (((0,), (0,)), ((), ())), preferred_element_type=F32)


N_SEM = 360
LAG = 6.5
T_D = 2.0
T_1 = 8.0
T_2 = 18.0
T_3 = 22.0
T_4 = 30.0
T_5 = 48.0
T_6 = 56.0
T_7 = 62.0
T_8 = 76.0
VMEM_LIMIT = 64 * 2**20 - 2**18

SCRATCH = dict(
    TOK=((256, 1024), BF),
    STT=((4, 8, 128), F32),
    ST=((1024, 128), F32),
    COS=((1024, 128), F32),
    SIN=((1024, 128), F32),
    FV=((1024, 256), BF),
    COT=((1024, 1024), BF),
    N1=((1024, 1024), BF),
    N2=((1024, 1024), BF),
    DB=((1024, 1024), BF),
    GAZ=((4, 16, 128), BF),
    GAS=((2, 16, 128), BF),
    GAJ=((4, 16, 128), BF),
    SYD=((4, 96, 1024), BF),
    GV=((8, 1024), F32),
    WA=((2, 4, 4, 32, QC), BF),
    WO=((2, 4, 32, 1024), BF),
    WG=((2, 4, 4, 32, GC), BF),
    WD=((2, 4, 96, 1024), BF),
    QS=((1024, 256), BF),
    KR=((1024, 256), BF),
    V=((1024, 256), BF),
    O=((1024, 256), BF),
    DA=((1024, 256), BF),
    P0=((4, 256, 256), BF),
    P1=((4, 256, 512), BF),
    P2=((4, 256, 768), BF),
    P3=((4, 256, 1024), BF),
    DQ=((1024, 256), BF),
    DK=((1024, 256), F32),
    DV=((1024, 256), F32),
    DQKV=((1024, QC), BF),
    H=((1024, 768), BF),
    DGU=((1024, GC), BF),
    RES=((256, 1024), F32),
    DRES=((256, 1024), F32),
    SSA=((2, 256, 1024), BF),
    SRA=((2, 256, 1024), BF),
    XSA=((256, 1024), BF),
    XRA=((256, 1024), BF),
    SSB=((2, 256, 1024), BF),
    SRB=((2, 256, 1024), BF),
    XSB=((256, 1024), BF),
    XRB=((256, 1024), BF),
    FF=((2, 256, 1024), F32),
    OUT=((256, 1024), BF),
    GQ=((4, 4, 32, QC), F32),
    GO=((4, 32, 1024), F32),
    GG=((4, 4, 32, GC), F32),
    GD=((4, 96, 1024), F32),
    RYQ=((4, 4, 32, QC), BF),
    RYO=((4, 32, 1024), BF),
    RYG=((4, 4, 32, GC), BF),
    RYD=((4, 96, 1024), BF),
    ZQ=((5, 4, 32, QC), BF),
    ZO=((5, 32, 1024), BF),
    ZG=((5, 4, 32, GC), BF),
    ZD=((5, 96, 1024), BF),
    GGS=((8, 1024), F32),
    GGR=((3, 8, 1024), F32),
    GGY=((8, 1024), F32),
    GGT=((8, 1024), F32),
    GGZ=((4, 8, 1024), F32),
)


def layer_kernel(*refs):
    (tok, fv, cot, stt, gt, sa, sg, wo, wd) = refs[:9]
    (o_block, o_gtok, o_gfv, o_gq, o_gg, o_go, o_gd, o_gain) = refs[9:17]
    R = types.SimpleNamespace(**dict(zip(SCRATCH, refs[17:])))
    ssem, rsem, lsem = refs[17 + len(SCRATCH) :]

    s = lax.axis_index("seq")
    z = lax.axis_index("ctx")
    y = s // 4
    j = s % 4
    x = j // 2
    k = j % 2
    ny = 1 - y
    sib = (4 * y + 2 * x + (1 - k), z)
    xp = (4 * y + 2 * (1 - x) + k, z)
    yp = (4 * ny + j, z)
    up_z, dn_z = (s, z + 1), (s, z - 1)
    column = (z + k) % 2
    crossing = x != column
    direct = x == column
    jp = 2 * (1 - x) + k

    def host(jj):
        return (4 * y + 2 * column + z // 2, jj)

    home = (4 * y + z, 2 * k + (x + z) % 2)
    at_home = (home[0] == s) & (home[1] == z)
    away = host(j)
    away_self = (away[0] == s) & (away[1] == z)
    b_me = 2 * k + (x + z) % 2
    b_x = 2 * k + (1 - x + z) % 2
    b_s = 2 * (1 - k) + (x + z) % 2
    b_xs = 2 * (1 - k) + (1 - x + z) % 2

    counters = [0, 0]
    pend = []

    def sems(n=1):
        first = counters[0]
        counters[0] += n
        assert counters[0] <= N_SEM
        return first

    def rows(b):
        return pl.ds(pl.multiple_of(b * BLK, BLK), BLK)

    def half_rows(b, h):
        return pl.ds(pl.multiple_of(b * BLK + 128 * h, 128), 128)

    def rc(src, dst, i, dev, r=None):
        return pltpu.make_async_remote_copy(
            src_ref=src,
            dst_ref=dst,
            send_sem=ssem.at[i],
            recv_sem=rsem.at[i if r is None else r],
            device_id=dev,
            device_id_type=MESH_ID,
        )

    def when(cond, fn):
        if cond is None:
            fn()
        else:
            pl.when(cond)(fn)

    def start(desc, cond=None):
        when(cond, desc.start)
        pend.append((cond, desc))

    def local(src, dst):
        d = pltpu.make_async_copy(src, dst, lsem.at[counters[1]])
        counters[1] += 1
        d.start()
        return d

    def both(p, q):
        return q if p is None else p & q

    def route(src, dst, i, self_cond, dev, r, cond=None):
        when(both(cond, self_cond), pltpu.make_async_copy(src, dst, rsem.at[r]).start)
        start(rc(src, dst, i, dev, r), both(cond, jnp.logical_not(self_cond)))

    def arrive(like_src, dst, r, self_cond):
        when(self_cond, pltpu.make_async_copy(like_src, dst, rsem.at[r]).wait)
        when(jnp.logical_not(self_cond), rc(dst, dst, r, sib).wait_recv)

    def group_dev(c, jj):
        return (4 * y + c, jj)

    barrier = pltpu.get_barrier_semaphore()
    me = s * 4 + z

    def greet(i, c):
        t = (me + i) % 32
        pl.semaphore_signal(barrier, inc=1, device_id=(t // 4, t % 4), device_id_type=MESH_ID)
        return c

    lax.fori_loop(1, 32, greet, 0)
    pl.semaphore_wait(barrier, 31)

    i_gz, i_gy, i_gj = sems(4), sems(), sems(4)
    loc_gt = local(gt, R.GAZ.at[z])
    for c in range(4):
        start(rc(gt, R.GAZ.at[z], i_gz + c, (s, c), i_gz + z), z != c)

    class Move:
        def __init__(self, src, stage, pieces, arrivals):
            self.src, self.stage, self.pieces, self.arrivals = src, stage, pieces, arrivals
            self.ix = sems(2)
            self.io, self.ir = sems(8), sems(8)

        def cross(self):
            for h in range(2):
                cut = pl.ds(128 * h, 128)
                start(rc(self.src.at[cut], self.stage.at[cut], self.ix + h, xp), crossing)

        def own(self):
            for n, (cut, dst, self_cond, dev, r) in enumerate(self.pieces(j)):
                route(self.src.at[cut], dst, self.io + n, self_cond, dev, r, direct)

        def relay(self):
            def take():
                for h in range(2):
                    part = self.stage.at[pl.ds(128 * h, 128)]
                    rc(part, part, self.ix + h, xp).wait_recv()

            pl.when(direct)(take)
            for n, (cut, dst, self_cond, dev, r) in enumerate(self.pieces(jp)):
                route(self.stage.at[cut], dst, self.ir + n, self_cond, dev, r, direct)

        def wait(self):
            for like, dst, r, self_cond in self.arrivals():
                arrive(like, dst, r, self_cond)

    last_hop_self = (z % 2 == k) & (b_me == z)

    def block_pieces(dst_at, base):
        def pieces(jj):
            dev = host(jj)
            self_cond = (dev[0] == s) & (dev[1] == z)
            return [
                (pl.ds(128 * h, 128), dst_at(z, h), self_cond, dev, base + h) for h in range(2)
            ]

        return pieces

    def block_arrivals(src, dst_at, base):
        return lambda: [
            (src.at[pl.ds(128 * h, 128)], dst_at(b_me, h), base + h, last_hop_self)
            for h in range(2)
        ]

    def tok_at(b, h):
        return R.TOK.at[pl.ds(128 * h, 128)]

    def cot_at(b, h):
        return R.COT.at[half_rows(b, h)]

    def fv_at(b, h):
        return R.FV.at[rows(b), pl.ds(128 * h, 128)]

    i_tok, i_cot, i_fv, i_st = sems(2), sems(2), sems(8), sems(4)

    def fv_pieces(jj):
        out = []
        for c in range(4):
            dev = group_dev(c, jj)
            self_cond = (dev[0] == s) & (dev[1] == z)
            for h in range(2):
                cut = (slice(None), pl.ds(128 * (c + 4 * h), 128))
                out.append((cut, fv_at(z, h), self_cond, dev, i_fv + 2 * z + h))
        return out

    def fv_arrivals():
        out = []
        for b in range(4):
            self_cond = (z % 2 == k) & (z == b) & (x == (b + k) % 2)
            for h in range(2):
                out.append((fv.at[:, pl.ds(128 * h, 128)], fv_at(b, h), i_fv + 2 * b + h, self_cond))
        return out

    m_tok = Move(tok, R.DB.at[0:256], block_pieces(tok_at, i_tok), block_arrivals(tok, tok_at, i_tok))
    m_cot = Move(cot, R.DB.at[512:768], block_pieces(cot_at, i_cot), block_arrivals(cot, cot_at, i_cot))
    m_fv = Move(fv, R.DB.at[256:512], fv_pieces, fv_arrivals)

    m_tok.cross()
    m_tok.own()
    for c in range(4):
        self_c = (j == z) & (j == c)
        route(stt, R.STT.at[z], i_st + c, self_c, group_dev(c, j), i_st + z)

    i_sa, i_sg = sems(4), sems(4)
    loc_sa = local(sa.at[j], R.WA.at[y, j, z])
    loc_wo = local(wo, R.WO.at[y, z])
    for c in range(4):
        start(rc(sa.at[c], R.WA.at[y, j, z], i_sa + c, group_dev(c, z), i_sa + j), j != c)
    loc_wd = local(wd, R.WD.at[y, z])
    loc_sg = local(sg.at[j], R.WG.at[y, j, z])
    for c in range(4):
        start(rc(sg.at[c], R.WG.at[y, j, z], i_sg + c, group_dev(c, z), i_sg + j), j != c)
    m_fv.cross()

    def wait_group(base, dst_of):
        for c in range(4):
            when(j != c, rc(dst_of(c), dst_of(c), base + c, sib).wait_recv)

    class Gather:
        def __init__(self, piece):
            self.piece = piece
            self.up, self.dn, self.ys = sems(4), sems(4), sems(4)

        def send_z(self, step):
            zu, zd = z - step, z + step
            src = self.piece(y, zu)
            start(rc(src, src, self.up + zu, up_z), (zu >= 0) & (z < 3))
            src = self.piece(y, zd)
            start(rc(src, src, self.dn + zd, dn_z), (zd <= 3) & (z > 0))

        def send_y(self, step):
            zu, zd = z - step, z + step
            src = self.piece(y, zu)
            start(rc(src, src, self.ys + zu, yp), zu >= 0)
            if step > 0:
                src = self.piece(y, zd)
                start(rc(src, src, self.ys + zd, yp), zd <= 3)

        def recv(self, step):
            zu, zd = z - step, z + step
            src = self.piece(y, zu)
            when(zu >= 0, rc(src, src, self.up + zu, sib).wait_recv)
            src = self.piece(y, zd)
            when(zd <= 3, rc(src, src, self.dn + zd, sib).wait_recv)

        def pass_on(self, step):
            self.recv(step)
            if step < 3:
                self.send_z(step)
            self.send_y(step)

        def finish(self):
            for zz in range(4):
                src = self.piece(ny, zz)
                rc(src, src, self.ys + zz, yp).wait_recv()

    g_a = Gather(lambda yy, zz: R.WA.at[yy, :, zz])
    g_o = Gather(lambda yy, zz: R.WO.at[yy, zz])
    g_d = Gather(lambda yy, zz: R.WD.at[yy, zz])
    g_g0 = Gather(lambda yy, zz: R.WG.at[yy, 0:2, zz])
    g_g1 = Gather(lambda yy, zz: R.WG.at[yy, 2:4, zz])

    loc_gt.wait()
    for c in range(4):
        slot = R.GAZ.at[c]
        when(z != c, rc(slot, slot, i_gz + c, sib).wait_recv)
    R.GAS[0] = R.GAZ[0] + R.GAZ[1] + R.GAZ[2] + R.GAZ[3]
    start(rc(R.GAS.at[0], R.GAS.at[1], i_gy, yp))

    wait_group(i_sa, lambda c: R.WA.at[y, c, z])
    loc_sa.wait()
    loc_wo.wait()
    g_a.send_z(0)
    g_a.send_y(0)
    g_o.send_z(0)
    g_o.send_y(0)

    rc(R.GAS.at[1], R.GAS.at[1], i_gy, yp).wait_recv()
    R.GAJ[j] = R.GAS[0] + R.GAS[1]
    for c in range(4):
        start(rc(R.GAJ.at[j], R.GAJ.at[j], i_gj + c, group_dev(c, z), i_gj + j), j != c)
    m_tok.relay()
    loc_wd.wait()
    g_d.send_y(0)
    wait_group(i_gj, lambda c: R.GAJ.at[c])
    gains = (R.GAJ[0] + R.GAJ[1] + R.GAJ[2] + R.GAJ[3]).astype(F32)
    for r in range(8):
        R.GV[0:1, 128 * r : 128 * r + 128] = gains[r : r + 1, :]
        R.GV[1:2, 128 * r : 128 * r + 128] = gains[8 + r : 9 + r, :]
    wait_group(i_sg, lambda c: R.WG.at[y, c, z])
    loc_sg.wait()
    g_a.pass_on(1)
    g_o.pass_on(1)
    g_g0.send_y(0)

    class Share:
        def __init__(self, buf):
            self.buf = buf
            self.i = sems(3)

        def piece(self, b):
            return self.buf.at[rows(b)]

        def send(self):
            p = self.piece(b_me)
            start(rc(p, p, self.i, xp))
            start(rc(p, p, self.i + 1, sib))

        def forward(self):
            p = self.piece(b_x)
            rc(p, p, self.i, xp).wait_recv()
            start(rc(p, p, self.i + 2, sib))

        def wait_sib(self):
            p = self.piece(b_s)
            rc(p, p, self.i + 1, sib).wait_recv()

        def finish(self):
            p = self.piece(b_xs)
            rc(p, p, self.i + 2, sib).wait_recv()

    m_tok.wait()
    xs = R.TOK[...].astype(F32)
    rs1 = lax.rsqrt(jnp.mean(xs * xs, axis=-1, keepdims=True) + norm_eps)
    R.N1[rows(b_me), :] = (xs * rs1 * R.GV[0:1, :]).astype(BF)
    sh1 = Share(R.N1)
    sh1.send()
    m_cot.cross()
    g_a.pass_on(2)
    g_o.pass_on(2)
    g_g1.send_y(0)
    m_fv.own()
    m_fv.relay()
    for g in (g_d, g_g0, g_g1):
        g.send_z(0)
    for c in range(4):
        arrive(stt, R.STT.at[c], i_st + c, (j == z) & (c == z))
    for b in range(4):
        for r in range(2):
            row = R.STT[b, r : r + 1, :]
            R.ST[256 * b + 128 * r : 256 * b + 128 * r + 128, :] = jnp.transpose(
                jnp.broadcast_to(row, (128, 128))
            )
    lane = lax.broadcasted_iota(jnp.int32, (1, 128), 1)
    low_half = (lane % 64) < 32
    freq = jnp.exp((lane % 32).astype(F32) * (-2.0 / HD * 9.210340371976184))

    def angle_body(b, c):
        pos = (lax.broadcasted_iota(jnp.int32, (BLK, 128), 0) + b * BLK).astype(F32)
        ang = (pos - R.ST[rows(b), :]) * freq
        R.COS[rows(b), :] = jnp.cos(ang)
        R.SIN[rows(b), :] = jnp.where(low_half, -jnp.sin(ang), jnp.sin(ang))
        return c

    lax.fori_loop(0, 4, angle_body, 0)
    g_a.pass_on(3)
    g_o.pass_on(3)
    sh1.forward()

    def turn(v):
        return jnp.where(low_half, pltpu.roll(v, 96, 1), pltpu.roll(v, 32, 1))

    g_a.finish()
    sh1.wait_sib()
    sh1.finish()
    m_fv.wait()

    def qkv_body(b, c):
        raw = dot_nn(R.N1[rows(b), :], R.WA[...].reshape(1024, QC))
        cs, sn = R.COS[rows(b), :], R.SIN[rows(b), :]
        for t in range(2):
            sl = slice(128 * t, 128 * t + 128)
            q = raw[:, sl]
            R.QS[rows(b), sl] = ((q * cs + turn(q) * sn).astype(BF).astype(F32) * 0.125).astype(BF)
            kk = raw[:, 256 + 128 * t : 384 + 128 * t]
            R.KR[rows(b), sl] = (kk * cs + turn(kk) * sn).astype(BF)
        R.V[rows(b), :] = (0.5 * raw[:, 512:768] + 0.5 * R.FV[rows(b), :].astype(F32)).astype(BF)
        return c

    lax.fori_loop(0, 4, qkv_body, 0)
    for g in (g_d, g_g0, g_g1):
        g.pass_on(1)
    m_cot.own()
    m_cot.relay()

    PB = [R.P0, R.P1, R.P2, R.P3]

    def head_parts(h):
        pair = pl.ds(pl.multiple_of((h // 2) * 128, 128), 128)
        mine = ((lane // 64) == (h % 2)).astype(F32)
        return pair, mine.astype(BF), mine

    def attn_body(h, c):
        pair, low_mine, mine = head_parts(h)
        for i in range(4):
            n = BLK * (i + 1)
            q = R.QS[BLK * i : n, pair] * low_mine
            sc = dot_nt(q, R.KR[0:n, pair])
            col = lax.broadcasted_iota(jnp.int32, (BLK, n), 1)
            row = lax.broadcasted_iota(jnp.int32, (BLK, n), 0) + BLK * i
            first = R.ST[BLK * i : n, 0:1].astype(jnp.int32)
            sc = jnp.where((col >= first) & (col <= row), sc, masked_score)
            top = jnp.max(sc, axis=-1, keepdims=True)
            e = jnp.exp(sc - top)
            p = (e * (1.0 / jnp.sum(e, axis=-1, keepdims=True))).astype(BF)
            PB[i][h] = p
            o = dot_nn(p, R.V[0:n, pair]) * mine
            R.O[BLK * i : n, pair] += o.astype(BF)
        return c

    R.O[...] = jnp.zeros((1024, 256), BF)
    lax.fori_loop(0, 2, attn_body, 0)
    for g in (g_d, g_g0, g_g1):
        g.pass_on(2)
    lax.fori_loop(2, 4, attn_body, 0)

    class GroupSum:
        def __init__(self, bufs):
            self.ss, self.sr, self.xs, self.xr = bufs
            self.i = sems(3)

        def run(self, fn):
            ff = R.FF
            self.ss[0] = fn(b_xs).astype(BF)
            d0 = rc(self.ss.at[0], self.sr.at[0], self.i, sib)
            d0.start()
            ff[0] = fn(b_x)
            d0.wait_recv()
            self.xs[...] = (ff[0] + self.sr[0].astype(F32)).astype(BF)
            d2 = rc(self.xs, self.xr, self.i + 2, xp)
            d2.start()
            self.ss[1] = fn(b_s).astype(BF)
            d1 = rc(self.ss.at[1], self.sr.at[1], self.i + 1, sib)
            d1.start()
            ff[1] = fn(b_me)
            d1.wait_recv()
            ff[1] = ff[1] + self.sr[1].astype(F32)
            self.descs = (d0, d1, d2)

        def result(self):
            d0, d1, d2 = self.descs
            d2.wait_recv()
            out = R.FF[1] + self.xr[...].astype(F32)
            d0.wait_send()
            d1.wait_send()
            d2.wait_send()
            return out

    set_a = (R.SSA, R.SRA, R.XSA, R.XRA)
    set_b = (R.SSB, R.SRB, R.XSB, R.XRB)
    g_o.finish()
    sum_attn = GroupSum(set_a)
    sum_attn.run(lambda b: dot_nn(R.O[rows(b), :], R.WO[...].reshape(256, 1024)))
    m_cot.wait()
    sh_cot = Share(R.COT)
    g_d.pass_on(3)
    res = R.TOK[...].astype(F32) + sum_attn.result()
    R.RES[...] = res
    rs2 = lax.rsqrt(jnp.mean(res * res, axis=-1, keepdims=True) + norm_eps)
    R.N2[rows(b_me), :] = (res * rs2 * R.GV[1:2, :]).astype(BF)
    sh2 = Share(R.N2)
    sh2.send()
    sh_cot.send()
    g_g0.pass_on(3)
    g_g1.pass_on(3)
    sh2.forward()
    sh_cot.forward()
    for g in (g_d, g_g0, g_g1):
        g.finish()
    for sh in (sh2, sh_cot):
        sh.wait_sib()
        sh.finish()

    def ffn_body(b, c):
        gu = dot_nn(R.N2[rows(b), :], R.WG[...].reshape(1024, GC))
        gate, up = gu[:, :768], gu[:, 768:]
        sig = 1.0 / (1.0 + jnp.exp(-gate))
        silu = gate * sig
        R.H[rows(b), :] = (silu * up).astype(BF)
        dh = dot_nt(R.COT[rows(b), :], R.WD[...].reshape(768, 1024))
        R.DGU[rows(b), 0:768] = (dh * up * (sig * (1.0 + gate * (1.0 - sig)))).astype(BF)
        R.DGU[rows(b), 768:1536] = (dh * silu).astype(BF)
        return c

    lax.fori_loop(0, 4, ffn_body, 0)
    for cond, desc in pend:
        when(cond, desc.wait_send)
    pend.clear()

    events = []

    class Reduce:
        def __init__(self, g, sy, ry, zr, cs):
            self.g, self.sy, self.ry, self.zr = g, sy, ry, zr
            self.cs = cs
            self.iy, self.up, self.dn = sems(4), sems(5), sems(5)

        def cut(self, ref, o):
            if self.cs is None:
                return ref.at[o]
            return ref.at[self.cs[0] : self.cs[1], o]

        def zslot(self, o):
            if self.cs is None:
                return self.zr.at[o]
            return self.zr.at[o, self.cs[0] : self.cs[1]]

        def chunks(self):
            return [None] if self.cs is None else range(*self.cs)

        def chunk(self, o, c):
            return self.zr.at[o] if c is None else self.zr.at[o, c]

        def term(self, o, c):
            at = o if c is None else (c, o)
            return self.g[at] + self.ry[at].astype(F32)

        def send_y(self):
            for o in (3, 0, 2, 1):
                start(rc(self.cut(self.sy, o), self.cut(self.ry, o), self.iy + o, yp))

        def recv_y(self, o):
            p = self.cut(self.ry, o)
            rc(p, p, self.iy + o, yp).wait_recv()

        def hop(self, o, upward, zz):
            if upward:
                head, target, base, slot_out = zz == 0, up_z, self.up, o
            else:
                head, target, base = zz == 3, dn_z, self.dn
                slot_out = 4 if zz - 1 == o else o
            d = rc(self.zslot(o), self.zslot(slot_out), base + o, target, base + slot_out)

            def go():
                if not head:
                    p = self.zslot(o)
                    rc(p, p, base + o, sib).wait_recv()
                for c in self.chunks():
                    p = self.chunk(o, c)
                    val = self.term(o, c)
                    if not head:
                        val = val + p[...].astype(F32)
                    p[...] = val.astype(BF)
                d.start()

            pl.when(z == zz)(go)
            pend.append((z == zz, d))

        def last(self, zz, put):
            def go():
                if zz > 0:
                    p = self.zslot(zz)
                    rc(p, p, self.up + zz, sib).wait_recv()
                if zz < 3:
                    p = self.zslot(4)
                    rc(p, p, self.dn + 4, sib).wait_recv()
                for c in self.chunks():
                    val = self.term(zz, c)
                    if zz > 0:
                        val = val + self.chunk(zz, c)[...].astype(F32)
                    if zz < 3:
                        val = val + self.chunk(4, c)[...].astype(F32)
                    put(c, val)

            pl.when(z == zz)(go)

        def schedule(self, t0, dt, lag, put):
            for n, o in enumerate((3, 0, 2, 1)):
                t = t0 + (n + 1) * dt
                events.append((t, lambda o=o: self.recv_y(o)))
                for zz in range(o):
                    events.append((t + 0.01 + zz * lag, lambda o=o, zz=zz: self.hop(o, True, zz)))
                for zz in range(3, o, -1):
                    events.append(
                        (t + 0.02 + (3 - zz) * lag, lambda o=o, zz=zz: self.hop(o, False, zz))
                    )
                events.append(
                    (t + 0.03 + max(o, 3 - o) * lag, lambda o=o: self.last(o, put))
                )

    def run_until(t):
        events.sort(key=lambda e: e[0])
        while events and events[0][0] <= t:
            events.pop(0)[1]()

    def half(yy, width):
        return pl.ds(pl.multiple_of(yy * width, width), width)

    def grad_cols(left, right, g, sy, yy, m, keep):
        width = right.shape[1]
        a = left[:, pl.ds(pl.multiple_of(yy * 512 + 256 * m, 256), 256)]
        val = dot_tn(a, right[...]).reshape(2, 4, 32, width)
        if keep:
            g[2 * m : 2 * m + 2] = val
        else:
            sy[2 * m : 2 * m + 2] = val.astype(BF)

    def grad_rows(left, right, g, sy, yy, per, keep):
        a = left[:, half(yy, 4 * per)]
        val = dot_tn(a, right[...]).reshape(4, per, 1024)
        if keep:
            g[...] = val
        else:
            sy[...] = val.astype(BF)

    red_d = Reduce(R.GD, R.SYD, R.RYD, R.ZD, None)
    red_g0 = Reduce(R.GG, R.WG.at[0], R.RYG, R.ZG, (0, 2))
    red_g1 = Reduce(R.GG, R.WG.at[0], R.RYG, R.ZG, (2, 4))
    red_o = Reduce(R.GO, R.WO.at[0], R.RYO, R.ZO, None)
    red_q = Reduce(R.GQ, R.WA.at[0], R.RYQ, R.ZQ, (0, 4))

    def put_rows(ref):
        def put(c, val):
            ref[...] = val

        return put

    def put_cols(ref):
        def put(c, val):
            ref[c, 0] = val

        return put

    sum_dn2 = GroupSum(set_a)
    sum_dn2.run(lambda b: dot_nt(R.DGU[rows(b), :], R.WG[...].reshape(1024, GC)))
    grad_rows(R.H, R.COT, None, R.SYD, ny, 96, False)
    red_d.send_y()
    for m, red in ((0, red_g0), (1, red_g1)):
        grad_cols(R.N2, R.DGU, None, R.WG.at[0], ny, m, False)
        red.send_y()
    grad_rows(R.H, R.COT, R.GD, None, y, 96, True)
    for m in range(2):
        grad_cols(R.N2, R.DGU, R.GG, None, y, m, True)
    red_d.schedule(T_D, 4.3, LAG, put_rows(R.GD.at[0]))
    red_g0.schedule(T_D + 4 * 4.3, 4.3, LAG, put_cols(R.GG))
    red_g1.schedule(T_D + 8 * 4.3, 4.3, LAG, put_cols(R.GG))

    dn2 = sum_dn2.result()
    res = R.RES[...]
    rs2 = lax.rsqrt(jnp.mean(res * res, axis=-1, keepdims=True) + norm_eps)
    xh = res * rs2
    gd = dn2 * R.GV[1:2, :]
    R.GGS[...] = jnp.zeros((8, 1024), F32)
    R.GGS[1:2, :] = jnp.sum(dn2 * xh, axis=0, keepdims=True)
    dres = R.COT[rows(b_me), :].astype(F32) + rs2 * (
        gd - xh * jnp.mean(gd * xh, axis=-1, keepdims=True)
    )
    R.DRES[...] = dres
    R.DB[rows(b_me), :] = dres.astype(BF)
    sh3 = Share(R.DB)
    sh3.send()
    run_until(T_1)
    sum_out = GroupSum(set_b)
    sum_out.run(lambda b: dot_nn(R.H[rows(b), :], R.WD[...].reshape(768, 1024)))
    run_until(T_2)
    sh3.forward()
    sh3.wait_sib()
    sh3.finish()

    def da_body(b, c):
        R.DA[rows(b), :] = dot_nt(R.DB[rows(b), :], R.WO[...].reshape(256, 1024)).astype(BF)
        return c

    lax.fori_loop(0, 4, da_body, 0)
    grad_rows(R.O, R.DB, None, R.WO.at[0], ny, 32, False)
    red_o.send_y()
    grad_rows(R.O, R.DB, R.GO, None, y, 32, True)
    red_o.schedule(T_D + 12 * 4.3, 1.4, LAG, put_rows(R.GO.at[0]))
    run_until(T_3)
    R.OUT[...] = (R.RES[...] + sum_out.result()).astype(BF)
    i_out = sems()
    route(R.OUT, o_block, i_out, at_home, home, i_out)
    R.DK[...] = jnp.zeros((1024, 256), F32)
    R.DV[...] = jnp.zeros((1024, 256), F32)

    def back_body(h, c):
        pair, low_mine, mine = head_parts(h)
        for i in range(4):
            n = BLK * (i + 1)
            do = R.DA[BLK * i : n, pair] * low_mine
            q = R.QS[BLK * i : n, pair] * low_mine
            dp = dot_nt(do, R.V[0:n, pair])
            pb = PB[i][h]
            p = pb.astype(F32)
            delta = jnp.sum(p * dp, axis=-1, keepdims=True)
            ds = (p * (dp - delta)).astype(BF)
            dq = dot_nn(ds, R.KR[0:n, pair]) * (0.125 * mine)
            R.DQ[BLK * i : n, pair] += dq.astype(BF)
            R.DK[0:n, pair] += dot_tn(ds, q)
            R.DV[0:n, pair] += dot_tn(pb, do)
        return c

    R.DQ[...] = jnp.zeros((1024, 256), BF)
    lax.fori_loop(0, 2, back_body, 0)
    run_until(T_4)
    lax.fori_loop(2, 4, back_body, 0)

    def dqkv_body(b, c):
        cs, sn = R.COS[rows(b), :], R.SIN[rows(b), :]
        for t in range(2):
            sl = slice(128 * t, 128 * t + 128)
            u = R.DQ[rows(b), sl].astype(F32)
            R.DQKV[rows(b), sl] = (u * cs - turn(u) * sn).astype(BF)
            u = R.DK[rows(b), sl].astype(BF).astype(F32)
            R.DQKV[rows(b), 256 + 128 * t : 384 + 128 * t] = (u * cs - turn(u) * sn).astype(BF)
        R.DQKV[rows(b), 512:768] = (0.5 * R.DV[rows(b), :].astype(BF).astype(F32)).astype(BF)
        return c

    lax.fori_loop(0, 4, dqkv_body, 0)
    sum_dn1 = GroupSum(set_a)
    sum_dn1.run(lambda b: dot_nt(R.DQKV[rows(b), :], R.WA[...].reshape(1024, QC)))
    for m in range(2):
        grad_cols(R.N1, R.DQKV, None, R.WA.at[0], ny, m, False)
    red_q.send_y()
    for m in range(2):
        grad_cols(R.N1, R.DQKV, R.GQ, None, y, m, True)
    red_q.schedule(T_D + 12 * 4.3 + 8, 4.3, LAG, put_cols(R.GQ))
    i_gf = sems(8)
    for b in range(4):
        self_b = (j == z) & (z == b)
        for h in range(2):
            src = R.DQKV.at[pl.ds(256 * b, 256), pl.ds(512 + 128 * h, 128)]
            dst = o_gfv.at[:, pl.ds(pl.multiple_of(128 * (j + 4 * h), 128), 128)]
            route(src, dst, i_gf + 2 * b + h, self_b, (4 * y + z, b), i_gf + 2 * j + h)
    run_until(T_5)

    dn1 = sum_dn1.result()
    xs = R.TOK[...].astype(F32)
    rs1 = lax.rsqrt(jnp.mean(xs * xs, axis=-1, keepdims=True) + norm_eps)
    xh = xs * rs1
    gd = dn1 * R.GV[0:1, :]
    R.GGS[0:1, :] = jnp.sum(dn1 * xh, axis=0, keepdims=True)
    R.XSB[...] = (
        R.DRES[...] + rs1 * (gd - xh * jnp.mean(gd * xh, axis=-1, keepdims=True))
    ).astype(BF)
    i_gtok = sems()
    route(R.XSB, o_gtok, i_gtok, at_home, home, i_gtok)

    i_ggg, i_ggy, i_ggz = sems(4), sems(), sems(4)
    for c in range(4):
        start(
            rc(R.GGS, R.GGR.at[(j - c - 1) % 4], i_ggg + c, group_dev(c, z), i_ggg + j), j != c
        )
    run_until(T_6)
    for c in range(4):
        slot = R.GGR.at[(c - j - 1) % 4]
        when(j != c, rc(slot, slot, i_ggg + c, sib).wait_recv)
    R.GGT[...] = R.GGS[...] + R.GGR[0] + R.GGR[1] + R.GGR[2]
    start(rc(R.GGT, R.GGY, i_ggy, yp))
    run_until(T_7)
    rc(R.GGY, R.GGY, i_ggy, yp).wait_recv()
    R.GGZ[z] = R.GGT[...] + R.GGY[...]
    for c in range(4):
        start(rc(R.GGZ.at[z], R.GGZ.at[z], i_ggz + c, (s, c), i_ggz + z), z != c)

    i_rg, i_rq = sems(4), sems(4)
    outs = []

    def hand_back(g, send, out, base):
        for c in range(4):
            send[c] = g[c, 0].astype(BF)
            start(rc(send.at[c], out.at[j], base + c, group_dev(c, z), base + j), j != c)
        outs.append(local(send.at[j], out.at[j]))

    run_until(T_8)
    hand_back(R.GG, R.RYG.at[0], o_gg, i_rg)
    outs.append(local(R.GD.at[0], o_gd))
    run_until(1e9)
    hand_back(R.GQ, R.RYQ.at[0], o_gq, i_rq)
    outs.append(local(R.GO.at[0], o_go))
    for c in range(4):
        when(z != c, rc(R.GGZ.at[c], R.GGZ.at[c], i_ggz + c, sib).wait_recv)
    R.GGY[...] = R.GGZ[0] + R.GGZ[1] + R.GGZ[2] + R.GGZ[3]
    outs.append(local(R.GGY, o_gain))

    arrive(R.OUT, o_block, i_out, away_self)
    arrive(R.XSB, o_gtok, i_gtok, away_self)
    for c in range(4):
        self_c = (j == z) & (j == c)
        for h in range(2):
            src = R.DQKV.at[pl.ds(256 * z, 256), pl.ds(512 + 128 * h, 128)]
            dst = o_gfv.at[:, pl.ds(pl.multiple_of(128 * (c + 4 * h), 128), 128)]
            arrive(src, dst, i_gf + 2 * c + h, self_c)
    wait_group(i_rg, lambda c: o_gg.at[c])
    wait_group(i_rq, lambda c: o_gq.at[c])
    for d in outs:
        d.wait()
    for cond, desc in pend:
        when(cond, desc.wait_send)


def slot_map():
    r = lax.broadcasted_iota(jnp.int32, (1408, 1536), 0)
    c = lax.broadcasted_iota(jnp.int32, (1408, 1536), 1)
    return ((r // 88 == c // 96) & (r % 88 == c % 96)).astype(BF)


def fast_device(
    tokens,
    first_values,
    gain_attn,
    w_query,
    w_key,
    w_value,
    w_out,
    gain_ffn,
    w_gate,
    w_up,
    w_down,
    segment_start,
    cotangent,
):
    d = lax.axis_index("seq") * 4 + lax.axis_index("ctx")
    place = slot_map()
    sa = jnp.stack([w_query, w_key, w_value]).reshape(3, 32, 2, 4, 128)
    sa = sa.transpose(3, 1, 0, 2, 4).reshape(4, 32, QC)
    gu = jnp.stack([w_gate, w_up]).reshape(128, 1408)
    gu = dot_nn(gu, place).astype(BF).reshape(2, 32, 2, 4, 384)
    sg = gu.transpose(3, 1, 0, 2, 4).reshape(4, 32, GC)
    wd = jnp.pad(w_down, ((0, 8), (0, 0)))

    def spot(g):
        return lax.dynamic_update_slice(jnp.zeros((1024,), BF), g, (32 * d,)).reshape(8, 128)

    gt = jnp.concatenate([spot(gain_attn), spot(gain_ffn)])
    stt = jnp.pad(segment_start.astype(F32).reshape(2, 128), ((0, 6), (0, 0)))
    hbm = pl.BlockSpec(memory_space=pl.ANY)
    outs = pl.pallas_call(
        layer_kernel,
        name="layer",
        out_shape=[
            jax.ShapeDtypeStruct((256, 1024), BF),
            jax.ShapeDtypeStruct((256, 1024), BF),
            jax.ShapeDtypeStruct((256, 1024), BF),
            jax.ShapeDtypeStruct((4, 32, QC), BF),
            jax.ShapeDtypeStruct((4, 32, GC), BF),
            jax.ShapeDtypeStruct((32, 1024), F32),
            jax.ShapeDtypeStruct((96, 1024), F32),
            jax.ShapeDtypeStruct((8, 1024), F32),
        ],
        in_specs=[hbm] * 9,
        out_specs=[hbm] * 8,
        scratch_shapes=[pltpu.VMEM(shape, dtype) for shape, dtype in SCRATCH.values()]
        + [
            pltpu.SemaphoreType.DMA((N_SEM,)),
            pltpu.SemaphoreType.DMA((N_SEM,)),
            pltpu.SemaphoreType.DMA((20,)),
        ],
        compiler_params=pltpu.CompilerParams(
            collective_id=0, has_side_effects=True, vmem_limit_bytes=VMEM_LIMIT
        ),
    )(tokens, first_values, cotangent, stt, gt, sa, sg, w_out, wd)
    block_out, grad_tokens, grad_first, gq, gg, grad_out, gd, gains = outs
    gq = gq.reshape(4, 32, 3, 2, 128).transpose(2, 1, 3, 0, 4).reshape(3, 32, 1024).astype(F32)
    gg = gg.reshape(4, 32, 2, 2, 384).transpose(2, 1, 3, 0, 4).reshape(128, 1536)
    gg = dot_nt(gg, place).reshape(2, 32, 2816)
    own_gains = lax.dynamic_slice(gains, (0, 32 * d), (2, 32))
    return (
        block_out,
        grad_tokens,
        grad_first,
        own_gains[0],
        gq[0],
        gq[1],
        gq[2],
        grad_out,
        own_gains[1],
        gg[0],
        gg[1],
        gd[:88],
    )


def solution(mesh):
    fits = mesh.shape["seq"] == 8 and mesh.shape["ctx"] == 4
    return jax.shard_map(
        fast_device if fits else per_device,
        mesh=mesh,
        in_specs=(
            P(("seq", "ctx"), None),
            P(("seq", "ctx"), None),
            P(("seq", "ctx")),
            P(("seq", "ctx"), None),
            P(("seq", "ctx"), None),
            P(("seq", "ctx"), None),
            P(("seq", "ctx"), None),
            P(("seq", "ctx")),
            P(("seq", "ctx"), None),
            P(("seq", "ctx"), None),
            P(("seq", "ctx"), None),
            P(("seq", "ctx")),
            P(("seq", "ctx"), None),
        ),
        out_specs=(
            P(("seq", "ctx"), None),
            P(("seq", "ctx"), None),
            P(("seq", "ctx"), None),
            P(("seq", "ctx")),
            P(("seq", "ctx"), None),
            P(("seq", "ctx"), None),
            P(("seq", "ctx"), None),
            P(("seq", "ctx"), None),
            P(("seq", "ctx")),
            P(("seq", "ctx"), None),
            P(("seq", "ctx"), None),
            P(("seq", "ctx"), None),
        ),
        check_vma=False,
    )
```

```python
import types

import jax
import jax.numpy as jnp
from jax import lax
from jax.experimental import pallas as pl
from jax.experimental.pallas import tpu as pltpu
from jax.sharding import PartitionSpec as P

HEADS = 16
HD = 64


norm_eps = 1e-06
masked_score = -2e30
start_score = -1e30


def rms_scale(features, scale_gain):
    return (
        features
        * lax.rsqrt(jnp.mean(features * features, axis=-1, keepdims=True) + norm_eps)
        * scale_gain
    )


def rope_angles(positions, head_size):
    half_size = head_size // 2
    frequency = 10000.0 ** (-(jnp.arange(half_size, dtype=jnp.float32) * 2.0) / head_size)
    angles = positions.astype(jnp.float32)[:, None] * frequency[None, :]
    return jnp.concatenate([angles, angles], axis=-1)


def rotate(features, angles):
    half_size = features.shape[-1] // 2
    turned = jnp.concatenate([-features[..., half_size:], features[..., :half_size]], axis=-1)
    return features * jnp.cos(angles)[:, None, :] + turned * jnp.sin(angles)[:, None, :]


def block_size(shard_rows):
    size_guess = shard_rows * max(1, 640 // shard_rows)
    return size_guess


def masked_scores(queries, keys_part, query_index, query_start, key_index, key_start, score_scale):
    scores = (
        jnp.einsum("qhd,khd->hqk", queries, keys_part, preferred_element_type=jnp.float32)
        * score_scale
    )
    allowed = (query_start[:, None] == key_start[None, :]) & (
        key_index[None, :] <= query_index[:, None]
    )
    return jnp.where(allowed[None], scores, masked_score)


def per_device(
    tokens,
    first_values,
    gain_attn,
    w_query,
    w_key,
    w_value,
    w_out,
    gain_ffn,
    w_gate,
    w_up,
    w_down,
    segment_start,
    cotangent,
):
    tok_rows, model_width = tokens.shape
    score_scale = HD ** (-0.5)
    own_weights = (gain_attn, w_query, w_key, w_value, w_out, gain_ffn, w_gate, w_up, w_down)
    full_weights = (
        lax.all_gather(own_weights[0], ("seq", "ctx"), axis=0, tiled=True),
        lax.all_gather(own_weights[1], ("seq", "ctx"), axis=0, tiled=True),
        lax.all_gather(own_weights[2], ("seq", "ctx"), axis=0, tiled=True),
        lax.all_gather(own_weights[3], ("seq", "ctx"), axis=0, tiled=True),
        lax.all_gather(own_weights[4], ("seq", "ctx"), axis=0, tiled=True),
        lax.all_gather(own_weights[5], ("seq", "ctx"), axis=0, tiled=True),
        lax.all_gather(own_weights[6], ("seq", "ctx"), axis=0, tiled=True),
        lax.all_gather(own_weights[7], ("seq", "ctx"), axis=0, tiled=True),
        lax.all_gather(own_weights[8], ("seq", "ctx"), axis=0, tiled=True),
    )
    all_starts = lax.all_gather(segment_start, "ctx", axis=0, tiled=True)
    own_index = lax.axis_index("ctx") * tok_rows + jnp.arange(tok_rows, dtype=jnp.int32)
    angles = rope_angles(own_index - segment_start, HD)
    (
        gain_one,
        query_weight,
        key_weight,
        value_weight,
        out_weight,
        gain_two,
        gate_weight,
        up_weight,
        down_weight,
    ) = full_weights
    token_float = tokens.astype(jnp.float32)
    normed = rms_scale(token_float, gain_one.astype(jnp.float32)).astype(jnp.bfloat16)
    query_raw = jnp.dot(normed, query_weight, preferred_element_type=jnp.float32).reshape(
        tok_rows, HEADS, HD
    )
    key_raw = jnp.dot(normed, key_weight, preferred_element_type=jnp.float32).reshape(
        tok_rows, HEADS, HD
    )
    queries = rotate(query_raw, angles).astype(jnp.bfloat16)
    keys_rot = rotate(key_raw, angles).astype(jnp.bfloat16)
    values = (
        0.5 * jnp.dot(normed, value_weight, preferred_element_type=jnp.float32)
        + 0.5 * first_values.astype(jnp.float32)
    ).astype(jnp.bfloat16)
    values_heads = values.reshape(tok_rows, HEADS, HD)
    keys_flat = keys_rot.reshape(tok_rows, model_width)
    forward_init = (
        jnp.full((HEADS, tok_rows), start_score, jnp.float32),
        jnp.zeros((HEADS, tok_rows), jnp.float32),
        jnp.zeros((HEADS, tok_rows, HD), jnp.float32),
    )
    running = forward_init
    key_piece = lax.all_gather(keys_flat, "ctx", axis=0, tiled=True)
    value_piece = lax.all_gather(values, "ctx", axis=0, tiled=True)
    piece_rows = key_piece.shape[0]
    size_now = block_size(tok_rows)
    block_count = piece_rows // size_now
    key_blocks = key_piece.reshape(block_count, size_now, HEADS, HD)
    value_blocks = value_piece.reshape(block_count, size_now, HEADS, HD)
    block_starts = jnp.arange(block_count, dtype=jnp.int32) * size_now

    def forward_one_block(partial_value, inputs):
        key_block, value_block, block_start = inputs
        key_index = block_start + jnp.arange(size_now, dtype=jnp.int32)
        key_start = lax.dynamic_slice_in_dim(all_starts, block_start, size_now)
        run_max, run_sum, accum_out = partial_value
        scores = masked_scores(
            queries, key_block, own_index, segment_start, key_index, key_start, score_scale
        )
        new_max = jnp.maximum(run_max, jnp.max(scores, axis=-1))
        weights = jnp.exp(scores - new_max[..., None])
        factor = jnp.exp(run_max - new_max)
        new_sum = run_sum * factor + jnp.sum(weights, axis=-1)
        new_accum = accum_out * factor[..., None] + jnp.einsum(
            "hqk,khd->hqd",
            weights.astype(jnp.bfloat16),
            value_block,
            preferred_element_type=jnp.float32,
        )
        partial_value = (new_max, new_sum, new_accum)
        return (partial_value, None)

    running, _ = lax.scan(forward_one_block, running, (key_blocks, value_blocks, block_starts))
    run_max, run_sum, accum_out = running
    attn_heads = accum_out / run_sum[..., None]
    log_total = run_max + jnp.log(run_sum)
    attn_low = attn_heads.transpose(1, 0, 2).reshape(tok_rows, model_width).astype(jnp.bfloat16)
    resid = token_float + jnp.dot(attn_low, out_weight, preferred_element_type=jnp.float32)
    normed_two = rms_scale(resid, gain_two.astype(jnp.float32)).astype(jnp.bfloat16)
    gate = jnp.dot(normed_two, gate_weight, preferred_element_type=jnp.float32)
    up_proj = jnp.dot(normed_two, up_weight, preferred_element_type=jnp.float32)
    hidden = (jax.nn.silu(gate) * up_proj).astype(jnp.bfloat16)
    block_out = (resid + jnp.dot(hidden, down_weight, preferred_element_type=jnp.float32)).astype(
        jnp.bfloat16
    )
    grad_down = jnp.einsum("tf,td->fd", hidden, cotangent, preferred_element_type=jnp.float32)
    d_hidden = jnp.einsum("td,fd->tf", cotangent, down_weight, preferred_element_type=jnp.float32)
    silu_value, silu_back = jax.vjp(jax.nn.silu, gate)
    d_gate = silu_back(d_hidden * up_proj)[0].astype(jnp.bfloat16)
    d_up = (d_hidden * silu_value).astype(jnp.bfloat16)
    grad_gate = jnp.einsum("td,tf->df", normed_two, d_gate, preferred_element_type=jnp.float32)
    grad_up = jnp.einsum("td,tf->df", normed_two, d_up, preferred_element_type=jnp.float32)
    d_normed_two = jnp.einsum(
        "tf,df->td", d_gate, gate_weight, preferred_element_type=jnp.float32
    ) + jnp.einsum("tf,df->td", d_up, up_weight, preferred_element_type=jnp.float32)
    _, norm_two_back = jax.vjp(rms_scale, resid, gain_two.astype(jnp.float32))
    resid_part, grad_gain_two = norm_two_back(d_normed_two)
    d_resid = cotangent.astype(jnp.float32) + resid_part
    d_branch = d_resid.astype(jnp.bfloat16)
    grad_out = jnp.einsum("td,te->de", attn_low, d_branch, preferred_element_type=jnp.float32)
    d_attn = jnp.einsum(
        "te,de->td", d_branch, out_weight, preferred_element_type=jnp.float32
    ).astype(jnp.bfloat16)
    d_attn_heads = d_attn.reshape(tok_rows, HEADS, HD)
    delta_heads = jnp.sum(d_attn_heads.astype(jnp.float32).transpose(1, 0, 2) * attn_heads, axis=-1)
    all_log_total, all_delta = (
        lax.all_gather(log_total.T.astype(jnp.bfloat16), "ctx", axis=0, tiled=True).astype(
            jnp.float32
        ),
        lax.all_gather(delta_heads.T.astype(jnp.bfloat16), "ctx", axis=0, tiled=True).astype(
            jnp.float32
        ),
    )
    d_query_sum = jnp.zeros((tok_rows, HEADS, HD), jnp.float32)
    key_piece = lax.all_gather(keys_flat, "ctx", axis=0, tiled=True)
    value_piece = lax.all_gather(values, "ctx", axis=0, tiled=True)
    piece_rows = key_piece.shape[0]
    query_size_now = block_size(tok_rows)
    block_count = piece_rows // query_size_now
    key_blocks = key_piece.reshape(block_count, query_size_now, HEADS, HD)
    value_blocks = value_piece.reshape(block_count, query_size_now, HEADS, HD)
    block_starts = jnp.arange(block_count, dtype=jnp.int32) * query_size_now

    def query_one_block(partial_value, inputs):
        key_block, value_block, block_start = inputs
        key_index = block_start + jnp.arange(query_size_now, dtype=jnp.int32)
        key_start = lax.dynamic_slice_in_dim(all_starts, block_start, query_size_now)
        scores = masked_scores(
            queries, key_block, own_index, segment_start, key_index, key_start, score_scale
        )
        probability = jnp.exp(scores - log_total[..., None])
        d_prob = jnp.einsum(
            "qhd,khd->hqk", d_attn_heads, value_block, preferred_element_type=jnp.float32
        )
        d_score = (probability * (d_prob - delta_heads[..., None])).astype(jnp.bfloat16)
        partial_value = (
            partial_value
            + jnp.einsum("hqk,khd->qhd", d_score, key_block, preferred_element_type=jnp.float32)
            * score_scale
        )
        return (partial_value, None)

    d_query_sum, _ = lax.scan(
        query_one_block, d_query_sum, (key_blocks, value_blocks, block_starts)
    )
    queries_flat = queries.reshape(tok_rows, model_width)
    key_init = (
        jnp.zeros((tok_rows, HEADS, HD), jnp.float32),
        jnp.zeros((tok_rows, HEADS, HD), jnp.float32),
    )
    sums_now = key_init
    query_piece = lax.all_gather(queries_flat, "ctx", axis=0, tiled=True)
    grad_piece = lax.all_gather(d_attn, "ctx", axis=0, tiled=True)
    piece_rows = query_piece.shape[0]
    key_size_now = block_size(tok_rows)
    block_count = piece_rows // key_size_now
    query_blocks = query_piece.reshape(block_count, key_size_now, HEADS, HD)
    grad_blocks = grad_piece.reshape(block_count, key_size_now, HEADS, HD)
    block_starts = jnp.arange(block_count, dtype=jnp.int32) * key_size_now

    def key_one_block(partial_value, inputs):
        query_block, grad_block, block_start = inputs
        query_index = block_start + jnp.arange(key_size_now, dtype=jnp.int32)
        query_start = lax.dynamic_slice_in_dim(all_starts, block_start, key_size_now)
        block_total = lax.dynamic_slice_in_dim(all_log_total, block_start, key_size_now).T
        block_delta = lax.dynamic_slice_in_dim(all_delta, block_start, key_size_now).T
        d_key_sum, d_value_sum = partial_value
        scores = masked_scores(
            query_block, keys_rot, query_index, query_start, own_index, segment_start, score_scale
        )
        probability = jnp.exp(scores - block_total[..., None])
        d_prob = jnp.einsum(
            "qhd,khd->hqk", grad_block, values_heads, preferred_element_type=jnp.float32
        )
        d_score = (probability * (d_prob - block_delta[..., None])).astype(jnp.bfloat16)
        d_value_sum = d_value_sum + jnp.einsum(
            "hqk,qhd->khd",
            probability.astype(jnp.bfloat16),
            grad_block,
            preferred_element_type=jnp.float32,
        )
        d_key_sum = (
            d_key_sum
            + jnp.einsum("hqk,qhd->khd", d_score, query_block, preferred_element_type=jnp.float32)
            * score_scale
        )
        partial_value = (d_key_sum, d_value_sum)
        return (partial_value, None)

    sums_now, _ = lax.scan(key_one_block, sums_now, (query_blocks, grad_blocks, block_starts))
    d_key_rot, d_values = sums_now

    def rotate_here(features):
        return rotate(features, angles)

    _, rotate_back = jax.vjp(rotate_here, query_raw)
    d_query = (
        rotate_back(d_query_sum.astype(jnp.bfloat16).astype(jnp.float32))[0]
        .astype(jnp.bfloat16)
        .reshape(tok_rows, model_width)
    )
    d_key = (
        rotate_back(d_key_rot.astype(jnp.bfloat16).astype(jnp.float32))[0]
        .astype(jnp.bfloat16)
        .reshape(tok_rows, model_width)
    )
    d_values_low = d_values.astype(jnp.bfloat16).reshape(tok_rows, model_width)
    grad_first = (0.5 * d_values_low.astype(jnp.float32)).astype(jnp.bfloat16)
    grad_query = jnp.einsum("td,te->de", normed, d_query, preferred_element_type=jnp.float32)
    grad_key = jnp.einsum("td,te->de", normed, d_key, preferred_element_type=jnp.float32)
    grad_value = jnp.einsum("td,te->de", normed, grad_first, preferred_element_type=jnp.float32)
    d_normed = jnp.einsum("te,de->td", d_query, query_weight, preferred_element_type=jnp.float32)
    d_normed = d_normed + jnp.einsum(
        "te,de->td", d_key, key_weight, preferred_element_type=jnp.float32
    )
    d_normed = d_normed + jnp.einsum(
        "te,de->td", grad_first, value_weight, preferred_element_type=jnp.float32
    )
    _, norm_one_back = jax.vjp(rms_scale, token_float, gain_one.astype(jnp.float32))
    token_part, grad_gain_one = norm_one_back(d_normed)
    grad_tokens = (d_resid + token_part).astype(jnp.bfloat16)
    reduced = (
        lax.psum_scatter(grad_gain_one, ("seq", "ctx"), scatter_dimension=0, tiled=True),
        lax.psum_scatter(grad_query, ("seq", "ctx"), scatter_dimension=0, tiled=True),
        lax.psum_scatter(grad_key, ("seq", "ctx"), scatter_dimension=0, tiled=True),
        lax.psum_scatter(grad_value, ("seq", "ctx"), scatter_dimension=0, tiled=True),
        lax.psum_scatter(grad_out, ("seq", "ctx"), scatter_dimension=0, tiled=True),
        lax.psum_scatter(grad_gain_two, ("seq", "ctx"), scatter_dimension=0, tiled=True),
        lax.psum_scatter(grad_gate, ("seq", "ctx"), scatter_dimension=0, tiled=True),
        lax.psum_scatter(grad_up, ("seq", "ctx"), scatter_dimension=0, tiled=True),
        lax.psum_scatter(grad_down, ("seq", "ctx"), scatter_dimension=0, tiled=True),
    )
    return (
        block_out,
        grad_tokens,
        grad_first,
        reduced[0],
        reduced[1],
        reduced[2],
        reduced[3],
        reduced[4],
        reduced[5],
        reduced[6],
        reduced[7],
        reduced[8],
    )


BF = jnp.bfloat16
F32 = jnp.float32
MESH_ID = pl.DeviceIdType.MESH
QC = 768
GC = 1536
BLK = 256
ALL_Z = range(4)


def dot_nn(a, b):
    return lax.dot_general(a, b, (((1,), (0,)), ((), ())), preferred_element_type=F32)


def dot_nt(a, b):
    return lax.dot_general(a, b, (((1,), (1,)), ((), ())), preferred_element_type=F32)


def dot_tn(a, b):
    return lax.dot_general(a, b, (((0,), (0,)), ((), ())), preferred_element_type=F32)


N_SEND = 228
N_RECV = 202
VMEM_LIMIT = 64 * 2**20 - 2**18
DUE = (
    (7.4, 3.9, 7.3, 7.4), (11.9, 11.7, 11.7, 12.0), (8.8, 14.2, 13.0, 9.7),
    (20.8, 28.3, 17.5, 23.4), (34.9, 1.2, -9.8, 34.1), (25.4, 29.2, 21.9, 26.0),
    (41.0, 39.9, 33.1, 36.3), (48.5, 42.6, 35.7, 44.5), (45.2, 47.8, 34.6, 46.9),
    (14.5, 15.6, 16.3, 14.5), (10.4, 16.5, 9.7, 12.4), (23.1, 29.8, 22.4, 27.0),
    (33.1, 1.2, -5.7, 39.2), (57.1, 65.3, 60.3, 62.3), (61.2, 66.7, 61.0, 64.5),
    (66.7, 71.9, 62.8, 67.3), (70.6, 76.7, 64.9, 72.8), (69.0, 80.2, 68.8, 76.6),
    (77.6, 84.6, 73.0, 80.9), (82.1, 0.4, -6.5, 84.3), (87.3, -0.8, -5.7, 89.0),
    (95.2, 3.5, -2.1, 96.7), (23.2, 20.8, 15.4, 22.8), (29.8, 25.2, 29.5, 25.4),
    (86.4, 75.1, 84.1, 79.5), (86.6, 75.1, 84.1, 78.2), (139.2, 133.0, 134.2, 133.3),
    (142.1, 136.0, 138.6, 136.9), (58.9, 49.4, 43.6, 46.6), (66.0, 55.7, 49.1, 55.7),
    (64.0, 57.5, 59.3, 54.2), (71.7, 62.2, 62.8, 63.8), (126.9, 122.2, 121.7, 121.0),
    (127.5, 122.5, 122.0, 121.3), (127.8, 123.5, 124.4, 124.4), (129.3, 126.7, 128.7, 128.1),
    (121.0, 0.0, 0.4, -1.4), (-0.6, 131.6, 0.4, 0.8), (-3.0, 0.0, 135.0, 0.8),
    (-2.4, 0.0, -11.0, 138.6), (131.4, -7.3, -11.2, -0.2), (-3.2, 129.0, -11.8, -0.8),
    (-3.2, -0.8, 93.9, -0.8), (-24.2, -0.8, -0.8, 120.8), (104.8, -2.6, -0.0, -0.0),
    (-2.4, 133.3, -0.0, 27.7), (-9.8, -1.2, 139.1, -1.2), (-5.8, 9.9, -14.5, 134.7),
    (121.2, 0.2, 0.2, 0.2), (-8.6, 141.3, 0.0, 0.0), (0.3, 0.3, 135.7, 0.3),
    (2.4, 0.3, 0.3, 129.1), (133.3, 130.6, 133.6, 132.6), (137.0, 134.1, 138.5, 138.2),
    (141.3, 140.0, 143.6, 141.2), (145.5, 143.0, 145.6, 145.3), (133.3, 0.0, 0.0, 0.0),
    (-0.2, 143.9, -0.2, -0.2), (0.0, 0.0, 149.1, -1.0), (0.0, 3.4, 0.0, 171.7),
    (151.0, 0.0, 1.1, 5.3), (0.0, 145.9, 0.0, 0.0), (0.0, 0.0, 142.5, -1.9),
    (0.0, -11.1, 0.0, 131.4), (141.7, -11.1, 0.0, -4.5), (0.0, 149.1, -4.7, -1.9),
    (23.5, 23.5, 179.2, 23.5), (0.0, 0.0, 0.0, 141.5), (145.5, -0.5, -11.4, -0.5),
    (0.5, 165.0, 0.3, 0.3), (-6.5, 2.9, 158.3, 0.3), (-34.6, -27.8, -27.9, 117.9),
    (152.9, 156.6, 150.7, 150.5), (159.7, 153.3, 155.8, 156.8), (156.3, 159.5, 159.3, 162.2),
    (163.1, 160.8, 165.8, 163.8), (148.1, -1.4, -1.4, -1.4), (-3.0, 164.7, -0.3, 1.1),
    (-4.9, -0.3, 171.0, 1.1), (-0.3, -0.3, -0.3, 178.3), (178.9, -0.8, -0.8, -0.8),
    (0.8, 176.5, 9.5, 0.8), (-10.9, -7.4, 160.6, -7.4), (0.8, 0.8, 0.8, 154.9),
    (156.0, -1.4, -1.4, -3.6), (-0.5, 174.8, -18.4, 0.8), (-0.2, 1.1, 184.5, 1.1),
    (-7.4, 0.8, 0.8, 164.4), (157.7, 0.8, 0.8, 0.8), (-8.2, 185.1, 0.0, 0.0),
    (-10.9, -2.7, 176.8, -4.6), (-1.9, -0.6, -0.6, 164.5), (163.6, 164.1, 164.2, 164.5),
    (165.1, 164.9, 163.4, 164.6), (167.2, 166.7, 165.1, 169.2), (177.5, 172.0, 174.5, 177.5),
    (185.7, 2.2, 2.2, 2.2), (6.1, 189.7, -0.6, -0.6), (11.3, 4.3, 190.4, 4.3),
    (4.9, -0.4, -1.0, 178.1), (174.1, 172.0, 169.4, 171.2), (177.1, 172.3, 174.6, 173.2),
    (174.7, 172.2, 170.5, 169.9), (178.3, 176.5, 175.5, 177.5), (164.3, -5.8, -5.8, -5.3),
    (-15.8, 183.4, -5.8, -5.8), (-5.0, -5.8, 188.0, -5.8), (-5.5, -8.0, -8.0, 187.1),
    (198.6, -0.1, -0.1, -1.7), (2.4, 194.0, -0.9, -3.7), (2.5, 0.0, 190.8, -11.6),
    (2.5, 0.0, -3.8, 170.2), (164.3, -15.1, -18.9, -16.4), (-4.6, 189.2, -6.0, -3.8),
    (7.3, 2.7, 200.9, 1.1), (4.6, 0.0, 0.0, 174.0), (184.9, 0.0, 0.0, -1.6),
    (6.0, 203.8, 1.4, -2.4), (0.1, -16.7, 194.9, -3.8), (2.8, 2.8, 2.8, 176.8),
    (189.5, 180.6, 181.3, 180.0), (178.6, 171.3, 170.1, 170.8), (189.0, 182.9, 180.5, 182.2),
    (190.9, 186.5, 180.6, 182.4), (189.5, 2.4, 22.5, -3.4), (0.3, 197.2, -2.7, -4.0),
    (-1.6, -1.6, 203.2, -3.8), (5.9, 5.9, 5.9, 211.5), (218.0, 10.2, 24.0, 13.9),
    (23.1, 227.2, 23.1, 22.0), (-1.7, -1.7, 197.8, -2.8), (-0.2, -0.2, -5.1, 181.3),
    (189.2, -2.9, 8.4, -0.8), (-0.2, 199.6, -0.2, -0.8), (-2.2, -3.4, 206.1, -1.3),
    (-12.8, 16.5, -11.3, 172.3), (177.4, 2.0, -11.3, -11.9), (-2.0, 227.9, -0.5, -1.1),
    (-2.0, 12.8, 208.9, -1.1), (-1.5, -2.7, 0.0, 185.8),
)
LOOK = (
    (4.2, 4.4, -5.6, 7.3), (11.6, 11.7, 11.6, 11.5), (-5.0, 6.6, 6.5, 6.4),
    (14.0, 14.6, 7.4, 14.6), (22.6, 14.8, 14.3, 19.3), (15.5, 15.9, 16.0, 15.4),
    (22.3, 16.1, 16.1, 15.6), (19.3, 12.2, 15.5, 10.9), (37.7, 33.4, 33.7, 36.9),
    (37.4, 33.6, 33.9, 37.1), (48.5, 42.8, 49.7, 41.6), (52.4, 46.4, 53.8, 45.2),
    (55.9, 50.8, 57.5, 49.2), (60.5, 54.8, 61.7, 56.6), (63.6, 58.6, 64.8, 60.9),
    (74.6, 69.7, 77.0, 67.9), (59.0, 54.2, 59.3, 52.3), (74.0, 69.0, 63.4, 62.5),
    (103.5, 103.3, 102.2, 102.0), (106.4, 106.2, 107.0, 104.2), (105.2, 115.1, 115.8, 107.9),
    (123.4, 120.6, 121.3, 118.5), (130.0, 119.3, 124.9, 122.9), (114.7, 128.8, 129.4, 127.5),
    (131.9, 128.8, 128.9, 127.5), (136.8, 132.5, 131.8, 130.8), (149.8, 145.5, 145.1, 144.6),
    (138.3, 131.9, 133.6, 132.9), (148.3, 142.7, 144.3, 140.7), (146.6, 142.3, 143.9, 140.3),
    (146.3, 141.6, 142.6, 136.5), (160.5, 149.4, 151.8, 148.4), (163.8, 152.7, 155.1, 151.7),
    (168.9, 157.2, 159.8, 163.9), (176.2, 165.0, 167.0, 162.9), (177.5, 166.3, 169.4, 172.6),
    (184.9, 173.2, 176.5, 171.9), (187.7, 180.4, 179.7, 178.8), (193.2, 175.3, 182.3, 173.6),
    (194.9, 180.5, 186.0, 179.6), (202.5, 190.4, 191.3, 186.8), (204.0, 186.4, 196.2, 191.8),
    (204.9, 180.7, 197.2, 192.8), (194.0, 207.7, 206.1, 208.7),
)


SCRATCH = dict(
    TOK=((256, 1024), BF),
    STT=((4, 8, 128), F32),
    ST=((1024, 128), F32),
    COS=((1024, 128), F32),
    SIN=((1024, 128), F32),
    FV=((1024, 256), BF),
    COT=((1024, 1024), BF),
    N1=((1024, 1024), BF),
    N2=((1024, 1024), BF),
    DB=((1024, 1024), BF),
    GAZ=((4, 16, 128), BF),
    GAS=((2, 16, 128), BF),
    GAJ=((4, 16, 128), BF),
    SYD=((4, 96, 1024), BF),
    GV=((8, 1024), F32),
    WA=((2, 4, 4, 32, QC), BF),
    WO=((2, 4, 32, 1024), BF),
    WG=((2, 4, 4, 32, GC), BF),
    WD=((2, 4, 96, 1024), BF),
    QS=((1024, 256), BF),
    KR=((1024, 256), BF),
    V=((1024, 256), BF),
    O=((1024, 256), BF),
    DA=((1024, 256), BF),
    P0=((4, 256, 256), BF),
    P1=((4, 256, 512), BF),
    P2=((4, 256, 768), BF),
    P3=((4, 256, 1024), BF),
    DQ=((1024, 256), BF),
    DK=((1024, 256), F32),
    DV=((1024, 256), F32),
    DQKV=((1024, QC), BF),
    H=((1024, 768), BF),
    DGU=((1024, GC), BF),
    RES=((256, 1024), F32),
    DRES=((256, 1024), F32),
    SSA=((2, 256, 1024), BF),
    SRA=((2, 256, 1024), BF),
    XSA=((256, 1024), BF),
    XRA=((256, 1024), BF),
    SSB=((2, 256, 1024), BF),
    SRB=((2, 256, 1024), BF),
    XSB=((256, 1024), BF),
    XRB=((256, 1024), BF),
    FF=((256, 1024), F32),
    OUT=((256, 1024), BF),
    GQ=((4, 4, 32, QC), F32),
    GO=((4, 32, 1024), F32),
    GG=((4, 4, 32, GC), F32),
    GD=((4, 96, 1024), F32),
    RYQ=((4, 4, 32, QC), BF),
    RYO=((4, 32, 1024), BF),
    RYG=((4, 4, 32, GC), BF),
    RYD=((4, 96, 1024), BF),
    ZQ=((5, 4, 32, QC), BF),
    ZO=((5, 32, 1024), BF),
    ZG=((5, 4, 32, GC), BF),
    ZD=((5, 96, 1024), BF),
    GGS=((16, 128), F32),
    GGR=((3, 16, 128), F32),
    GGY=((16, 128), F32),
    GGT=((16, 128), F32),
    GGZ=((4, 16, 128), F32),
)


def slot_window(c):
    return 352 * c // 128 * 128, (352 * c + 352 + 127) // 128 * 128


def slot_map(c):
    lo, hi = slot_window(c)
    unit = lax.broadcasted_iota(jnp.int32, (hi - lo, 384), 0) + (lo - 352 * c)
    slot = lax.broadcasted_iota(jnp.int32, (hi - lo, 384), 1)
    block = (slot >= 96).astype(jnp.int32) + (slot >= 192).astype(jnp.int32)
    block = block + (slot >= 288).astype(jnp.int32)
    within = slot - 96 * block
    return ((unit == 88 * block + within) & (within < 88)).astype(F32).astype(BF)


def finish_kernel(*refs):
    (block, gtok, gfv, gq, gg, go, gd, gain) = refs[:8]
    (o_block, o_gtok, o_gfv, o_ga, o_q, o_k, o_v, o_o, o_gf, o_g, o_u, o_d) = refs[8:]
    o_block[...] = block[...]
    o_gtok[...] = gtok[...]
    o_gfv[...] = gfv[...]
    o_o[...] = go[...]
    o_d[...] = gd[0:88, :]
    for t, out in enumerate((o_q, o_k, o_v)):
        for h in range(2):
            for c in range(4):
                part = gq[c, :, 384 * h + 128 * t : 384 * h + 128 * t + 128]
                out[:, 128 * (c + 4 * h) : 128 * (c + 4 * h) + 128] = part.astype(F32)
    o_g[...] = jnp.zeros((32, 2816), F32)
    o_u[...] = jnp.zeros((32, 2816), F32)
    for c in range(4):
        lo, hi = slot_window(c)
        place = slot_map(c)
        for t, out in enumerate((o_g, o_u)):
            for h in range(2):
                part = gg[c, :, 768 * t + 384 * h : 768 * t + 384 * h + 384]
                out[:, 1408 * h + lo : 1408 * h + hi] += dot_nt(part, place)
    d = lax.axis_index("seq") * 4 + lax.axis_index("ctx")
    lane = lax.broadcasted_iota(jnp.int32, (32, 128), 1)
    row = lax.broadcasted_iota(jnp.int32, (32, 128), 0)
    pick = lane == row + 32 * (d % 4)
    line = lax.broadcasted_iota(jnp.int32, (8, 128), 0) == d // 4
    for r, out in ((0, o_ga), (8, o_gf)):
        own = jnp.sum(jnp.where(line, gain[r : r + 8, :], 0.0), axis=0, keepdims=True)
        full = jnp.broadcast_to(own, (32, 128))
        out[...] = jnp.sum(jnp.where(pick, full, 0.0), axis=-1, keepdims=True)


class Step(tuple):
    def __lt__(self, other):
        return self[:2] < other[:2]


def layer_kernel(*refs):
    (tok, fv, cot, stt, gt, wq, wk, wv, wg, wu, wo, wdn) = refs[:12]
    (o_block, o_gtok, o_gfv, o_gq, o_gg, o_go, o_gd, o_gain) = refs[12:20]
    R = types.SimpleNamespace(**dict(zip(SCRATCH, refs[20:])))
    ssem, rsem, lsem = refs[20 + len(SCRATCH) :]
    sa, sg, wd = R.DQKV, R.DGU, R.DB.at[768:864]

    def pack(c):
        return slice(32 * c, 32 * c + 32)

    def prep():
        for t, w in enumerate((wq, wk, wv)):
            for h in range(2):
                for c in range(4):
                    lanes = pl.ds(128 * (c + 4 * h), 128)
                    sa[pack(c), 384 * h + 128 * t : 384 * h + 128 * t + 128] = w[:, lanes]
        for c in range(4):
            lo, hi = slot_window(c)
            place = slot_map(c)
            for t, w in enumerate((wg, wu)):
                for h in range(2):
                    part = dot_nn(w[:, 1408 * h + lo : 1408 * h + hi], place)
                    sg[pack(c), 768 * t + 384 * h : 768 * t + 384 * h + 384] = part.astype(BF)
        wd[0:88, :] = wdn[...]
        wd[88:96, :] = jnp.zeros((8, 1024), BF)

    s = lax.axis_index("seq")
    z = lax.axis_index("ctx")
    y = s // 4
    j = s % 4
    x = j // 2
    k = j % 2
    ny = 1 - y
    sib = (4 * y + 2 * x + (1 - k), z)
    xp = (4 * y + 2 * (1 - x) + k, z)
    yp = (4 * ny + j, z)
    up_z, dn_z = (s, z + 1), (s, z - 1)
    column = (z + k) % 2
    crossing = x != column
    direct = x == column
    jp = 2 * (1 - x) + k

    def host(jj):
        return (4 * y + 2 * column + z // 2, jj)

    home = (4 * y + z, 2 * k + (x + z) % 2)
    at_home = (home[0] == s) & (home[1] == z)
    away = host(j)
    away_self = (away[0] == s) & (away[1] == z)
    b_me = 2 * k + (x + z) % 2
    b_x = 2 * k + (1 - x + z) % 2
    b_s = 2 * (1 - k) + (x + z) % 2
    b_xs = 2 * (1 - k) + (1 - x + z) % 2

    counters = [0, 0, 0]
    pend = []
    tasks = []
    made = [0, 0]

    def ids(n):
        made[0] += n
        return made[0] - n

    on_z = {q: z == q for q in ALL_Z}
    turn_of = [None]

    def guard():
        return None if turn_of[0] is None else on_z[turn_of[0]]

    def place():
        return z if turn_of[0] is None else turn_of[0]

    def later(i, fn, of=None):
        for q in ALL_Z if turn_of[0] is None else turn_of:
            tasks.append(Step((DUE[i][q], i, fn, of, q)))

    def due(q):
        return min([e for e in tasks if e[4] == q], default=None)

    def take(step):
        tasks.remove(step)
        turn_of[0] = step[4]
        step[2]()
        turn_of[0] = None

    def look():
        for q in ALL_Z:
            step = due(q)
            while step is not None and step[0] <= LOOK[made[1]][q]:
                take(step)
                step = due(q)
        made[1] += 1

    def flush(of=None):
        for q in ALL_Z:
            while any((of is None or e[3] is of) and e[4] == q for e in tasks):
                take(due(q))

    def snd(n=1):
        counters[0] += n
        assert counters[0] <= N_SEND
        return counters[0] - n

    def rcv(n=1):
        counters[2] += n
        assert counters[2] <= N_RECV
        return counters[2] - n

    def rows(b):
        return pl.ds(pl.multiple_of(b * BLK, BLK), BLK)

    def half_rows(b, h):
        return pl.ds(pl.multiple_of(b * BLK + 128 * h, 128), 128)

    def came(dst, r):
        return rc(dst, dst, 0, sib, r).wait_recv

    def rc(src, dst, i, dev, r):
        return pltpu.make_async_remote_copy(
            src_ref=src,
            dst_ref=dst,
            send_sem=ssem.at[i],
            recv_sem=rsem.at[r],
            device_id=dev,
            device_id_type=MESH_ID,
        )

    def both(p, q):
        if p is None or q is None or isinstance(p, bool) or isinstance(q, bool):
            if p is False or q is False:
                return False
            return p if q is None or q is True else q
        return p & q

    def when(cond, fn):
        cond = both(guard(), cond)
        if cond is None or cond is True:
            fn()
        elif cond is not False:
            pl.when(cond)(fn)

    def start(desc, cond=None):
        when(cond, desc.start)
        cond = both(guard(), cond)
        if cond is not False:
            pend.append((cond, desc))

    def local(src, dst):
        d = pltpu.make_async_copy(src, dst, lsem.at[counters[1]])
        counters[1] += 1
        d.start()
        return d

    def route(src, dst, i, self_cond, dev, r, cond=None):
        when(both(cond, self_cond), pltpu.make_async_copy(src, dst, rsem.at[r]).start)
        start(rc(src, dst, i, dev, r), both(cond, jnp.logical_not(self_cond)))

    def arrive(like_src, dst, r, self_cond):
        when(self_cond, pltpu.make_async_copy(like_src, dst, rsem.at[r]).wait)
        when(jnp.logical_not(self_cond), came(dst, r))

    def group_dev(c, jj):
        return (4 * y + c, jj)

    barrier = pltpu.get_barrier_semaphore()
    me = j * 4 + z
    for i in range(1, 16):
        t = (me + i) % 16
        pl.semaphore_signal(
            barrier, inc=1, device_id=(4 * y + t // 4, t % 4), device_id_type=MESH_ID
        )
    pl.semaphore_signal(barrier, inc=1, device_id=yp, device_id_type=MESH_ID)
    prep()
    pl.semaphore_wait(barrier, 16)

    i_gz, i_gy, i_gj = snd(4), snd(), snd(4)
    r_gz, r_gy, r_gj = rcv(4), rcv(), rcv(4)
    loc_gt = local(gt, R.GAZ.at[z])
    for c in range(4):
        start(rc(gt, R.GAZ.at[z], i_gz + c, (s, c), r_gz + z), z != c)

    class Move:
        def __init__(self, src, stage, pieces, arrivals):
            self.src, self.stage, self.pieces, self.arrivals = src, stage, pieces, arrivals
            n = len(pieces(j))
            self.ix, self.io, self.ir = snd(2), snd(n), snd(n)
            self.rx = rcv(2)

        def cross(self):
            for h in range(2):
                cut = pl.ds(128 * h, 128)
                start(rc(self.src.at[cut], self.stage.at[cut], self.ix + h, xp, self.rx + h), crossing)

        def own(self):
            for n, (cut, dst, self_cond, dev, r) in enumerate(self.pieces(j)):
                route(self.src.at[cut], dst, self.io + n, self_cond, dev, r, direct)

        def relay(self, h):
            pieces = self.pieces(jp)
            part = self.stage.at[pl.ds(128 * h, 128)]
            when(direct, came(part, self.rx + h))
            for n, (cut, dst, self_cond, dev, r) in enumerate(pieces):
                if (n == h) if len(pieces) == 2 else h == 1:
                    route(self.stage.at[cut], dst, self.ir + n, self_cond, dev, r, direct)

        def wait(self, part=None):
            for n, (like, dst, r, self_cond) in enumerate(self.arrivals()):
                if part is None or n == part:
                    arrive(like, dst, r, self_cond)

    last_hop_self = (z % 2 == k) & (b_me == z)

    def block_pieces(dst_at, base):
        def pieces(jj):
            dev = host(jj)
            self_cond = (dev[0] == s) & (dev[1] == z)
            return [
                (pl.ds(128 * h, 128), dst_at(z, h), self_cond, dev, base + h) for h in range(2)
            ]

        return pieces

    def block_arrivals(src, dst_at, base):
        return lambda: [
            (src.at[pl.ds(128 * h, 128)], dst_at(b_me, h), base + h, last_hop_self)
            for h in range(2)
        ]

    def tok_at(b, h):
        return R.TOK.at[pl.ds(128 * h, 128)]

    def cot_at(b, h):
        return R.COT.at[half_rows(b, h)]

    def fv_at(b, h):
        return R.FV.at[rows(b), pl.ds(128 * h, 128)]

    i_tok, i_cot, i_fv, i_st = rcv(2), rcv(2), rcv(8), rcv(4)
    s_st = snd(4)

    def fv_pieces(jj):
        out = []
        for c in range(4):
            dev = group_dev(c, jj)
            self_cond = (dev[0] == s) & (dev[1] == z)
            for h in range(2):
                cut = (slice(None), pl.ds(128 * (c + 4 * h), 128))
                out.append((cut, fv_at(z, h), self_cond, dev, i_fv + 2 * z + h))
        return out

    def fv_arrivals():
        out = []
        for b in range(4):
            self_cond = (z % 2 == k) & (z == b) & (x == (b + k) % 2)
            for h in range(2):
                out.append((fv.at[:, pl.ds(128 * h, 128)], fv_at(b, h), i_fv + 2 * b + h, self_cond))
        return out

    m_tok = Move(tok, R.DB.at[0:256], block_pieces(tok_at, i_tok), block_arrivals(tok, tok_at, i_tok))
    m_cot = Move(cot, R.DB.at[512:768], block_pieces(cot_at, i_cot), block_arrivals(cot, cot_at, i_cot))
    m_fv = Move(fv, R.DB.at[256:512], fv_pieces, fv_arrivals)

    m_tok.own()
    i_sa, i_sg, r_sa, r_sg = snd(4), snd(4), rcv(4), rcv(4)
    own_pack = pl.ds(pl.multiple_of(32 * j, 32), 32)
    loc_sa = local(sa.at[own_pack], R.WA.at[y, j, z])
    loc_wo = local(wo, R.WO.at[y, z])
    for c in range(4):
        start(rc(sa.at[pack(c)], R.WA.at[y, j, z], i_sa + c, group_dev(c, z), r_sa + j), j != c)
    m_tok.cross()
    loc_wd = local(wd, R.WD.at[y, z])
    loc_sg = local(sg.at[own_pack], R.WG.at[y, j, z])

    def wait_group(base, dst_of):
        for c in range(4):
            when(j != c, came(dst_of(c), base + c))

    class Gather:
        def __init__(self, piece):
            self.piece = piece
            self.iz, self.iy, self.rz, self.ry = snd(8), snd(4), rcv(4), rcv(4)

        def sources(self, step):
            at = place()
            below, above = at - step, at + step
            out = []
            for src, sem, target, here, on in (
                (below, self.iz, up_z, below >= 0, at < 3),
                (above, self.iz + 4, dn_z, above <= 3, at > 0),
            ):
                if here is not False:
                    out.append((src, sem, target, here, on))
            return out

        def send_z(self, step, cond=None):
            for src, sem, target, here, on in self.sources(step):
                p = self.piece(y, src)
                start(rc(p, p, sem + src, target, self.rz + src), both(cond, both(here, on)))

        def send_y(self, step):
            for src, _, _, here, _ in self.sources(step)[: 1 if step == 0 else 2]:
                p = self.piece(y, src)
                start(rc(p, p, self.iy + src, yp, self.ry + src), here)

        def recv(self, step):
            for src, _, _, here, _ in self.sources(step):
                when(here, came(self.piece(y, src), self.rz + src))

        def pass_on(self, step):
            self.recv(step)
            if step < 3:
                self.send_z(step)
            self.send_y(step)

        def finish(self):
            for zz in range(4):
                came(self.piece(ny, zz), self.ry + zz)()

    g_a = Gather(lambda yy, zz: R.WA.at[yy, :, zz])
    g_o = Gather(lambda yy, zz: R.WO.at[yy, zz])
    g_d = Gather(lambda yy, zz: R.WD.at[yy, zz])
    g_g0 = Gather(lambda yy, zz: R.WG.at[yy, 0:2, zz])
    g_g1 = Gather(lambda yy, zz: R.WG.at[yy, 2:4, zz])

    loc_gt.wait()
    for c in range(4):
        when(z != c, came(R.GAZ.at[c], r_gz + c))
    R.GAS[0] = R.GAZ[0] + R.GAZ[1] + R.GAZ[2] + R.GAZ[3]
    start(rc(R.GAS.at[0], R.GAS.at[1], i_gy, yp, r_gy))

    wait_group(r_sa, lambda c: R.WA.at[y, c, z])
    loc_sa.wait()
    loc_wo.wait()
    g_a.send_z(0)
    g_a.send_y(0)
    g_o.send_z(0)
    g_o.send_y(0)
    t_tok, t_a, t_move, t_o, t_ffn = ids(2), ids(3), ids(5), ids(3), ids(9)
    t_n1, t_n2, t_db, t_cot = ids(2), ids(2), ids(2), ids(4)
    later(t_tok, lambda: m_tok.relay(0), m_tok)
    later(t_tok + 1, lambda: m_tok.relay(1), m_tok)
    def pass_a(step):
        g_a.pass_on(step)
        later(t_o + step - 1, lambda: g_o.pass_on(step), g_o)
        if step == 1:
            later(t_a + 1, lambda: pass_a(2), g_a)
        if step == 2:
            later(t_a + 2, lambda: pass_a(3), g_a)
            later(t_move, first_move, m_fv)

    later(t_a, lambda: pass_a(1), g_a)

    came(R.GAS.at[1], r_gy)()
    R.GAJ[j] = R.GAS[0] + R.GAS[1]
    for c in range(4):
        start(rc(R.GAJ.at[j], R.GAJ.at[j], i_gj + c, group_dev(c, z), r_gj + j), j != c)
    for c in range(4):
        start(rc(sg.at[pack(c)], R.WG.at[y, j, z], i_sg + c, group_dev(c, z), r_sg + j), j != c)
    look()
    for c in range(4):
        self_c = (j == z) & (j == c)
        route(stt, R.STT.at[z], s_st + c, self_c, group_dev(c, j), i_st + z)
    loc_wd.wait()
    g_d.send_y(0)

    def own_shard():
        wait_group(r_sg, lambda c: R.WG.at[y, c, z])
        when(None, loc_sg.wait)
        g_g0.send_y(0)

    def first_move():
        m_fv.own()
        later(t_move + 1, second_move, m_fv)

    def second_move():
        m_fv.relay(0)
        m_fv.relay(1)
        m_cot.own()
        later(t_move + 2, lambda: third_move(0))

    def third_move(h):
        m_cot.relay(h)
        if h == 0:
            later(t_move + 3, lambda: third_move(1))
        else:
            for g in (g_d, g_g0, g_g1):
                g.send_z(0, direct)
            g_g1.send_y(0)
            for n in range(3):
                later(t_ffn + n, lambda n=n: pass_ffn(1, n))

    def pass_ffn(step, n):
        (g_d, g_g0, g_g1)[n].pass_on(step)
        if step < 3:
            later(t_ffn + 3 * step + n, lambda: pass_ffn(step + 1, n))

    later(t_move + 4, own_shard, m_tok)
    look()
    wait_group(r_gj, lambda c: R.GAJ.at[c])
    gains = (R.GAJ[0] + R.GAJ[1] + R.GAJ[2] + R.GAJ[3]).astype(F32)
    for r in range(8):
        R.GV[0:1, 128 * r : 128 * r + 128] = gains[r : r + 1, :]
        R.GV[1:2, 128 * r : 128 * r + 128] = gains[8 + r : 9 + r, :]
    look()

    class Share:
        def __init__(self, buf):
            self.buf = buf
            self.i, self.r = snd(6), rcv(6)

        def piece(self, b, h):
            return self.buf.at[half_rows(b, h)]

        def send(self, h):
            p = self.piece(b_me, h)
            start(rc(p, p, self.i + h, xp, self.r + h))
            start(rc(p, p, self.i + 2 + h, sib, self.r + 2 + h))

        def forward(self, h):
            p = self.piece(b_x, h)
            when(None, came(p, self.r + h))
            start(rc(p, p, self.i + 4 + h, sib, self.r + 4 + h))

        def finish(self):
            for h in range(2):
                came(self.piece(b_s, h), self.r + 2 + h)()
            for h in range(2):
                came(self.piece(b_xs, h), self.r + 4 + h)()

    sh1, sh2, sh3, sh_cot = Share(R.N1), Share(R.N2), Share(R.DB), Share(R.COT)

    def send_cot(h):
        m_cot.wait(h)
        sh_cot.send(h)
        later(t_cot + 2 + h, lambda: sh_cot.forward(h))
        if h == 0:
            later(t_cot + 1, lambda: send_cot(1))

    for h in range(2):
        flush(m_tok)
        look()
        m_tok.wait(h)
        xs = R.TOK[128 * h : 128 * h + 128, :].astype(F32)
        rs1 = lax.rsqrt(jnp.mean(xs * xs, axis=-1, keepdims=True) + norm_eps)
        R.N1[half_rows(b_me, h), :] = (xs * rs1 * R.GV[0:1, :]).astype(BF)
        sh1.send(h)
        later(t_n1 + h, lambda h=h: sh1.forward(h), sh1)
        look()
    m_fv.cross()
    m_cot.cross()
    later(t_cot, lambda: send_cot(0))
    look()
    for c in range(4):
        arrive(stt, R.STT.at[c], i_st + c, (j == z) & (c == z))
    for b in range(4):
        for r in range(2):
            row = R.STT[b, r : r + 1, :]
            R.ST[256 * b + 128 * r : 256 * b + 128 * r + 128, :] = jnp.transpose(
                jnp.broadcast_to(row, (128, 128))
            )
    lane = lax.broadcasted_iota(jnp.int32, (1, 128), 1)
    low_half = (lane % 64) < 32
    freq = jnp.exp((lane % 32).astype(F32) * (-2.0 / HD * 9.210340371976184))

    def angle_body(b, c):
        pos = (lax.broadcasted_iota(jnp.int32, (BLK, 128), 0) + b * BLK).astype(F32)
        ang = (pos - R.ST[rows(b), :]) * freq
        R.COS[rows(b), :] = jnp.cos(ang)
        R.SIN[rows(b), :] = jnp.where(low_half, -jnp.sin(ang), jnp.sin(ang))
        return c

    lax.fori_loop(0, 4, angle_body, 0)

    def turn(v):
        return jnp.where(low_half, pltpu.roll(v, 96, 1), pltpu.roll(v, 32, 1))

    flush(g_a)
    look()
    g_a.finish()
    flush(sh1)
    look()
    sh1.finish()
    flush(m_fv)
    look()
    m_fv.wait()
    for g in (g_d, g_g0, g_g1):
        g.send_z(0, crossing)

    def qkv_body(b, c):
        raw = dot_nn(R.N1[rows(b), :], R.WA[...].reshape(1024, QC))
        cs, sn = R.COS[rows(b), :], R.SIN[rows(b), :]
        for t in range(2):
            sl = slice(128 * t, 128 * t + 128)
            q = raw[:, 384 * t : 384 * t + 128]
            R.QS[rows(b), sl] = ((q * cs + turn(q) * sn).astype(BF).astype(F32) * 0.125).astype(BF)
            kk = raw[:, 384 * t + 128 : 384 * t + 256]
            R.KR[rows(b), sl] = (kk * cs + turn(kk) * sn).astype(BF)
            v = raw[:, 384 * t + 256 : 384 * t + 384]
            R.V[rows(b), sl] = (0.5 * v + 0.5 * R.FV[rows(b), sl].astype(F32)).astype(BF)
        return c

    lax.fori_loop(0, 4, qkv_body, 0)
    look()

    PB = [R.P0, R.P1, R.P2, R.P3]

    def head_parts(h):
        pair = pl.ds(pl.multiple_of((h // 2) * 128, 128), 128)
        mine = ((lane // 64) == (h % 2)).astype(F32)
        return pair, mine.astype(BF), mine

    def attn_body(h, c):
        pair, low_mine, mine = head_parts(h)
        for i in range(4):
            n = BLK * (i + 1)
            q = R.QS[BLK * i : n, pair] * low_mine
            sc = dot_nt(q, R.KR[0:n, pair])
            col = lax.broadcasted_iota(jnp.int32, (BLK, n), 1)
            row = lax.broadcasted_iota(jnp.int32, (BLK, n), 0) + BLK * i
            first = R.ST[BLK * i : n, 0:1].astype(jnp.int32)
            sc = jnp.where((col >= first) & (col <= row), sc, masked_score)
            top = jnp.max(sc, axis=-1, keepdims=True)
            e = jnp.exp(sc - top)
            p = (e * (1.0 / jnp.sum(e, axis=-1, keepdims=True))).astype(BF)
            PB[i][h] = p
            o = dot_nn(p, R.V[0:n, pair]) * mine
            R.O[BLK * i : n, pair] += o.astype(BF)
        return c

    R.O[...] = jnp.zeros((1024, 256), BF)
    lax.fori_loop(0, 2, attn_body, 0)
    look()
    lax.fori_loop(2, 4, attn_body, 0)
    look()

    class GroupSum:
        def __init__(self, bufs):
            self.ss, self.sr, self.xs, self.xr = bufs
            self.i, self.r = snd(4), rcv(4)

        def run(self, fn):
            self.ss[0] = fn(b_xs).astype(BF)
            d0 = rc(self.ss.at[0], self.sr.at[0], self.i, sib, self.r)
            d0.start()
            self.ss[1] = fn(b_s).astype(BF)
            d1 = rc(self.ss.at[1], self.sr.at[1], self.i + 1, sib, self.r + 1)
            d1.start()
            look()
            d0.wait_recv()
            self.xs[...] = (fn(b_x) + self.sr[0].astype(F32)).astype(BF)
            d2 = []
            for h in range(2):
                cut = pl.ds(128 * h, 128)
                d2.append(rc(self.xs.at[cut], self.xr.at[cut], self.i + 2 + h, xp, self.r + 2 + h))
                d2[h].start()
            R.FF[...] = fn(b_me)
            look()
            d1.wait_recv()
            R.FF[...] += self.sr[1].astype(F32)
            self.descs = (d0, d1, *d2)

        def result(self, h):
            look()
            self.descs[2 + h].wait_recv()
            cut = slice(128 * h, 128 * h + 128)
            return R.FF[cut, :] + self.xr[cut, :].astype(F32)

        def end(self):
            for d in self.descs:
                d.wait_send()

    set_a = (R.SSA, R.SRA, R.XSA, R.XRA)
    set_b = (R.SSB, R.SRB, R.XSB, R.XRB)
    flush(g_o)
    look()
    g_o.finish()
    sum_attn = GroupSum(set_a)
    sum_attn.run(lambda b: dot_nn(R.O[rows(b), :], R.WO[...].reshape(256, 1024)))
    for h in range(2):
        cut = slice(128 * h, 128 * h + 128)
        res = R.TOK[cut, :].astype(F32) + sum_attn.result(h)
        R.RES[cut, :] = res
        rs2 = lax.rsqrt(jnp.mean(res * res, axis=-1, keepdims=True) + norm_eps)
        R.N2[half_rows(b_me, h), :] = (res * rs2 * R.GV[1:2, :]).astype(BF)
        sh2.send(h)
        later(t_n2 + h, lambda h=h: sh2.forward(h))
    sum_attn.end()
    flush()
    for g in (g_d, g_g0, g_g1):
        g.finish()
    sh2.finish()
    sh_cot.finish()

    def ffn_body(b, c):
        gu = dot_nn(R.N2[rows(b), :], R.WG[...].reshape(1024, GC))
        gate, up = gu[:, :768], gu[:, 768:]
        sig = 1.0 / (1.0 + jnp.exp(-gate))
        silu = gate * sig
        R.H[rows(b), :] = (silu * up).astype(BF)
        dh = dot_nt(R.COT[rows(b), :], R.WD[...].reshape(768, 1024))
        R.DGU[rows(b), 0:768] = (dh * up * (sig * (1.0 + gate * (1.0 - sig)))).astype(BF)
        R.DGU[rows(b), 768:1536] = (dh * silu).astype(BF)
        return c

    for cond, desc in pend:
        when(cond, desc.wait_send)
    pend.clear()
    lax.fori_loop(0, 4, ffn_body, 0)

    class Reduce:
        def __init__(self, g, sy, ry, zr, cs):
            self.g, self.sy, self.ry, self.zr = g, sy, ry, zr
            self.cs = cs
            self.iy, self.iz, self.r, self.rz = snd(4), snd(4), rcv(4), rcv(5)

        def cut(self, ref, o):
            if self.cs is None:
                return ref.at[o]
            return ref.at[self.cs[0] : self.cs[1], o]

        def zslot(self, o):
            if self.cs is None:
                return self.zr.at[o]
            return self.zr.at[o, self.cs[0] : self.cs[1]]

        def chunks(self):
            return [None] if self.cs is None else range(*self.cs)

        def chunk(self, o, c):
            return self.zr.at[o] if c is None else self.zr.at[o, c]

        def term(self, o, c):
            at = o if c is None else (c, o)
            return self.g[at] + self.ry[at].astype(F32)

        def send_y(self):
            for o in (3, 0, 2, 1):
                start(rc(self.cut(self.sy, o), self.cut(self.ry, o), self.iy + o, yp, self.r + o))

        def recv_y(self, o):
            when(None, came(self.cut(self.ry, o), self.r + o))

        def hop(self, o, upward, zz):
            if upward:
                head, target, slot_out = zz == 0, up_z, o
            else:
                head, target = zz == 3, dn_z
                slot_out = 4 if zz - 1 == o else o
            d = rc(self.zslot(o), self.zslot(slot_out), self.iz + o, target, self.rz + slot_out)

            def go():
                if not head:
                    came(self.zslot(o), self.rz + o)()
                for c in self.chunks():
                    p = self.chunk(o, c)
                    val = self.term(o, c)
                    if not head:
                        val = val + p[...].astype(F32)
                    p[...] = val.astype(BF)
                d.start()

            pl.when(z == zz)(go)
            pend.append((z == zz, d))

        def last(self, zz, put):
            def go():
                if zz > 0:
                    came(self.zslot(zz), self.rz + zz)()
                if zz < 3:
                    came(self.zslot(4), self.rz + 4)()
                for c in self.chunks():
                    val = self.term(zz, c)
                    if zz > 0:
                        val = val + self.chunk(zz, c)[...].astype(F32)
                    if zz < 3:
                        val = val + self.chunk(4, c)[...].astype(F32)
                    put(c, val)

            pl.when(z == zz)(go)

        def schedule(self, put):
            t = ids(20)

            def take_y(n):
                o = (3, 0, 2, 1)[n]
                self.recv_y(o)
                zz = turn_of[0]
                later(t + 4 + 4 * n + zz, lambda: step(o, zz), self)
                if n < 3:
                    later(t + n + 1, lambda: take_y(n + 1), self)

            def step(o, zz):
                if zz == o:
                    self.last(o, put)
                else:
                    self.hop(o, zz < o, zz)

            later(t, lambda: take_y(0), self)

    class Direct(Reduce):
        def send_term(self, o):
            d = rc(self.cut(self.ry, o), self.zslot(z), self.iz + o, (s, o), self.rz + z)

            def go():
                for c in self.chunks():
                    p = self.ry.at[o] if c is None else self.ry.at[c, o]
                    p[...] = self.term(o, c).astype(BF)
                d.start()

            if place() != o:
                when(None, go)
                pend.append((guard(), d))

        def gather(self, zz, put):
            def go():
                for o in range(4):
                    if o != zz:
                        came(self.zslot(o), self.rz + o)()
                for c in self.chunks():
                    val = self.term(zz, c)
                    for o in range(4):
                        if o != zz:
                            val = val + self.chunk(o, c)[...].astype(F32)
                    put(c, val)

            pl.when(z == zz)(go)

        def schedule(self, put):
            t = ids(8)

            def take_y(n):
                o = (3, 0, 2, 1)[n]
                self.recv_y(o)
                self.send_term(o)
                if n < 3:
                    later(t + n + 1, lambda: take_y(n + 1), self)
                else:
                    zz = turn_of[0]
                    later(t + 4 + zz, lambda: self.gather(zz, put), self)

            later(t, lambda: take_y(0), self)

    def half(yy, width):
        return pl.ds(pl.multiple_of(yy * width, width), width)

    def grad_cols(left, right, g, sy, yy, m, keep):
        width = right.shape[1]
        a = left[:, pl.ds(pl.multiple_of(yy * 512 + 256 * m, 256), 256)]
        val = dot_tn(a, right[...]).reshape(2, 4, 32, width)
        if keep:
            g[2 * m : 2 * m + 2] = val
        else:
            sy[2 * m : 2 * m + 2] = val.astype(BF)

    def grad_rows(left, right, g, sy, yy, per, keep):
        a = left[:, half(yy, 4 * per)]
        val = dot_tn(a, right[...]).reshape(4, per, 1024)
        if keep:
            g[...] = val
        else:
            sy[...] = val.astype(BF)

    red_d = Reduce(R.GD, R.SYD, R.RYD, R.ZD, None)
    red_g0 = Reduce(R.GG, R.WG.at[0], R.RYG, R.ZG, (0, 2))
    red_g1 = Reduce(R.GG, R.WG.at[0], R.RYG, R.ZG, (2, 4))
    red_o = Direct(R.GO, R.WO.at[0], R.RYO, R.ZO, None)

    def put_rows(ref):
        def put(c, val):
            ref[...] = val

        return put

    def put_cols(ref):
        def put(c, val):
            ref[c, 0] = val

        return put

    grad_rows(R.H, R.COT, None, R.SYD, ny, 96, False)
    red_d.send_y()
    sum_dn2 = GroupSum(set_a)
    sum_dn2.run(lambda b: dot_nt(R.DGU[rows(b), :], R.WG[...].reshape(1024, GC)))
    for m, red in ((0, red_g0), (1, red_g1)):
        grad_cols(R.N2, R.DGU, None, R.WG.at[0], ny, m, False)
        red.send_y()
    grad_rows(R.H, R.COT, R.GD, None, y, 96, True)
    red_d.schedule(put_rows(R.GD.at[0]))
    look()
    for m in range(2):
        grad_cols(R.N2, R.DGU, R.GG, None, y, m, True)
    red_g0.schedule(put_cols(R.GG))
    red_g1.schedule(put_cols(R.GG))

    R.GGS[...] = jnp.zeros((16, 128), F32)

    def add_gain(first, row):
        for r in range(8):
            R.GGS[first + r : first + r + 1, :] += row[:, 128 * r : 128 * r + 128]

    for h in range(2):
        cut = slice(128 * h, 128 * h + 128)
        dn2 = sum_dn2.result(h)
        res = R.RES[cut, :]
        rs2 = lax.rsqrt(jnp.mean(res * res, axis=-1, keepdims=True) + norm_eps)
        xh = res * rs2
        gd = dn2 * R.GV[1:2, :]
        add_gain(8, jnp.sum(dn2 * xh, axis=0, keepdims=True))
        dres = R.COT[half_rows(b_me, h), :].astype(F32) + rs2 * (
            gd - xh * jnp.mean(gd * xh, axis=-1, keepdims=True)
        )
        R.DRES[cut, :] = dres
        R.DB[half_rows(b_me, h), :] = dres.astype(BF)
        sh3.send(h)
        later(t_db + h, lambda h=h: sh3.forward(h), sh3)
    sum_dn2.end()
    look()
    sum_out = GroupSum(set_b)
    sum_out.run(lambda b: dot_nn(R.H[rows(b), :], R.WD[...].reshape(768, 1024)))
    look()
    flush(sh3)
    look()
    sh3.finish()

    def da_body(b, c):
        R.DA[rows(b), :] = dot_nt(R.DB[rows(b), :], R.WO[...].reshape(256, 1024)).astype(BF)
        return c

    lax.fori_loop(0, 4, da_body, 0)
    grad_rows(R.O, R.DB, None, R.WO.at[0], ny, 32, False)
    red_o.send_y()
    grad_rows(R.O, R.DB, R.GO, None, y, 32, True)
    red_o.schedule(put_rows(R.GO.at[0]))
    look()
    i_out, r_out = snd(2), rcv(2)
    for h in range(2):
        cut = slice(128 * h, 128 * h + 128)
        R.OUT[cut, :] = (R.RES[cut, :] + sum_out.result(h)).astype(BF)
        part = pl.ds(128 * h, 128)
        route(R.OUT.at[part], o_block.at[part], i_out + h, at_home, home, r_out + h)
    sum_out.end()
    R.DK[...] = jnp.zeros((1024, 256), F32)
    R.DV[...] = jnp.zeros((1024, 256), F32)

    def back_body(h, c):
        pair, low_mine, mine = head_parts(h)
        for i in range(4):
            n = BLK * (i + 1)
            do = R.DA[BLK * i : n, pair] * low_mine
            q = R.QS[BLK * i : n, pair] * low_mine
            dp = dot_nt(do, R.V[0:n, pair])
            pb = PB[i][h]
            p = pb.astype(F32)
            delta = jnp.sum(p * dp, axis=-1, keepdims=True)
            ds = (p * (dp - delta)).astype(BF)
            dq = dot_nn(ds, R.KR[0:n, pair]) * (0.125 * mine)
            R.DQ[BLK * i : n, pair] += dq.astype(BF)
            R.DK[0:n, pair] += dot_tn(ds, q)
            R.DV[0:n, pair] += dot_tn(pb, do)
        return c

    def pair_lanes(p):
        return pl.ds(384 * p, 384)

    def grad_pair(p, sy, yy, keep):
        for m in range(2):
            a = R.N1[:, pl.ds(pl.multiple_of(yy * 512 + 256 * m, 256), 256)]
            val = dot_tn(a, R.DQKV[:, pair_lanes(p)]).reshape(2, 4, 32, 384)
            if keep:
                R.GQ[2 * m : 2 * m + 2, :, :, pair_lanes(p)] = val
            else:
                sy[2 * m : 2 * m + 2] = val.astype(BF)

    red_q, i_gf, r_gf = [], snd(8), rcv(8)
    for p in range(2):
        sy = R.WG.at[1, :, :, :, pair_lanes(p)]
        cut = [r.at[:, :, :, pair_lanes(p)] for r in (R.GQ, R.RYQ, R.ZQ)]
        red_q.append(Reduce(cut[0], sy, cut[1], cut[2], (0, 4)))
    R.DQ[...] = jnp.zeros((1024, 256), BF)
    for p in range(2):
        for h in (2 * p, 2 * p + 1):
            lax.fori_loop(h, h + 1, back_body, 0)
            look()

        def dqkv_body(b, c):
            cs, sn = R.COS[rows(b), :], R.SIN[rows(b), :]
            sl = slice(128 * p, 128 * p + 128)
            u = R.DQ[rows(b), sl].astype(F32)
            R.DQKV[rows(b), 384 * p : 384 * p + 128] = (u * cs - turn(u) * sn).astype(BF)
            u = R.DK[rows(b), sl].astype(BF).astype(F32)
            R.DQKV[rows(b), 384 * p + 128 : 384 * p + 256] = (u * cs - turn(u) * sn).astype(BF)
            R.DQKV[rows(b), 384 * p + 256 : 384 * p + 384] = (
                0.5 * R.DV[rows(b), sl].astype(BF).astype(F32)
            ).astype(BF)
            return c

        lax.fori_loop(0, 4, dqkv_body, 0)
        grad_pair(p, red_q[p].sy, ny, False)
        red_q[p].send_y()
        for b in range(4):
            self_b = (j == z) & (z == b)
            src = R.DQKV.at[pl.ds(256 * b, 256), pl.ds(384 * p + 256, 128)]
            dst = o_gfv.at[:, pl.ds(pl.multiple_of(128 * (j + 4 * p), 128), 128)]
            route(src, dst, i_gf + 2 * b + p, self_b, (4 * y + z, b), r_gf + 2 * j + p)
        if p == 0:
            grad_pair(p, None, y, True)
            red_q[p].schedule(put_cols(red_q[p].g))
    sum_dn1 = GroupSum(set_a)
    sum_dn1.run(lambda b: dot_nt(R.DQKV[rows(b), :], R.WA[...].reshape(1024, QC)))
    grad_pair(1, None, y, True)
    red_q[1].schedule(put_cols(red_q[1].g))
    look()

    i_gtok, r_gtok = snd(2), rcv(2)
    for h in range(2):
        cut = slice(128 * h, 128 * h + 128)
        dn1 = sum_dn1.result(h)
        xs = R.TOK[cut, :].astype(F32)
        rs1 = lax.rsqrt(jnp.mean(xs * xs, axis=-1, keepdims=True) + norm_eps)
        xh = xs * rs1
        gd = dn1 * R.GV[0:1, :]
        add_gain(0, jnp.sum(dn1 * xh, axis=0, keepdims=True))
        R.XSB[cut, :] = (
            R.DRES[cut, :] + rs1 * (gd - xh * jnp.mean(gd * xh, axis=-1, keepdims=True))
        ).astype(BF)
        part = pl.ds(128 * h, 128)
        route(R.XSB.at[part], o_gtok.at[part], i_gtok + h, at_home, home, r_gtok + h)
    sum_dn1.end()

    i_ggg, i_ggy, i_ggz = snd(4), snd(), snd(4)
    r_ggg, r_ggy, r_ggz = rcv(4), rcv(), rcv(4)
    for c in range(4):
        start(
            rc(R.GGS, R.GGR.at[(j - c - 1) % 4], i_ggg + c, group_dev(c, z), r_ggg + j), j != c
        )
    look()
    for c in range(4):
        when(j != c, came(R.GGR.at[(c - j - 1) % 4], r_ggg + c))
    R.GGT[...] = R.GGS[...] + R.GGR[0] + R.GGR[1] + R.GGR[2]
    start(rc(R.GGT, R.GGY, i_ggy, yp, r_ggy))
    look()
    came(R.GGY, r_ggy)()
    R.GGZ[z] = R.GGT[...] + R.GGY[...]
    for c in range(4):
        start(rc(R.GGZ.at[z], R.GGZ.at[z], i_ggz + c, (s, c), r_ggz + z), z != c)

    i_rg, i_rq, r_rg, r_rq = snd(4), snd(4), rcv(4), rcv(4)
    outs = []

    def hand_back(g, send, out, base, r):
        for c in range(4):
            send[c] = g[c, 0].astype(BF)
            start(rc(send.at[c], out.at[j], base + c, group_dev(c, z), r + j), j != c)
        outs.append(local(send.at[j], out.at[j]))

    look()
    for red in (red_d, red_g0, red_g1):
        flush(red)
    hand_back(R.GG, R.RYG.at[0], o_gg, i_rg, r_rg)
    outs.append(local(R.GD.at[0], o_gd))
    flush()
    hand_back(R.GQ, R.RYQ.at[0], o_gq, i_rq, r_rq)
    outs.append(local(R.GO.at[0], o_go))
    for c in range(4):
        when(z != c, came(R.GGZ.at[c], r_ggz + c))
    R.GGY[...] = R.GGZ[0] + R.GGZ[1] + R.GGZ[2] + R.GGZ[3]
    outs.append(local(R.GGY, o_gain))

    for h in range(2):
        part = pl.ds(128 * h, 128)
        arrive(R.OUT.at[part], o_block.at[part], r_out + h, away_self)
        arrive(R.XSB.at[part], o_gtok.at[part], r_gtok + h, away_self)
    for c in range(4):
        self_c = (j == z) & (j == c)
        for h in range(2):
            src = R.DQKV.at[pl.ds(256 * z, 256), pl.ds(384 * h + 256, 128)]
            dst = o_gfv.at[:, pl.ds(pl.multiple_of(128 * (c + 4 * h), 128), 128)]
            arrive(src, dst, r_gf + 2 * c + h, self_c)
    wait_group(r_rg, lambda c: o_gg.at[c])
    wait_group(r_rq, lambda c: o_gq.at[c])
    for d in outs:
        d.wait()
    for cond, desc in pend:
        when(cond, desc.wait_send)


def fast_device(
    tokens,
    first_values,
    gain_attn,
    w_query,
    w_key,
    w_value,
    w_out,
    gain_ffn,
    w_gate,
    w_up,
    w_down,
    segment_start,
    cotangent,
):
    d = lax.axis_index("seq") * 4 + lax.axis_index("ctx")
    mine = jnp.arange(1024, dtype=jnp.int32) // 32 == d

    def spot(g):
        return jnp.where(mine, jnp.tile(g, 32), jnp.zeros((), BF)).reshape(8, 128)

    gt = jnp.concatenate([spot(gain_attn), spot(gain_ffn)])
    stt = jnp.pad(segment_start.astype(F32).reshape(2, 128), ((0, 6), (0, 0)))
    hbm = pl.BlockSpec(memory_space=pl.ANY)
    vmem = pl.BlockSpec(memory_space=pltpu.VMEM)
    outs = pl.pallas_call(
        layer_kernel,
        name="layer",
        out_shape=[
            jax.ShapeDtypeStruct((256, 1024), BF),
            jax.ShapeDtypeStruct((256, 1024), BF),
            jax.ShapeDtypeStruct((256, 1024), BF),
            jax.ShapeDtypeStruct((4, 32, QC), BF),
            jax.ShapeDtypeStruct((4, 32, GC), BF),
            jax.ShapeDtypeStruct((32, 1024), F32),
            jax.ShapeDtypeStruct((96, 1024), F32),
            jax.ShapeDtypeStruct((16, 128), F32),
        ],
        in_specs=[hbm] * 5 + [vmem] * 5 + [hbm, vmem],
        out_specs=[hbm] * 8,
        scratch_shapes=[pltpu.VMEM(shape, dtype) for shape, dtype in SCRATCH.values()]
        + [
            pltpu.SemaphoreType.DMA((N_SEND,)),
            pltpu.SemaphoreType.DMA((N_RECV,)),
            pltpu.SemaphoreType.DMA((14,)),
        ],
        compiler_params=pltpu.CompilerParams(
            collective_id=0, has_side_effects=True, vmem_limit_bytes=VMEM_LIMIT
        ),
    )(
        tokens,
        first_values,
        cotangent,
        stt,
        gt,
        w_query,
        w_key,
        w_value,
        w_gate,
        w_up,
        w_out,
        w_down,
    )
    res = pl.pallas_call(
        finish_kernel,
        name="finish",
        out_shape=[
            jax.ShapeDtypeStruct((256, 1024), BF),
            jax.ShapeDtypeStruct((256, 1024), BF),
            jax.ShapeDtypeStruct((256, 1024), BF),
            jax.ShapeDtypeStruct((32, 1), F32),
            jax.ShapeDtypeStruct((32, 1024), F32),
            jax.ShapeDtypeStruct((32, 1024), F32),
            jax.ShapeDtypeStruct((32, 1024), F32),
            jax.ShapeDtypeStruct((32, 1024), F32),
            jax.ShapeDtypeStruct((32, 1), F32),
            jax.ShapeDtypeStruct((32, 2816), F32),
            jax.ShapeDtypeStruct((32, 2816), F32),
            jax.ShapeDtypeStruct((88, 1024), F32),
        ],
        in_specs=[vmem] * 8,
        out_specs=[vmem] * 12,
        compiler_params=pltpu.CompilerParams(vmem_limit_bytes=VMEM_LIMIT),
    )(*outs)
    return tuple(r.reshape(32) if n in (3, 8) else r for n, r in enumerate(res))


def solution(mesh):
    fits = mesh.shape["seq"] == 8 and mesh.shape["ctx"] == 4
    return jax.shard_map(
        fast_device if fits else per_device,
        mesh=mesh,
        in_specs=(
            P(("seq", "ctx"), None),
            P(("seq", "ctx"), None),
            P(("seq", "ctx")),
            P(("seq", "ctx"), None),
            P(("seq", "ctx"), None),
            P(("seq", "ctx"), None),
            P(("seq", "ctx"), None),
            P(("seq", "ctx")),
            P(("seq", "ctx"), None),
            P(("seq", "ctx"), None),
            P(("seq", "ctx"), None),
            P(("seq", "ctx")),
            P(("seq", "ctx"), None),
        ),
        out_specs=(
            P(("seq", "ctx"), None),
            P(("seq", "ctx"), None),
            P(("seq", "ctx"), None),
            P(("seq", "ctx")),
            P(("seq", "ctx"), None),
            P(("seq", "ctx"), None),
            P(("seq", "ctx"), None),
            P(("seq", "ctx"), None),
            P(("seq", "ctx")),
            P(("seq", "ctx"), None),
            P(("seq", "ctx"), None),
            P(("seq", "ctx"), None),
        ),
        check_vma=False,
    )
```

```python
import types

import jax
import jax.numpy as jnp
from jax import lax
from jax.experimental import pallas as pl
from jax.experimental.pallas import tpu as pltpu
from jax.sharding import PartitionSpec as P

HEADS = 16
HD = 64


norm_eps = 1e-06
masked_score = -2e30
start_score = -1e30


def rms_scale(features, scale_gain):
    return (
        features
        * lax.rsqrt(jnp.mean(features * features, axis=-1, keepdims=True) + norm_eps)
        * scale_gain
    )


def rope_angles(positions, head_size):
    half_size = head_size // 2
    frequency = 10000.0 ** (-(jnp.arange(half_size, dtype=jnp.float32) * 2.0) / head_size)
    angles = positions.astype(jnp.float32)[:, None] * frequency[None, :]
    return jnp.concatenate([angles, angles], axis=-1)


def rotate(features, angles):
    half_size = features.shape[-1] // 2
    turned = jnp.concatenate([-features[..., half_size:], features[..., :half_size]], axis=-1)
    return features * jnp.cos(angles)[:, None, :] + turned * jnp.sin(angles)[:, None, :]


def block_size(shard_rows):
    size_guess = shard_rows * max(1, 640 // shard_rows)
    return size_guess


def masked_scores(queries, keys_part, query_index, query_start, key_index, key_start, score_scale):
    scores = (
        jnp.einsum("qhd,khd->hqk", queries, keys_part, preferred_element_type=jnp.float32)
        * score_scale
    )
    allowed = (query_start[:, None] == key_start[None, :]) & (
        key_index[None, :] <= query_index[:, None]
    )
    return jnp.where(allowed[None], scores, masked_score)


def per_device(
    tokens,
    first_values,
    gain_attn,
    w_query,
    w_key,
    w_value,
    w_out,
    gain_ffn,
    w_gate,
    w_up,
    w_down,
    segment_start,
    cotangent,
):
    tok_rows, model_width = tokens.shape
    score_scale = HD ** (-0.5)
    own_weights = (gain_attn, w_query, w_key, w_value, w_out, gain_ffn, w_gate, w_up, w_down)
    full_weights = (
        lax.all_gather(own_weights[0], ("seq", "ctx"), axis=0, tiled=True),
        lax.all_gather(own_weights[1], ("seq", "ctx"), axis=0, tiled=True),
        lax.all_gather(own_weights[2], ("seq", "ctx"), axis=0, tiled=True),
        lax.all_gather(own_weights[3], ("seq", "ctx"), axis=0, tiled=True),
        lax.all_gather(own_weights[4], ("seq", "ctx"), axis=0, tiled=True),
        lax.all_gather(own_weights[5], ("seq", "ctx"), axis=0, tiled=True),
        lax.all_gather(own_weights[6], ("seq", "ctx"), axis=0, tiled=True),
        lax.all_gather(own_weights[7], ("seq", "ctx"), axis=0, tiled=True),
        lax.all_gather(own_weights[8], ("seq", "ctx"), axis=0, tiled=True),
    )
    all_starts = lax.all_gather(segment_start, "ctx", axis=0, tiled=True)
    own_index = lax.axis_index("ctx") * tok_rows + jnp.arange(tok_rows, dtype=jnp.int32)
    angles = rope_angles(own_index - segment_start, HD)
    (
        gain_one,
        query_weight,
        key_weight,
        value_weight,
        out_weight,
        gain_two,
        gate_weight,
        up_weight,
        down_weight,
    ) = full_weights
    token_float = tokens.astype(jnp.float32)
    normed = rms_scale(token_float, gain_one.astype(jnp.float32)).astype(jnp.bfloat16)
    query_raw = jnp.dot(normed, query_weight, preferred_element_type=jnp.float32).reshape(
        tok_rows, HEADS, HD
    )
    key_raw = jnp.dot(normed, key_weight, preferred_element_type=jnp.float32).reshape(
        tok_rows, HEADS, HD
    )
    queries = rotate(query_raw, angles).astype(jnp.bfloat16)
    keys_rot = rotate(key_raw, angles).astype(jnp.bfloat16)
    values = (
        0.5 * jnp.dot(normed, value_weight, preferred_element_type=jnp.float32)
        + 0.5 * first_values.astype(jnp.float32)
    ).astype(jnp.bfloat16)
    values_heads = values.reshape(tok_rows, HEADS, HD)
    keys_flat = keys_rot.reshape(tok_rows, model_width)
    forward_init = (
        jnp.full((HEADS, tok_rows), start_score, jnp.float32),
        jnp.zeros((HEADS, tok_rows), jnp.float32),
        jnp.zeros((HEADS, tok_rows, HD), jnp.float32),
    )
    running = forward_init
    key_piece = lax.all_gather(keys_flat, "ctx", axis=0, tiled=True)
    value_piece = lax.all_gather(values, "ctx", axis=0, tiled=True)
    piece_rows = key_piece.shape[0]
    size_now = block_size(tok_rows)
    block_count = piece_rows // size_now
    key_blocks = key_piece.reshape(block_count, size_now, HEADS, HD)
    value_blocks = value_piece.reshape(block_count, size_now, HEADS, HD)
    block_starts = jnp.arange(block_count, dtype=jnp.int32) * size_now

    def forward_one_block(partial_value, inputs):
        key_block, value_block, block_start = inputs
        key_index = block_start + jnp.arange(size_now, dtype=jnp.int32)
        key_start = lax.dynamic_slice_in_dim(all_starts, block_start, size_now)
        run_max, run_sum, accum_out = partial_value
        scores = masked_scores(
            queries, key_block, own_index, segment_start, key_index, key_start, score_scale
        )
        new_max = jnp.maximum(run_max, jnp.max(scores, axis=-1))
        weights = jnp.exp(scores - new_max[..., None])
        factor = jnp.exp(run_max - new_max)
        new_sum = run_sum * factor + jnp.sum(weights, axis=-1)
        new_accum = accum_out * factor[..., None] + jnp.einsum(
            "hqk,khd->hqd",
            weights.astype(jnp.bfloat16),
            value_block,
            preferred_element_type=jnp.float32,
        )
        partial_value = (new_max, new_sum, new_accum)
        return (partial_value, None)

    running, _ = lax.scan(forward_one_block, running, (key_blocks, value_blocks, block_starts))
    run_max, run_sum, accum_out = running
    attn_heads = accum_out / run_sum[..., None]
    log_total = run_max + jnp.log(run_sum)
    attn_low = attn_heads.transpose(1, 0, 2).reshape(tok_rows, model_width).astype(jnp.bfloat16)
    resid = token_float + jnp.dot(attn_low, out_weight, preferred_element_type=jnp.float32)
    normed_two = rms_scale(resid, gain_two.astype(jnp.float32)).astype(jnp.bfloat16)
    gate = jnp.dot(normed_two, gate_weight, preferred_element_type=jnp.float32)
    up_proj = jnp.dot(normed_two, up_weight, preferred_element_type=jnp.float32)
    hidden = (jax.nn.silu(gate) * up_proj).astype(jnp.bfloat16)
    block_out = (resid + jnp.dot(hidden, down_weight, preferred_element_type=jnp.float32)).astype(
        jnp.bfloat16
    )
    grad_down = jnp.einsum("tf,td->fd", hidden, cotangent, preferred_element_type=jnp.float32)
    d_hidden = jnp.einsum("td,fd->tf", cotangent, down_weight, preferred_element_type=jnp.float32)
    silu_value, silu_back = jax.vjp(jax.nn.silu, gate)
    d_gate = silu_back(d_hidden * up_proj)[0].astype(jnp.bfloat16)
    d_up = (d_hidden * silu_value).astype(jnp.bfloat16)
    grad_gate = jnp.einsum("td,tf->df", normed_two, d_gate, preferred_element_type=jnp.float32)
    grad_up = jnp.einsum("td,tf->df", normed_two, d_up, preferred_element_type=jnp.float32)
    d_normed_two = jnp.einsum(
        "tf,df->td", d_gate, gate_weight, preferred_element_type=jnp.float32
    ) + jnp.einsum("tf,df->td", d_up, up_weight, preferred_element_type=jnp.float32)
    _, norm_two_back = jax.vjp(rms_scale, resid, gain_two.astype(jnp.float32))
    resid_part, grad_gain_two = norm_two_back(d_normed_two)
    d_resid = cotangent.astype(jnp.float32) + resid_part
    d_branch = d_resid.astype(jnp.bfloat16)
    grad_out = jnp.einsum("td,te->de", attn_low, d_branch, preferred_element_type=jnp.float32)
    d_attn = jnp.einsum(
        "te,de->td", d_branch, out_weight, preferred_element_type=jnp.float32
    ).astype(jnp.bfloat16)
    d_attn_heads = d_attn.reshape(tok_rows, HEADS, HD)
    delta_heads = jnp.sum(d_attn_heads.astype(jnp.float32).transpose(1, 0, 2) * attn_heads, axis=-1)
    all_log_total, all_delta = (
        lax.all_gather(log_total.T.astype(jnp.bfloat16), "ctx", axis=0, tiled=True).astype(
            jnp.float32
        ),
        lax.all_gather(delta_heads.T.astype(jnp.bfloat16), "ctx", axis=0, tiled=True).astype(
            jnp.float32
        ),
    )
    d_query_sum = jnp.zeros((tok_rows, HEADS, HD), jnp.float32)
    key_piece = lax.all_gather(keys_flat, "ctx", axis=0, tiled=True)
    value_piece = lax.all_gather(values, "ctx", axis=0, tiled=True)
    piece_rows = key_piece.shape[0]
    query_size_now = block_size(tok_rows)
    block_count = piece_rows // query_size_now
    key_blocks = key_piece.reshape(block_count, query_size_now, HEADS, HD)
    value_blocks = value_piece.reshape(block_count, query_size_now, HEADS, HD)
    block_starts = jnp.arange(block_count, dtype=jnp.int32) * query_size_now

    def query_one_block(partial_value, inputs):
        key_block, value_block, block_start = inputs
        key_index = block_start + jnp.arange(query_size_now, dtype=jnp.int32)
        key_start = lax.dynamic_slice_in_dim(all_starts, block_start, query_size_now)
        scores = masked_scores(
            queries, key_block, own_index, segment_start, key_index, key_start, score_scale
        )
        probability = jnp.exp(scores - log_total[..., None])
        d_prob = jnp.einsum(
            "qhd,khd->hqk", d_attn_heads, value_block, preferred_element_type=jnp.float32
        )
        d_score = (probability * (d_prob - delta_heads[..., None])).astype(jnp.bfloat16)
        partial_value = (
            partial_value
            + jnp.einsum("hqk,khd->qhd", d_score, key_block, preferred_element_type=jnp.float32)
            * score_scale
        )
        return (partial_value, None)

    d_query_sum, _ = lax.scan(
        query_one_block, d_query_sum, (key_blocks, value_blocks, block_starts)
    )
    queries_flat = queries.reshape(tok_rows, model_width)
    key_init = (
        jnp.zeros((tok_rows, HEADS, HD), jnp.float32),
        jnp.zeros((tok_rows, HEADS, HD), jnp.float32),
    )
    sums_now = key_init
    query_piece = lax.all_gather(queries_flat, "ctx", axis=0, tiled=True)
    grad_piece = lax.all_gather(d_attn, "ctx", axis=0, tiled=True)
    piece_rows = query_piece.shape[0]
    key_size_now = block_size(tok_rows)
    block_count = piece_rows // key_size_now
    query_blocks = query_piece.reshape(block_count, key_size_now, HEADS, HD)
    grad_blocks = grad_piece.reshape(block_count, key_size_now, HEADS, HD)
    block_starts = jnp.arange(block_count, dtype=jnp.int32) * key_size_now

    def key_one_block(partial_value, inputs):
        query_block, grad_block, block_start = inputs
        query_index = block_start + jnp.arange(key_size_now, dtype=jnp.int32)
        query_start = lax.dynamic_slice_in_dim(all_starts, block_start, key_size_now)
        block_total = lax.dynamic_slice_in_dim(all_log_total, block_start, key_size_now).T
        block_delta = lax.dynamic_slice_in_dim(all_delta, block_start, key_size_now).T
        d_key_sum, d_value_sum = partial_value
        scores = masked_scores(
            query_block, keys_rot, query_index, query_start, own_index, segment_start, score_scale
        )
        probability = jnp.exp(scores - block_total[..., None])
        d_prob = jnp.einsum(
            "qhd,khd->hqk", grad_block, values_heads, preferred_element_type=jnp.float32
        )
        d_score = (probability * (d_prob - block_delta[..., None])).astype(jnp.bfloat16)
        d_value_sum = d_value_sum + jnp.einsum(
            "hqk,qhd->khd",
            probability.astype(jnp.bfloat16),
            grad_block,
            preferred_element_type=jnp.float32,
        )
        d_key_sum = (
            d_key_sum
            + jnp.einsum("hqk,qhd->khd", d_score, query_block, preferred_element_type=jnp.float32)
            * score_scale
        )
        partial_value = (d_key_sum, d_value_sum)
        return (partial_value, None)

    sums_now, _ = lax.scan(key_one_block, sums_now, (query_blocks, grad_blocks, block_starts))
    d_key_rot, d_values = sums_now

    def rotate_here(features):
        return rotate(features, angles)

    _, rotate_back = jax.vjp(rotate_here, query_raw)
    d_query = (
        rotate_back(d_query_sum.astype(jnp.bfloat16).astype(jnp.float32))[0]
        .astype(jnp.bfloat16)
        .reshape(tok_rows, model_width)
    )
    d_key = (
        rotate_back(d_key_rot.astype(jnp.bfloat16).astype(jnp.float32))[0]
        .astype(jnp.bfloat16)
        .reshape(tok_rows, model_width)
    )
    d_values_low = d_values.astype(jnp.bfloat16).reshape(tok_rows, model_width)
    grad_first = (0.5 * d_values_low.astype(jnp.float32)).astype(jnp.bfloat16)
    grad_query = jnp.einsum("td,te->de", normed, d_query, preferred_element_type=jnp.float32)
    grad_key = jnp.einsum("td,te->de", normed, d_key, preferred_element_type=jnp.float32)
    grad_value = jnp.einsum("td,te->de", normed, grad_first, preferred_element_type=jnp.float32)
    d_normed = jnp.einsum("te,de->td", d_query, query_weight, preferred_element_type=jnp.float32)
    d_normed = d_normed + jnp.einsum(
        "te,de->td", d_key, key_weight, preferred_element_type=jnp.float32
    )
    d_normed = d_normed + jnp.einsum(
        "te,de->td", grad_first, value_weight, preferred_element_type=jnp.float32
    )
    _, norm_one_back = jax.vjp(rms_scale, token_float, gain_one.astype(jnp.float32))
    token_part, grad_gain_one = norm_one_back(d_normed)
    grad_tokens = (d_resid + token_part).astype(jnp.bfloat16)
    reduced = (
        lax.psum_scatter(grad_gain_one, ("seq", "ctx"), scatter_dimension=0, tiled=True),
        lax.psum_scatter(grad_query, ("seq", "ctx"), scatter_dimension=0, tiled=True),
        lax.psum_scatter(grad_key, ("seq", "ctx"), scatter_dimension=0, tiled=True),
        lax.psum_scatter(grad_value, ("seq", "ctx"), scatter_dimension=0, tiled=True),
        lax.psum_scatter(grad_out, ("seq", "ctx"), scatter_dimension=0, tiled=True),
        lax.psum_scatter(grad_gain_two, ("seq", "ctx"), scatter_dimension=0, tiled=True),
        lax.psum_scatter(grad_gate, ("seq", "ctx"), scatter_dimension=0, tiled=True),
        lax.psum_scatter(grad_up, ("seq", "ctx"), scatter_dimension=0, tiled=True),
        lax.psum_scatter(grad_down, ("seq", "ctx"), scatter_dimension=0, tiled=True),
    )
    return (
        block_out,
        grad_tokens,
        grad_first,
        reduced[0],
        reduced[1],
        reduced[2],
        reduced[3],
        reduced[4],
        reduced[5],
        reduced[6],
        reduced[7],
        reduced[8],
    )


BF = jnp.bfloat16
F32 = jnp.float32
MESH_ID = pl.DeviceIdType.MESH
QC = 768
GC = 1536
BLK = 256
ALL_Z = range(4)


def dot_nn(a, b):
    return lax.dot_general(a, b, (((1,), (0,)), ((), ())), preferred_element_type=F32)


def dot_nt(a, b):
    return lax.dot_general(a, b, (((1,), (1,)), ((), ())), preferred_element_type=F32)


def dot_tn(a, b):
    return lax.dot_general(a, b, (((0,), (0,)), ((), ())), preferred_element_type=F32)


N_SEND = 228
N_RECV = 202
VMEM_LIMIT = 64 * 2**20 - 2**18
DUE = (
    (7.4, 3.9, 7.3, 7.4), (11.9, 11.7, 11.7, 12.0), (8.8, 14.2, 13.0, 9.7),
    (20.8, 27.2, 17.5, 23.4), (34.9, 0.1, -9.8, 34.1), (25.4, 28.1, 21.9, 26.0),
    (40.3, 38.1, 32.4, 36.6), (48.5, 42.6, 35.7, 44.5), (45.2, 47.8, 34.6, 46.9),
    (14.5, 15.6, 16.3, 14.5), (10.4, 16.5, 9.7, 12.4), (23.1, 29.8, 22.4, 27.0),
    (32.0, 0.1, -6.8, 38.1), (57.0, 65.2, 60.2, 62.2), (61.7, 67.2, 61.5, 65.0),
    (66.1, 71.3, 62.2, 66.7), (69.3, 75.4, 63.6, 71.5), (68.4, 79.6, 68.2, 76.0),
    (77.0, 90.8, 72.4, 80.3), (81.5, -1.6, -7.1, 83.7), (87.1, -2.2, -5.7, 89.0),
    (93.9, 3.5, -2.1, 96.7), (23.0, 20.8, 15.4, 22.8), (30.9, 25.2, 29.5, 25.4),
    (87.5, 75.1, 84.1, 79.5), (86.6, 75.1, 84.1, 78.2), (138.0, 131.8, 133.0, 132.1),
    (140.9, 134.8, 137.4, 135.7), (57.7, 48.2, 42.4, 45.4), (64.8, 54.5, 47.9, 54.5),
    (64.0, 57.5, 56.9, 54.2), (71.7, 62.2, 62.8, 63.8), (126.9, 122.2, 121.7, 123.1),
    (127.5, 122.5, 122.0, 121.3), (127.8, 123.5, 124.4, 124.4), (129.3, 126.7, 128.7, 128.1),
    (121.0, -0.6, 0.4, -1.4), (-0.6, 131.6, 0.4, 0.8), (-3.0, 0.0, 135.0, 15.9),
    (-2.4, 0.0, -11.0, 138.6), (131.4, -4.5, -11.2, -0.2), (-3.2, 129.0, -11.8, -0.8),
    (-3.9, -1.5, 93.2, -1.5), (-31.7, -8.3, -8.3, 109.9), (111.3, -0.0, 2.6, 2.6),
    (4.1, 135.9, 12.0, 30.3), (-5.9, -1.2, 139.8, -1.2), (-22.8, -11.0, -35.4, 113.8),
    (121.2, 0.2, 0.2, 0.2), (-8.6, 141.6, 0.0, 0.0), (0.3, 0.6, 135.7, 0.2),
    (2.4, 0.3, 0.3, 129.0), (133.3, 130.6, 133.6, 132.5), (137.0, 134.1, 138.5, 138.2),
    (141.3, 140.0, 143.6, 141.2), (145.5, 143.0, 145.6, 144.5), (136.9, 0.0, 0.0, 22.1),
    (-3.0, 143.9, -0.2, 21.9), (-1.3, 0.0, 150.1, -1.8), (-1.3, 3.4, 0.0, 165.7),
    (149.7, 0.0, 1.1, 9.2), (0.0, 145.9, 0.0, 0.0), (0.0, 0.0, 142.5, -1.9),
    (0.0, -11.1, 0.0, 131.4), (135.9, -33.7, -6.1, -10.3), (0.0, 149.1, -4.7, -1.9),
    (42.9, 37.3, 197.8, 42.1), (0.0, -4.8, 0.0, 141.5), (145.5, -0.5, -11.4, -0.5),
    (0.5, 165.0, 0.3, 0.3), (-6.5, 2.9, 158.3, 0.3), (-32.2, -25.4, -25.5, 120.3),
    (151.0, 154.7, 148.8, 148.6), (161.6, 155.2, 157.7, 158.7), (155.8, 159.0, 158.8, 161.7),
    (162.6, 160.3, 165.3, 163.3), (147.6, -1.9, -1.9, -1.3), (-3.0, 164.7, -0.3, 1.1),
    (-4.9, -0.3, 171.0, 1.1), (-0.2, -0.2, 1.7, 178.4), (179.0, -0.7, 1.2, -0.7),
    (0.8, 176.5, 11.4, 0.8), (-10.9, -7.4, 160.6, -7.4), (0.8, 0.8, 1.8, 154.9),
    (156.0, 1.9, -1.4, -3.6), (-0.5, 174.8, -18.4, 0.8), (-6.1, -4.8, 178.6, -4.8),
    (-7.4, 0.8, 0.8, 164.4), (157.7, 1.3, 0.8, 3.4), (-8.2, 184.6, 0.0, 0.0),
    (0.6, -2.7, 176.8, -4.6), (-1.9, -0.6, -0.6, 164.5), (163.7, 164.2, 164.3, 164.6),
    (163.0, 164.9, 163.4, 164.6), (167.2, 166.7, 165.1, 169.2), (177.5, 172.0, 174.5, 177.5),
    (185.7, 2.2, 2.2, 2.2), (6.1, 189.7, -0.6, -0.6), (20.4, 13.4, 199.5, 13.4),
    (4.9, -0.4, -1.0, 178.1), (174.1, 172.0, 169.4, 171.2), (177.1, 172.3, 174.6, 173.2),
    (174.7, 172.2, 170.5, 169.9), (178.3, 167.3, 175.5, 177.5), (171.3, 1.2, 1.2, 1.7),
    (18.2, 183.3, -5.8, -5.8), (29.0, -5.9, 188.0, -5.8), (30.4, -5.5, -5.4, 189.7),
    (235.3, 2.5, 2.6, -2.8), (2.4, 194.0, -0.9, -3.7), (2.5, 0.0, 190.8, -22.0),
    (2.5, 0.0, -3.8, 159.8), (161.8, -17.6, -15.5, -29.3), (-4.6, 189.2, -0.1, -3.8),
    (7.3, 2.7, 204.9, 1.1), (4.4, -1.7, 3.1, 172.3), (184.9, 0.0, 5.9, -1.6),
    (6.0, 203.8, 7.3, -2.4), (0.1, -16.7, 200.8, -3.8), (2.8, 2.8, 8.7, 176.8),
    (189.5, 180.6, 181.3, 180.0), (178.6, 171.3, 170.1, 170.8), (188.9, 182.8, 180.4, 182.1),
    (190.8, 186.4, 180.5, 182.3), (189.4, 2.3, 22.4, -3.5), (0.2, 197.1, -2.8, -4.1),
    (-1.6, -1.6, 203.2, -3.8), (5.9, 5.9, 5.9, 211.5), (213.1, 10.2, 24.0, 13.9),
    (25.6, 227.2, 23.1, 11.7), (-1.7, -1.7, 197.8, -13.1), (5.4, 2.7, -5.1, 171.0),
    (189.2, -0.0, 8.4, -11.1), (-0.2, 202.5, -0.2, -11.1), (-2.2, -0.5, 206.1, -11.6),
    (-12.8, 19.4, -11.3, 162.0), (195.4, 4.9, -13.2, -22.2), (-2.0, 227.3, -7.8, -1.1),
    (-2.0, 12.2, 207.1, -1.1), (-11.1, -15.8, -11.4, 176.2),
)
LOOK = (
    (4.2, -4.7, -5.6, 7.3), (11.6, 11.7, 11.6, 11.5), (-5.0, 6.6, 6.5, 6.4),
    (14.0, 14.6, 7.4, 15.6), (21.6, 13.4, 13.3, 18.3), (15.5, 15.9, 16.0, 15.4),
    (18.6, 6.4, 12.4, 11.9), (19.3, 12.2, 17.8, 10.9), (37.7, 33.4, 33.0, 36.9),
    (37.4, 33.7, 34.5, 37.1), (48.5, 42.8, 49.7, 41.6), (52.4, 46.4, 53.8, 45.2),
    (55.9, 50.8, 57.5, 49.2), (60.5, 54.8, 61.7, 56.6), (58.7, 58.6, 64.8, 60.9),
    (74.6, 69.7, 77.0, 67.9), (59.0, 54.2, 59.3, 57.3), (68.8, 69.0, 70.2, 62.5),
    (96.9, 103.8, 95.6, 95.4), (106.4, 106.2, 107.0, 97.8), (114.3, 124.2, 124.9, 117.0),
    (123.4, 120.6, 121.3, 118.2), (130.0, 119.3, 124.9, 122.9), (114.7, 128.8, 129.4, 127.5),
    (131.9, 132.6, 130.3, 127.5), (140.0, 132.5, 131.8, 130.8), (148.4, 145.5, 137.3, 144.6),
    (132.9, 134.4, 124.2, 127.5), (148.3, 142.7, 144.3, 135.0), (143.8, 142.3, 143.9, 140.3),
    (146.3, 145.1, 142.6, 136.5), (160.5, 149.4, 151.8, 148.6), (163.8, 153.6, 152.8, 151.7),
    (168.9, 157.2, 159.8, 163.9), (176.2, 165.0, 167.3, 162.9), (177.5, 166.3, 169.4, 172.6),
    (185.2, 173.2, 176.5, 171.9), (184.9, 177.6, 176.9, 176.0), (198.3, 180.4, 187.4, 175.9),
    (194.9, 180.5, 186.0, 179.6), (202.5, 190.4, 191.3, 186.8), (204.0, 186.4, 196.2, 191.8),
    (204.9, 180.0, 197.2, 192.8), (194.0, 195.5, 206.1, 208.7),
)


SCRATCH = dict(
    TOK=((256, 1024), BF),
    STT=((4, 8, 128), F32),
    ST=((1024, 128), F32),
    COS=((1024, 128), F32),
    SIN=((1024, 128), F32),
    FV=((1024, 256), BF),
    COT=((1024, 1024), BF),
    N1=((1024, 1024), BF),
    N2=((1024, 1024), BF),
    DB=((1024, 1024), BF),
    GAZ=((4, 16, 128), F32),
    GAS=((2, 16, 128), F32),
    GAJ=((4, 16, 128), F32),
    RAW=((3, 32, 1024), BF),
    RAWG=((2, 32, 2816), BF),
    RAWD=((88, 1024), BF),
    SYD=((4, 96, 1024), BF),
    GV=((8, 1024), F32),
    WA=((2, 4, 4, 32, QC), BF),
    WO=((2, 4, 32, 1024), BF),
    WG=((2, 4, 4, 32, GC), BF),
    WD=((2, 4, 96, 1024), BF),
    QS=((1024, 256), BF),
    KR=((1024, 256), BF),
    V=((1024, 256), BF),
    O=((1024, 256), BF),
    DA=((1024, 256), BF),
    P0=((4, 256, 256), BF),
    P1=((4, 256, 512), BF),
    P2=((4, 256, 768), BF),
    P3=((4, 256, 1024), BF),
    DQ=((1024, 256), BF),
    DK=((1024, 256), F32),
    DV=((1024, 256), F32),
    DQKV=((1024, QC), BF),
    H=((1024, 768), BF),
    DGU=((1024, GC), BF),
    RES=((256, 1024), F32),
    DRES=((256, 1024), F32),
    SSA=((2, 256, 1024), BF),
    SRA=((2, 256, 1024), BF),
    XSA=((256, 1024), BF),
    XRA=((256, 1024), BF),
    SSB=((2, 256, 1024), BF),
    SRB=((2, 256, 1024), BF),
    XSB=((256, 1024), BF),
    XRB=((256, 1024), BF),
    FF=((256, 1024), F32),
    OUT=((256, 1024), BF),
    GQ=((4, 4, 32, QC), F32),
    GO=((4, 32, 1024), F32),
    GG=((4, 4, 32, GC), F32),
    GD=((4, 96, 1024), F32),
    RYQ=((4, 4, 32, QC), BF),
    RYO=((4, 32, 1024), BF),
    RYG=((4, 4, 32, GC), BF),
    RYD=((4, 96, 1024), BF),
    ZQ=((5, 4, 32, QC), BF),
    ZO=((5, 32, 1024), BF),
    ZG=((5, 4, 32, GC), BF),
    ZD=((5, 96, 1024), BF),
    GGS=((16, 128), F32),
    GGR=((3, 16, 128), F32),
    GGY=((16, 128), F32),
    GGT=((16, 128), F32),
    GGZ=((4, 16, 128), F32),
)


def slot_window(c):
    return 352 * c // 128 * 128, (352 * c + 352 + 127) // 128 * 128


def slot_map(c):
    lo, hi = slot_window(c)
    unit = lax.broadcasted_iota(jnp.int32, (hi - lo, 384), 0) + (lo - 352 * c)
    slot = lax.broadcasted_iota(jnp.int32, (hi - lo, 384), 1)
    block = (slot >= 96).astype(jnp.int32) + (slot >= 192).astype(jnp.int32)
    block = block + (slot >= 288).astype(jnp.int32)
    within = slot - 96 * block
    return ((unit == 88 * block + within) & (within < 88)).astype(F32).astype(BF)


def finish_kernel(*refs):
    (block, gtok, gfv, gq, gg, go, gd, gain) = refs[:8]
    (o_block, o_gtok, o_gfv, o_ga, o_q, o_k, o_v, o_o, o_gf, o_g, o_u, o_d) = refs[8:]
    o_block[...] = block[...]
    o_gtok[...] = gtok[...]
    o_gfv[...] = gfv[...]
    o_o[...] = go[...]
    o_d[...] = gd[0:88, :]
    for t, out in enumerate((o_q, o_k, o_v)):
        for h in range(2):
            for c in range(4):
                part = gq[c, :, 384 * h + 128 * t : 384 * h + 128 * t + 128]
                out[:, 128 * (c + 4 * h) : 128 * (c + 4 * h) + 128] = part.astype(F32)
    o_g[...] = jnp.zeros((32, 2816), F32)
    o_u[...] = jnp.zeros((32, 2816), F32)
    for c in range(4):
        lo, hi = slot_window(c)
        place = slot_map(c)
        parts = [gg[c, :, 384 * n : 384 * n + 384] for n in range(4)]
        back = dot_nt(jnp.concatenate(parts, axis=0), place)
        for t, out in enumerate((o_g, o_u)):
            for h in range(2):
                n = 2 * t + h
                out[:, 1408 * h + lo : 1408 * h + hi] += back[32 * n : 32 * n + 32, :]
    d = lax.axis_index("seq") * 4 + lax.axis_index("ctx")
    line = lax.broadcasted_iota(jnp.int32, (8, 128), 0) == d // 4
    for r, out in ((0, o_ga), (8, o_gf)):
        own = jnp.sum(jnp.where(line, gain[r : r + 8, :], 0.0), axis=0, keepdims=True)
        own = pltpu.roll(jnp.broadcast_to(own, (8, 128)), (128 - 32 * (d % 4)) % 128, 1)
        out[...] = own[0:1, 0:32]


class Step(tuple):
    def __lt__(self, other):
        return self[:2] < other[:2]


def layer_kernel(*refs):
    (tok, fv, cot, small, wq, wk, wv, wg, wu, wo, wdn) = refs[:11]
    (o_block, o_gtok, o_gfv, o_gq, o_gg, o_go, o_gd, o_gain) = refs[11:19]
    R = types.SimpleNamespace(**dict(zip(SCRATCH, refs[19:])))
    ssem, rsem, lsem = refs[19 + len(SCRATCH) :]
    gt, stt = small.at[0:16], small.at[16:24]
    sa, sg, wd = R.DQKV, R.DGU, R.DB.at[768:864]

    def pack(c):
        return slice(32 * c, 32 * c + 32)

    raw = [R.RAW.at[0], R.RAW.at[1], R.RAW.at[2], R.RAWG.at[0], R.RAWG.at[1], R.RAWD]
    fetch = [
        pltpu.make_async_copy(src, dst, lsem.at[14 + n])
        for n, (src, dst) in enumerate(zip((wq, wk, wv, wg, wu, wdn), raw))
    ]
    for f in fetch:
        f.start()
    wq, wk, wv, wg, wu, wdn = raw

    def prep():
        for f in fetch:
            f.wait()
        for t, w in enumerate((wq, wk, wv)):
            for h in range(2):
                for c in range(4):
                    lanes = pl.ds(128 * (c + 4 * h), 128)
                    sa[pack(c), 384 * h + 128 * t : 384 * h + 128 * t + 128] = w[:, lanes]
        for c in range(4):
            lo, hi = slot_window(c)
            place = slot_map(c)
            parts = [
                w[:, 1408 * h + lo : 1408 * h + hi] for w in (wg, wu) for h in range(2)
            ]
            part = dot_nn(jnp.concatenate(parts, axis=0), place).astype(BF)
            for n in range(4):
                sg[pack(c), 384 * n : 384 * n + 384] = part[32 * n : 32 * n + 32, :]
        wd[0:88, :] = wdn[...]
        wd[88:96, :] = jnp.zeros((8, 1024), BF)

    s = lax.axis_index("seq")
    z = lax.axis_index("ctx")
    y = s // 4
    j = s % 4
    x = j // 2
    k = j % 2
    ny = 1 - y
    sib = (4 * y + 2 * x + (1 - k), z)
    xp = (4 * y + 2 * (1 - x) + k, z)
    yp = (4 * ny + j, z)
    up_z, dn_z = (s, z + 1), (s, z - 1)
    column = (z + k) % 2
    crossing = x != column
    direct = x == column
    jp = 2 * (1 - x) + k

    def host(jj):
        return (4 * y + 2 * column + z // 2, jj)

    home = (4 * y + z, 2 * k + (x + z) % 2)
    at_home = (home[0] == s) & (home[1] == z)
    away = host(j)
    away_self = (away[0] == s) & (away[1] == z)
    b_me = 2 * k + (x + z) % 2
    b_x = 2 * k + (1 - x + z) % 2
    b_s = 2 * (1 - k) + (x + z) % 2
    b_xs = 2 * (1 - k) + (1 - x + z) % 2

    counters = [0, 0, 0]
    pend = []
    tasks = []
    made = [0, 0]

    def ids(n):
        made[0] += n
        return made[0] - n

    on_z = {q: z == q for q in ALL_Z}
    turn_of = [None]

    def guard():
        return None if turn_of[0] is None else on_z[turn_of[0]]

    def place():
        return z if turn_of[0] is None else turn_of[0]

    def later(i, fn, of=None):
        for q in ALL_Z if turn_of[0] is None else turn_of:
            tasks.append(Step((DUE[i][q], i, fn, of, q)))

    def due(q):
        return min([e for e in tasks if e[4] == q], default=None)

    def take(step):
        tasks.remove(step)
        turn_of[0] = step[4]
        step[2]()
        turn_of[0] = None

    def look():
        for q in ALL_Z:
            step = due(q)
            while step is not None and step[0] <= LOOK[made[1]][q]:
                take(step)
                step = due(q)
        made[1] += 1

    def flush(of=None):
        for q in ALL_Z:
            while any((of is None or e[3] is of) and e[4] == q for e in tasks):
                take(due(q))

    def snd(n=1):
        counters[0] += n
        assert counters[0] <= N_SEND
        return counters[0] - n

    def rcv(n=1):
        counters[2] += n
        assert counters[2] <= N_RECV
        return counters[2] - n

    def rows(b):
        return pl.ds(pl.multiple_of(b * BLK, BLK), BLK)

    def half_rows(b, h):
        return pl.ds(pl.multiple_of(b * BLK + 128 * h, 128), 128)

    def came(dst, r):
        return rc(dst, dst, 0, sib, r).wait_recv

    def rc(src, dst, i, dev, r):
        return pltpu.make_async_remote_copy(
            src_ref=src,
            dst_ref=dst,
            send_sem=ssem.at[i],
            recv_sem=rsem.at[r],
            device_id=dev,
            device_id_type=MESH_ID,
        )

    def both(p, q):
        if p is None or q is None or isinstance(p, bool) or isinstance(q, bool):
            if p is False or q is False:
                return False
            return p if q is None or q is True else q
        return p & q

    def when(cond, fn):
        cond = both(guard(), cond)
        if cond is None or cond is True:
            fn()
        elif cond is not False:
            pl.when(cond)(fn)

    def start(desc, cond=None):
        when(cond, desc.start)
        cond = both(guard(), cond)
        if cond is not False:
            pend.append((cond, desc))

    def local(src, dst):
        d = pltpu.make_async_copy(src, dst, lsem.at[counters[1]])
        counters[1] += 1
        d.start()
        return d

    def route(src, dst, i, self_cond, dev, r, cond=None):
        when(both(cond, self_cond), pltpu.make_async_copy(src, dst, rsem.at[r]).start)
        start(rc(src, dst, i, dev, r), both(cond, jnp.logical_not(self_cond)))

    def arrive(like_src, dst, r, self_cond):
        when(self_cond, pltpu.make_async_copy(like_src, dst, rsem.at[r]).wait)
        when(jnp.logical_not(self_cond), came(dst, r))

    def group_dev(c, jj):
        return (4 * y + c, jj)

    barrier = pltpu.get_barrier_semaphore()
    me = j * 4 + z
    for i in range(1, 16):
        t = (me + i) % 16
        pl.semaphore_signal(
            barrier, inc=1, device_id=(4 * y + t // 4, t % 4), device_id_type=MESH_ID
        )
    pl.semaphore_signal(barrier, inc=1, device_id=yp, device_id_type=MESH_ID)
    prep()
    pl.semaphore_wait(barrier, 16)

    i_gz, i_gy, i_gj = snd(4), snd(), snd(4)
    r_gz, r_gy, r_gj = rcv(4), rcv(), rcv(4)
    loc_gt = local(gt, R.GAZ.at[z])
    for c in range(4):
        start(rc(gt, R.GAZ.at[z], i_gz + c, (s, c), r_gz + z), z != c)

    class Move:
        def __init__(self, src, stage, pieces, arrivals):
            self.src, self.stage, self.pieces, self.arrivals = src, stage, pieces, arrivals
            n = len(pieces(j))
            self.ix, self.io, self.ir = snd(2), snd(n), snd(n)
            self.rx = rcv(2)

        def cross(self):
            for h in range(2):
                cut = pl.ds(128 * h, 128)
                start(rc(self.src.at[cut], self.stage.at[cut], self.ix + h, xp, self.rx + h), crossing)

        def own(self):
            for n, (cut, dst, self_cond, dev, r) in enumerate(self.pieces(j)):
                route(self.src.at[cut], dst, self.io + n, self_cond, dev, r, direct)

        def relay(self, h):
            pieces = self.pieces(jp)
            part = self.stage.at[pl.ds(128 * h, 128)]
            when(direct, came(part, self.rx + h))
            for n, (cut, dst, self_cond, dev, r) in enumerate(pieces):
                if (n == h) if len(pieces) == 2 else h == 1:
                    route(self.stage.at[cut], dst, self.ir + n, self_cond, dev, r, direct)

        def wait(self, part=None):
            for n, (like, dst, r, self_cond) in enumerate(self.arrivals()):
                if part is None or n == part:
                    arrive(like, dst, r, self_cond)

    last_hop_self = (z % 2 == k) & (b_me == z)

    def block_pieces(dst_at, base):
        def pieces(jj):
            dev = host(jj)
            self_cond = (dev[0] == s) & (dev[1] == z)
            return [
                (pl.ds(128 * h, 128), dst_at(z, h), self_cond, dev, base + h) for h in range(2)
            ]

        return pieces

    def block_arrivals(src, dst_at, base):
        return lambda: [
            (src.at[pl.ds(128 * h, 128)], dst_at(b_me, h), base + h, last_hop_self)
            for h in range(2)
        ]

    def tok_at(b, h):
        return R.TOK.at[pl.ds(128 * h, 128)]

    def cot_at(b, h):
        return R.COT.at[half_rows(b, h)]

    def fv_at(b, h):
        return R.FV.at[rows(b), pl.ds(128 * h, 128)]

    i_tok, i_cot, i_fv, i_st = rcv(2), rcv(2), rcv(8), rcv(4)
    s_st = snd(4)

    def fv_pieces(jj):
        out = []
        for c in range(4):
            dev = group_dev(c, jj)
            self_cond = (dev[0] == s) & (dev[1] == z)
            for h in range(2):
                cut = (slice(None), pl.ds(128 * (c + 4 * h), 128))
                out.append((cut, fv_at(z, h), self_cond, dev, i_fv + 2 * z + h))
        return out

    def fv_arrivals():
        out = []
        for b in range(4):
            self_cond = (z % 2 == k) & (z == b) & (x == (b + k) % 2)
            for h in range(2):
                out.append((fv.at[:, pl.ds(128 * h, 128)], fv_at(b, h), i_fv + 2 * b + h, self_cond))
        return out

    m_tok = Move(tok, R.DB.at[0:256], block_pieces(tok_at, i_tok), block_arrivals(tok, tok_at, i_tok))
    m_cot = Move(cot, R.DB.at[512:768], block_pieces(cot_at, i_cot), block_arrivals(cot, cot_at, i_cot))
    m_fv = Move(fv, R.DB.at[256:512], fv_pieces, fv_arrivals)

    m_tok.own()
    i_sa, i_sg, r_sa, r_sg = snd(4), snd(4), rcv(4), rcv(4)
    own_pack = pl.ds(pl.multiple_of(32 * j, 32), 32)
    loc_sa = local(sa.at[own_pack], R.WA.at[y, j, z])
    loc_wo = local(wo, R.WO.at[y, z])
    for c in range(4):
        start(rc(sa.at[pack(c)], R.WA.at[y, j, z], i_sa + c, group_dev(c, z), r_sa + j), j != c)
    m_tok.cross()
    loc_wd = local(wd, R.WD.at[y, z])
    loc_sg = local(sg.at[own_pack], R.WG.at[y, j, z])

    def wait_group(base, dst_of):
        for c in range(4):
            when(j != c, came(dst_of(c), base + c))

    class Gather:
        def __init__(self, piece):
            self.piece = piece
            self.iz, self.iy, self.rz, self.ry = snd(8), snd(4), rcv(4), rcv(4)

        def sources(self, step):
            at = place()
            below, above = at - step, at + step
            out = []
            for src, sem, target, here, on in (
                (below, self.iz, up_z, below >= 0, at < 3),
                (above, self.iz + 4, dn_z, above <= 3, at > 0),
            ):
                if here is not False:
                    out.append((src, sem, target, here, on))
            return out

        def send_z(self, step, cond=None):
            for src, sem, target, here, on in self.sources(step):
                p = self.piece(y, src)
                start(rc(p, p, sem + src, target, self.rz + src), both(cond, both(here, on)))

        def send_y(self, step):
            for src, _, _, here, _ in self.sources(step)[: 1 if step == 0 else 2]:
                p = self.piece(y, src)
                start(rc(p, p, self.iy + src, yp, self.ry + src), here)

        def recv(self, step):
            for src, _, _, here, _ in self.sources(step):
                when(here, came(self.piece(y, src), self.rz + src))

        def pass_on(self, step):
            self.recv(step)
            if step < 3:
                self.send_z(step)
            self.send_y(step)

        def finish(self):
            for zz in range(4):
                came(self.piece(ny, zz), self.ry + zz)()

    g_a = Gather(lambda yy, zz: R.WA.at[yy, :, zz])
    g_o = Gather(lambda yy, zz: R.WO.at[yy, zz])
    g_d = Gather(lambda yy, zz: R.WD.at[yy, zz])
    g_g0 = Gather(lambda yy, zz: R.WG.at[yy, 0:2, zz])
    g_g1 = Gather(lambda yy, zz: R.WG.at[yy, 2:4, zz])

    loc_gt.wait()
    for c in range(4):
        when(z != c, came(R.GAZ.at[c], r_gz + c))
    R.GAS[0] = R.GAZ[0] + R.GAZ[1] + R.GAZ[2] + R.GAZ[3]
    start(rc(R.GAS.at[0], R.GAS.at[1], i_gy, yp, r_gy))

    wait_group(r_sa, lambda c: R.WA.at[y, c, z])
    loc_sa.wait()
    loc_wo.wait()
    g_a.send_z(0)
    g_a.send_y(0)
    g_o.send_z(0)
    g_o.send_y(0)
    t_tok, t_a, t_move, t_o, t_ffn = ids(2), ids(3), ids(5), ids(3), ids(9)
    t_n1, t_n2, t_db, t_cot = ids(2), ids(2), ids(2), ids(4)
    later(t_tok, lambda: m_tok.relay(0), m_tok)
    later(t_tok + 1, lambda: m_tok.relay(1), m_tok)
    def pass_a(step):
        g_a.pass_on(step)
        later(t_o + step - 1, lambda: g_o.pass_on(step), g_o)
        if step == 1:
            later(t_a + 1, lambda: pass_a(2), g_a)
        if step == 2:
            later(t_a + 2, lambda: pass_a(3), g_a)
            later(t_move, first_move, m_fv)

    later(t_a, lambda: pass_a(1), g_a)

    came(R.GAS.at[1], r_gy)()
    R.GAJ[j] = R.GAS[0] + R.GAS[1]
    for c in range(4):
        start(rc(R.GAJ.at[j], R.GAJ.at[j], i_gj + c, group_dev(c, z), r_gj + j), j != c)
    first_packed = len(pend)
    for c in range(4):
        start(rc(sg.at[pack(c)], R.WG.at[y, j, z], i_sg + c, group_dev(c, z), r_sg + j), j != c)
    packed = pend[first_packed:]
    del pend[first_packed:]
    look()
    for c in range(4):
        self_c = (j == z) & (j == c)
        route(stt, R.STT.at[z], s_st + c, self_c, group_dev(c, j), i_st + z)
    loc_wd.wait()
    g_d.send_y(0)

    def own_shard():
        wait_group(r_sg, lambda c: R.WG.at[y, c, z])
        when(None, loc_sg.wait)
        g_g0.send_y(0)

    def first_move():
        m_fv.own()
        later(t_move + 1, second_move, m_fv)

    def second_move():
        m_fv.relay(0)
        m_fv.relay(1)
        m_cot.own()
        later(t_move + 2, lambda: third_move(0))

    def third_move(h):
        m_cot.relay(h)
        if h == 0:
            later(t_move + 3, lambda: third_move(1))
        else:
            for g in (g_d, g_g0, g_g1):
                g.send_z(0, direct)
            g_g1.send_y(0)
            for n in range(3):
                later(t_ffn + n, lambda n=n: pass_ffn(1, n))

    def pass_ffn(step, n):
        (g_d, g_g0, g_g1)[n].pass_on(step)
        if step < 3:
            later(t_ffn + 3 * step + n, lambda: pass_ffn(step + 1, n))

    later(t_move + 4, own_shard, m_tok)
    look()
    wait_group(r_gj, lambda c: R.GAJ.at[c])
    gains = R.GAJ[0] + R.GAJ[1] + R.GAJ[2] + R.GAJ[3]
    for r in range(8):
        R.GV[0:1, 128 * r : 128 * r + 128] = gains[r : r + 1, :]
        R.GV[1:2, 128 * r : 128 * r + 128] = gains[8 + r : 9 + r, :]
    look()

    class Share:
        def __init__(self, buf):
            self.buf = buf
            self.i, self.r = snd(6), rcv(6)

        def piece(self, b, h):
            return self.buf.at[half_rows(b, h)]

        def send(self, h):
            p = self.piece(b_me, h)
            start(rc(p, p, self.i + h, xp, self.r + h))
            start(rc(p, p, self.i + 2 + h, sib, self.r + 2 + h))

        def forward(self, h):
            p = self.piece(b_x, h)
            when(None, came(p, self.r + h))
            start(rc(p, p, self.i + 4 + h, sib, self.r + 4 + h))

        def near(self):
            for h in range(2):
                came(self.piece(b_s, h), self.r + 2 + h)()

        def far(self):
            for h in range(2):
                came(self.piece(b_xs, h), self.r + 4 + h)()

        def finish(self):
            self.near()
            self.far()

    sh1, sh2, sh3, sh_cot = Share(R.N1), Share(R.N2), Share(R.DB), Share(R.COT)

    def send_cot(h):
        m_cot.wait(h)
        sh_cot.send(h)
        if h == 0:
            later(t_cot + 1, lambda: send_cot(1))

    for h in range(2):
        flush(m_tok)
        look()
        m_tok.wait(h)
        xs = R.TOK[128 * h : 128 * h + 128, :].astype(F32)
        rs1 = lax.rsqrt(jnp.mean(xs * xs, axis=-1, keepdims=True) + norm_eps)
        R.N1[half_rows(b_me, h), :] = (xs * rs1 * R.GV[0:1, :]).astype(BF)
        sh1.send(h)
        later(t_n1 + h, lambda h=h: sh1.forward(h), sh1)
        look()
    m_fv.cross()
    m_cot.cross()
    later(t_cot, lambda: send_cot(0))
    look()
    for c in range(4):
        arrive(stt, R.STT.at[c], i_st + c, (j == z) & (c == z))
    for b in range(4):
        for r in range(2):
            row = R.STT[b, r : r + 1, :]
            R.ST[256 * b + 128 * r : 256 * b + 128 * r + 128, :] = jnp.transpose(
                jnp.broadcast_to(row, (128, 128))
            )
    lane = lax.broadcasted_iota(jnp.int32, (1, 128), 1)
    low_half = (lane % 64) < 32
    freq = jnp.exp((lane % 32).astype(F32) * (-2.0 / HD * 9.210340371976184))

    def angle_body(b, c):
        pos = (lax.broadcasted_iota(jnp.int32, (BLK, 128), 0) + b * BLK).astype(F32)
        ang = (pos - R.ST[rows(b), :]) * freq
        R.COS[rows(b), :] = jnp.cos(ang)
        R.SIN[rows(b), :] = jnp.where(low_half, -jnp.sin(ang), jnp.sin(ang))
        return c

    lax.fori_loop(0, 4, angle_body, 0)

    def turn(v):
        return jnp.where(low_half, pltpu.roll(v, 96, 1), pltpu.roll(v, 32, 1))

    flush(g_a)
    look()
    g_a.finish()
    flush(sh1)
    look()
    sh1.finish()
    flush(m_fv)
    look()
    m_fv.wait()
    for g in (g_d, g_g0, g_g1):
        g.send_z(0, crossing)

    def qkv_body(b, c):
        raw = dot_nn(R.N1[rows(b), :], R.WA[...].reshape(1024, QC))
        cs, sn = R.COS[rows(b), :], R.SIN[rows(b), :]
        for t in range(2):
            sl = slice(128 * t, 128 * t + 128)
            q = raw[:, 384 * t : 384 * t + 128]
            R.QS[rows(b), sl] = ((q * cs + turn(q) * sn).astype(BF).astype(F32) * 0.125).astype(BF)
            kk = raw[:, 384 * t + 128 : 384 * t + 256]
            R.KR[rows(b), sl] = (kk * cs + turn(kk) * sn).astype(BF)
            v = raw[:, 384 * t + 256 : 384 * t + 384]
            R.V[rows(b), sl] = (0.5 * v + 0.5 * R.FV[rows(b), sl].astype(F32)).astype(BF)
        return c

    lax.fori_loop(0, 4, qkv_body, 0)
    look()

    PB = [R.P0, R.P1, R.P2, R.P3]

    def head_parts(h):
        pair = pl.ds(pl.multiple_of((h // 2) * 128, 128), 128)
        mine = ((lane // 64) == (h % 2)).astype(F32)
        return pair, mine.astype(BF), mine

    def attn_body(h, c):
        pair, low_mine, mine = head_parts(h)
        for i in range(4):
            n = BLK * (i + 1)
            q = R.QS[BLK * i : n, pair] * low_mine
            sc = dot_nt(q, R.KR[0:n, pair])
            col = lax.broadcasted_iota(jnp.int32, (BLK, n), 1)
            row = lax.broadcasted_iota(jnp.int32, (BLK, n), 0) + BLK * i
            first = R.ST[BLK * i : n, 0:1].astype(jnp.int32)
            sc = jnp.where((col >= first) & (col <= row), sc, masked_score)
            top = jnp.max(sc, axis=-1, keepdims=True)
            e = jnp.exp(sc - top)
            p = (e * (1.0 / jnp.sum(e, axis=-1, keepdims=True))).astype(BF)
            PB[i][h] = p
            o = dot_nn(p, R.V[0:n, pair]) * mine
            R.O[BLK * i : n, pair] += o.astype(BF)
        return c

    R.O[...] = jnp.zeros((1024, 256), BF)
    lax.fori_loop(0, 2, attn_body, 0)
    look()
    lax.fori_loop(2, 4, attn_body, 0)
    look()

    class GroupSum:
        def __init__(self, bufs):
            self.ss, self.sr, self.xs, self.xr = bufs
            self.i, self.r = snd(4), rcv(4)

        def run(self, fn):
            self.ss[0] = fn(b_xs).astype(BF)
            d0 = rc(self.ss.at[0], self.sr.at[0], self.i, sib, self.r)
            d0.start()
            self.ss[1] = fn(b_s).astype(BF)
            d1 = rc(self.ss.at[1], self.sr.at[1], self.i + 1, sib, self.r + 1)
            d1.start()
            look()
            d0.wait_recv()
            self.xs[...] = (fn(b_x) + self.sr[0].astype(F32)).astype(BF)
            d2 = []
            for h in range(2):
                cut = pl.ds(128 * h, 128)
                d2.append(rc(self.xs.at[cut], self.xr.at[cut], self.i + 2 + h, xp, self.r + 2 + h))
                d2[h].start()
            R.FF[...] = fn(b_me)
            look()
            d1.wait_recv()
            R.FF[...] += self.sr[1].astype(F32)
            self.descs = (d0, d1, *d2)

        def result(self, h):
            look()
            self.descs[2 + h].wait_recv()
            cut = slice(128 * h, 128 * h + 128)
            return R.FF[cut, :] + self.xr[cut, :].astype(F32)

        def end(self):
            for d in self.descs:
                d.wait_send()

    set_a = (R.SSA, R.SRA, R.XSA, R.XRA)
    set_b = (R.SSB, R.SRB, R.XSB, R.XRB)
    flush(g_o)
    look()
    g_o.finish()
    sum_attn = GroupSum(set_a)
    sum_attn.run(lambda b: dot_nn(R.O[rows(b), :], R.WO[...].reshape(256, 1024)))
    for h in range(2):
        cut = slice(128 * h, 128 * h + 128)
        res = R.TOK[cut, :].astype(F32) + sum_attn.result(h)
        R.RES[cut, :] = res
        rs2 = lax.rsqrt(jnp.mean(res * res, axis=-1, keepdims=True) + norm_eps)
        R.N2[half_rows(b_me, h), :] = (res * rs2 * R.GV[1:2, :]).astype(BF)
        sh2.send(h)
    sum_attn.end()
    flush()
    sh_cot.forward(0)
    sh_cot.forward(1)
    for g in (g_d, g_g0, g_g1):
        g.finish()

    def ffn_body(b, c):
        gu = dot_nn(R.N2[rows(b), :], R.WG[...].reshape(1024, GC))
        gate, up = gu[:, :768], gu[:, 768:]
        sig = 1.0 / (1.0 + jnp.exp(-gate))
        silu = gate * sig
        R.H[rows(b), :] = (silu * up).astype(BF)
        dh = dot_nt(R.COT[rows(b), :], R.WD[...].reshape(768, 1024))
        R.DGU[rows(b), 0:768] = (dh * up * (sig * (1.0 + gate * (1.0 - sig)))).astype(BF)
        R.DGU[rows(b), 768:1536] = (dh * silu).astype(BF)
        return c

    for cond, desc in packed:
        when(cond, desc.wait_send)
    ffn_body(b_me, 0)
    sh2.near()
    sh_cot.near()
    ffn_body(b_s, 0)
    sh2.forward(0)
    sh2.forward(1)
    ffn_body(b_x, 0)
    sh2.far()
    sh_cot.far()
    ffn_body(b_xs, 0)
    for cond, desc in pend:
        when(cond, desc.wait_send)
    pend.clear()

    class Reduce:
        def __init__(self, g, sy, ry, zr, cs):
            self.g, self.sy, self.ry, self.zr = g, sy, ry, zr
            self.cs = cs
            self.iy, self.iz, self.r, self.rz = snd(4), snd(4), rcv(4), rcv(5)

        def cut(self, ref, o):
            if self.cs is None:
                return ref.at[o]
            return ref.at[self.cs[0] : self.cs[1], o]

        def zslot(self, o):
            if self.cs is None:
                return self.zr.at[o]
            return self.zr.at[o, self.cs[0] : self.cs[1]]

        def chunks(self):
            return [None] if self.cs is None else range(*self.cs)

        def chunk(self, o, c):
            return self.zr.at[o] if c is None else self.zr.at[o, c]

        def term(self, o, c):
            at = o if c is None else (c, o)
            return self.g[at] + self.ry[at].astype(F32)

        def send_y(self):
            for o in (3, 0, 2, 1):
                start(rc(self.cut(self.sy, o), self.cut(self.ry, o), self.iy + o, yp, self.r + o))

        def recv_y(self, o):
            when(None, came(self.cut(self.ry, o), self.r + o))

        def hop(self, o, upward, zz):
            if upward:
                head, target, slot_out = zz == 0, up_z, o
            else:
                head, target = zz == 3, dn_z
                slot_out = 4 if zz - 1 == o else o
            d = rc(self.zslot(o), self.zslot(slot_out), self.iz + o, target, self.rz + slot_out)

            def go():
                if not head:
                    came(self.zslot(o), self.rz + o)()
                for c in self.chunks():
                    p = self.chunk(o, c)
                    val = self.term(o, c)
                    if not head:
                        val = val + p[...].astype(F32)
                    p[...] = val.astype(BF)
                d.start()

            pl.when(z == zz)(go)
            pend.append((z == zz, d))

        def last(self, zz, put):
            def go():
                if zz > 0:
                    came(self.zslot(zz), self.rz + zz)()
                if zz < 3:
                    came(self.zslot(4), self.rz + 4)()
                for c in self.chunks():
                    val = self.term(zz, c)
                    if zz > 0:
                        val = val + self.chunk(zz, c)[...].astype(F32)
                    if zz < 3:
                        val = val + self.chunk(4, c)[...].astype(F32)
                    put(c, val)

            pl.when(z == zz)(go)

        def schedule(self, put):
            t = ids(20)

            def take_y(n):
                o = (3, 0, 2, 1)[n]
                self.recv_y(o)
                zz = turn_of[0]
                later(t + 4 + 4 * n + zz, lambda: step(o, zz), self)
                if n < 3:
                    later(t + n + 1, lambda: take_y(n + 1), self)

            def step(o, zz):
                if zz == o:
                    self.last(o, put)
                else:
                    self.hop(o, zz < o, zz)

            later(t, lambda: take_y(0), self)

    class Direct(Reduce):
        def send_term(self, o):
            d = rc(self.cut(self.ry, o), self.zslot(z), self.iz + o, (s, o), self.rz + z)

            def go():
                for c in self.chunks():
                    p = self.ry.at[o] if c is None else self.ry.at[c, o]
                    p[...] = self.term(o, c).astype(BF)
                d.start()

            if place() != o:
                when(None, go)
                pend.append((guard(), d))

        def gather(self, zz, put):
            def go():
                for o in range(4):
                    if o != zz:
                        came(self.zslot(o), self.rz + o)()
                for c in self.chunks():
                    val = self.term(zz, c)
                    for o in range(4):
                        if o != zz:
                            val = val + self.chunk(o, c)[...].astype(F32)
                    put(c, val)

            pl.when(z == zz)(go)

        def schedule(self, put):
            t = ids(8)

            def take_y(n):
                o = (3, 0, 2, 1)[n]
                self.recv_y(o)
                self.send_term(o)
                if n < 3:
                    later(t + n + 1, lambda: take_y(n + 1), self)
                else:
                    zz = turn_of[0]
                    later(t + 4 + zz, lambda: self.gather(zz, put), self)

            later(t, lambda: take_y(0), self)

    def half(yy, width):
        return pl.ds(pl.multiple_of(yy * width, width), width)

    def grad_cols(left, right, g, sy, yy, m, keep):
        width = right.shape[1]
        a = left[:, pl.ds(pl.multiple_of(yy * 512 + 256 * m, 256), 256)]
        val = dot_tn(a, right[...]).reshape(2, 4, 32, width)
        if keep:
            g[2 * m : 2 * m + 2] = val
        else:
            sy[2 * m : 2 * m + 2] = val.astype(BF)

    def grad_rows(left, right, g, sy, yy, per, keep):
        a = left[:, half(yy, 4 * per)]
        val = dot_tn(a, right[...]).reshape(4, per, 1024)
        if keep:
            g[...] = val
        else:
            sy[...] = val.astype(BF)

    red_d = Reduce(R.GD, R.SYD, R.RYD, R.ZD, None)
    red_g0 = Reduce(R.GG, R.WG.at[0], R.RYG, R.ZG, (0, 2))
    red_g1 = Reduce(R.GG, R.WG.at[0], R.RYG, R.ZG, (2, 4))
    red_o = Direct(R.GO, R.WO.at[0], R.RYO, R.ZO, None)

    def put_rows(ref):
        def put(c, val):
            ref[...] = val

        return put

    def put_cols(ref):
        def put(c, val):
            ref[c, 0] = val

        return put

    grad_rows(R.H, R.COT, None, R.SYD, ny, 96, False)
    red_d.send_y()
    sum_dn2 = GroupSum(set_a)
    sum_dn2.run(lambda b: dot_nt(R.DGU[rows(b), :], R.WG[...].reshape(1024, GC)))
    for m, red in ((0, red_g0), (1, red_g1)):
        grad_cols(R.N2, R.DGU, None, R.WG.at[0], ny, m, False)
        red.send_y()
    grad_rows(R.H, R.COT, R.GD, None, y, 96, True)
    red_d.schedule(put_rows(R.GD.at[0]))
    look()
    for m in range(2):
        grad_cols(R.N2, R.DGU, R.GG, None, y, m, True)
    red_g0.schedule(put_cols(R.GG))
    red_g1.schedule(put_cols(R.GG))

    R.GGS[...] = jnp.zeros((16, 128), F32)

    def add_gain(first, row):
        for r in range(8):
            R.GGS[first + r : first + r + 1, :] += row[:, 128 * r : 128 * r + 128]

    for h in range(2):
        cut = slice(128 * h, 128 * h + 128)
        dn2 = sum_dn2.result(h)
        res = R.RES[cut, :]
        rs2 = lax.rsqrt(jnp.mean(res * res, axis=-1, keepdims=True) + norm_eps)
        xh = res * rs2
        gd = dn2 * R.GV[1:2, :]
        add_gain(8, jnp.sum(dn2 * xh, axis=0, keepdims=True))
        dres = R.COT[half_rows(b_me, h), :].astype(F32) + rs2 * (
            gd - xh * jnp.mean(gd * xh, axis=-1, keepdims=True)
        )
        R.DRES[cut, :] = dres
        R.DB[half_rows(b_me, h), :] = dres.astype(BF)
        sh3.send(h)
        later(t_db + h, lambda h=h: sh3.forward(h), sh3)
    sum_dn2.end()
    look()
    sum_out = GroupSum(set_b)
    sum_out.run(lambda b: dot_nn(R.H[rows(b), :], R.WD[...].reshape(768, 1024)))
    look()
    flush(sh3)
    look()
    sh3.finish()

    def da_body(b, c):
        R.DA[rows(b), :] = dot_nt(R.DB[rows(b), :], R.WO[...].reshape(256, 1024)).astype(BF)
        return c

    lax.fori_loop(0, 4, da_body, 0)
    grad_rows(R.O, R.DB, None, R.WO.at[0], ny, 32, False)
    red_o.send_y()
    grad_rows(R.O, R.DB, R.GO, None, y, 32, True)
    red_o.schedule(put_rows(R.GO.at[0]))
    look()
    i_out, r_out = snd(2), rcv(2)
    for h in range(2):
        cut = slice(128 * h, 128 * h + 128)
        R.OUT[cut, :] = (R.RES[cut, :] + sum_out.result(h)).astype(BF)
        part = pl.ds(128 * h, 128)
        route(R.OUT.at[part], o_block.at[part], i_out + h, at_home, home, r_out + h)
    sum_out.end()
    R.DK[...] = jnp.zeros((1024, 256), F32)
    R.DV[...] = jnp.zeros((1024, 256), F32)

    def back_body(h, c):
        pair, low_mine, mine = head_parts(h)
        for i in range(4):
            n = BLK * (i + 1)
            do = R.DA[BLK * i : n, pair] * low_mine
            q = R.QS[BLK * i : n, pair] * low_mine
            dp = dot_nt(do, R.V[0:n, pair])
            pb = PB[i][h]
            p = pb.astype(F32)
            delta = jnp.sum(p * dp, axis=-1, keepdims=True)
            ds = (p * (dp - delta)).astype(BF)
            dq = dot_nn(ds, R.KR[0:n, pair]) * (0.125 * mine)
            R.DQ[BLK * i : n, pair] += dq.astype(BF)
            R.DK[0:n, pair] += dot_tn(ds, q)
            R.DV[0:n, pair] += dot_tn(pb, do)
        return c

    def pair_lanes(p):
        return pl.ds(384 * p, 384)

    def grad_pair(p, sy, yy, keep):
        for m in range(2):
            a = R.N1[:, pl.ds(pl.multiple_of(yy * 512 + 256 * m, 256), 256)]
            val = dot_tn(a, R.DQKV[:, pair_lanes(p)]).reshape(2, 4, 32, 384)
            if keep:
                R.GQ[2 * m : 2 * m + 2, :, :, pair_lanes(p)] = val
            else:
                sy[2 * m : 2 * m + 2] = val.astype(BF)

    red_q, i_gf, r_gf = [], snd(8), rcv(8)
    for p in range(2):
        sy = R.WG.at[1, :, :, :, pair_lanes(p)]
        cut = [r.at[:, :, :, pair_lanes(p)] for r in (R.GQ, R.RYQ, R.ZQ)]
        red_q.append(Reduce(cut[0], sy, cut[1], cut[2], (0, 4)))
    R.DQ[...] = jnp.zeros((1024, 256), BF)
    for p in range(2):
        for h in (2 * p, 2 * p + 1):
            lax.fori_loop(h, h + 1, back_body, 0)
            look()

        def dqkv_body(b, c):
            cs, sn = R.COS[rows(b), :], R.SIN[rows(b), :]
            sl = slice(128 * p, 128 * p + 128)
            u = R.DQ[rows(b), sl].astype(F32)
            R.DQKV[rows(b), 384 * p : 384 * p + 128] = (u * cs - turn(u) * sn).astype(BF)
            u = R.DK[rows(b), sl].astype(BF).astype(F32)
            R.DQKV[rows(b), 384 * p + 128 : 384 * p + 256] = (u * cs - turn(u) * sn).astype(BF)
            R.DQKV[rows(b), 384 * p + 256 : 384 * p + 384] = (
                0.5 * R.DV[rows(b), sl].astype(BF).astype(F32)
            ).astype(BF)
            return c

        lax.fori_loop(0, 4, dqkv_body, 0)
        grad_pair(p, red_q[p].sy, ny, False)
        red_q[p].send_y()
        for b in range(4):
            self_b = (j == z) & (z == b)
            src = R.DQKV.at[pl.ds(256 * b, 256), pl.ds(384 * p + 256, 128)]
            dst = o_gfv.at[:, pl.ds(pl.multiple_of(128 * (j + 4 * p), 128), 128)]
            route(src, dst, i_gf + 2 * b + p, self_b, (4 * y + z, b), r_gf + 2 * j + p)
        if p == 0:
            grad_pair(p, None, y, True)
            red_q[p].schedule(put_cols(red_q[p].g))
    sum_dn1 = GroupSum(set_a)
    sum_dn1.run(lambda b: dot_nt(R.DQKV[rows(b), :], R.WA[...].reshape(1024, QC)))
    grad_pair(1, None, y, True)
    red_q[1].schedule(put_cols(red_q[1].g))
    look()

    i_gtok, r_gtok = snd(2), rcv(2)
    for h in range(2):
        cut = slice(128 * h, 128 * h + 128)
        dn1 = sum_dn1.result(h)
        xs = R.TOK[cut, :].astype(F32)
        rs1 = lax.rsqrt(jnp.mean(xs * xs, axis=-1, keepdims=True) + norm_eps)
        xh = xs * rs1
        gd = dn1 * R.GV[0:1, :]
        add_gain(0, jnp.sum(dn1 * xh, axis=0, keepdims=True))
        R.XSB[cut, :] = (
            R.DRES[cut, :] + rs1 * (gd - xh * jnp.mean(gd * xh, axis=-1, keepdims=True))
        ).astype(BF)
        part = pl.ds(128 * h, 128)
        route(R.XSB.at[part], o_gtok.at[part], i_gtok + h, at_home, home, r_gtok + h)
    sum_dn1.end()

    i_ggg, i_ggy, i_ggz = snd(4), snd(), snd(4)
    r_ggg, r_ggy, r_ggz = rcv(4), rcv(), rcv(4)
    for c in range(4):
        start(
            rc(R.GGS, R.GGR.at[(j - c - 1) % 4], i_ggg + c, group_dev(c, z), r_ggg + j), j != c
        )
    look()
    for c in range(4):
        when(j != c, came(R.GGR.at[(c - j - 1) % 4], r_ggg + c))
    R.GGT[...] = R.GGS[...] + R.GGR[0] + R.GGR[1] + R.GGR[2]
    start(rc(R.GGT, R.GGY, i_ggy, yp, r_ggy))
    look()
    came(R.GGY, r_ggy)()
    R.GGZ[z] = R.GGT[...] + R.GGY[...]
    for c in range(4):
        start(rc(R.GGZ.at[z], R.GGZ.at[z], i_ggz + c, (s, c), r_ggz + z), z != c)

    i_rg, i_rq, r_rg, r_rq = snd(4), snd(4), rcv(4), rcv(4)
    outs = []

    def hand_back(g, send, out, base, r):
        for c in range(4):
            send[c] = g[c, 0].astype(BF)
            start(rc(send.at[c], out.at[j], base + c, group_dev(c, z), r + j), j != c)
        outs.append(local(send.at[j], out.at[j]))

    look()
    for red in (red_d, red_g0, red_g1):
        flush(red)
    hand_back(R.GG, R.RYG.at[0], o_gg, i_rg, r_rg)
    outs.append(local(R.GD.at[0], o_gd))
    flush()
    hand_back(R.GQ, R.RYQ.at[0], o_gq, i_rq, r_rq)
    outs.append(local(R.GO.at[0], o_go))
    for c in range(4):
        when(z != c, came(R.GGZ.at[c], r_ggz + c))
    R.GGY[...] = R.GGZ[0] + R.GGZ[1] + R.GGZ[2] + R.GGZ[3]
    outs.append(local(R.GGY, o_gain))

    for h in range(2):
        part = pl.ds(128 * h, 128)
        arrive(R.OUT.at[part], o_block.at[part], r_out + h, away_self)
        arrive(R.XSB.at[part], o_gtok.at[part], r_gtok + h, away_self)
    for c in range(4):
        self_c = (j == z) & (j == c)
        for h in range(2):
            src = R.DQKV.at[pl.ds(256 * z, 256), pl.ds(384 * h + 256, 128)]
            dst = o_gfv.at[:, pl.ds(pl.multiple_of(128 * (c + 4 * h), 128), 128)]
            arrive(src, dst, r_gf + 2 * c + h, self_c)
    wait_group(r_rg, lambda c: o_gg.at[c])
    wait_group(r_rq, lambda c: o_gq.at[c])
    for d in outs:
        d.wait()
    for cond, desc in pend:
        when(cond, desc.wait_send)


def fast_device(
    tokens,
    first_values,
    gain_attn,
    w_query,
    w_key,
    w_value,
    w_out,
    gain_ffn,
    w_gate,
    w_up,
    w_down,
    segment_start,
    cotangent,
):
    d = lax.axis_index("seq") * 4 + lax.axis_index("ctx")
    mine = jnp.arange(1024, dtype=jnp.int32) // 32 == d

    def spot(g):
        return jnp.where(mine, jnp.tile(g.astype(F32), 32), 0.0).reshape(8, 128)

    starts = jnp.pad(segment_start.astype(F32).reshape(2, 128), ((0, 6), (0, 0)))
    small = jnp.concatenate([spot(gain_attn), spot(gain_ffn), starts])
    hbm = pl.BlockSpec(memory_space=pl.ANY)
    vmem = pl.BlockSpec(memory_space=pltpu.VMEM)
    outs = pl.pallas_call(
        layer_kernel,
        name="layer",
        out_shape=[
            jax.ShapeDtypeStruct((256, 1024), BF),
            jax.ShapeDtypeStruct((256, 1024), BF),
            jax.ShapeDtypeStruct((256, 1024), BF),
            jax.ShapeDtypeStruct((4, 32, QC), BF),
            jax.ShapeDtypeStruct((4, 32, GC), BF),
            jax.ShapeDtypeStruct((32, 1024), F32),
            jax.ShapeDtypeStruct((96, 1024), F32),
            jax.ShapeDtypeStruct((16, 128), F32),
        ],
        in_specs=[hbm] * 11,
        out_specs=[hbm] * 8,
        scratch_shapes=[pltpu.VMEM(shape, dtype) for shape, dtype in SCRATCH.values()]
        + [
            pltpu.SemaphoreType.DMA((N_SEND,)),
            pltpu.SemaphoreType.DMA((N_RECV,)),
            pltpu.SemaphoreType.DMA((20,)),
        ],
        compiler_params=pltpu.CompilerParams(
            collective_id=0, has_side_effects=True, vmem_limit_bytes=VMEM_LIMIT
        ),
    )(
        tokens,
        first_values,
        cotangent,
        small,
        w_query,
        w_key,
        w_value,
        w_gate,
        w_up,
        w_out,
        w_down,
    )
    res = pl.pallas_call(
        finish_kernel,
        name="finish",
        out_shape=[
            jax.ShapeDtypeStruct((256, 1024), BF),
            jax.ShapeDtypeStruct((256, 1024), BF),
            jax.ShapeDtypeStruct((256, 1024), BF),
            jax.ShapeDtypeStruct((1, 32), F32),
            jax.ShapeDtypeStruct((32, 1024), F32),
            jax.ShapeDtypeStruct((32, 1024), F32),
            jax.ShapeDtypeStruct((32, 1024), F32),
            jax.ShapeDtypeStruct((32, 1024), F32),
            jax.ShapeDtypeStruct((1, 32), F32),
            jax.ShapeDtypeStruct((32, 2816), F32),
            jax.ShapeDtypeStruct((32, 2816), F32),
            jax.ShapeDtypeStruct((88, 1024), F32),
        ],
        in_specs=[vmem] * 8,
        out_specs=[vmem] * 12,
        compiler_params=pltpu.CompilerParams(vmem_limit_bytes=64 * 2**20),
    )(*outs)
    return tuple(r.reshape(32) if n in (3, 8) else r for n, r in enumerate(res))


def solution(mesh):
    fits = mesh.shape["seq"] == 8 and mesh.shape["ctx"] == 4
    return jax.shard_map(
        fast_device if fits else per_device,
        mesh=mesh,
        in_specs=(
            P(("seq", "ctx"), None),
            P(("seq", "ctx"), None),
            P(("seq", "ctx")),
            P(("seq", "ctx"), None),
            P(("seq", "ctx"), None),
            P(("seq", "ctx"), None),
            P(("seq", "ctx"), None),
            P(("seq", "ctx")),
            P(("seq", "ctx"), None),
            P(("seq", "ctx"), None),
            P(("seq", "ctx"), None),
            P(("seq", "ctx")),
            P(("seq", "ctx"), None),
        ),
        out_specs=(
            P(("seq", "ctx"), None),
            P(("seq", "ctx"), None),
            P(("seq", "ctx"), None),
            P(("seq", "ctx")),
            P(("seq", "ctx"), None),
            P(("seq", "ctx"), None),
            P(("seq", "ctx"), None),
            P(("seq", "ctx"), None),
            P(("seq", "ctx")),
            P(("seq", "ctx"), None),
            P(("seq", "ctx"), None),
            P(("seq", "ctx"), None),
        ),
        check_vma=False,
    )
```

```python
import types

import jax
import jax.numpy as jnp
from jax import lax
from jax.experimental import pallas as pl
from jax.experimental.pallas import tpu as pltpu
from jax.sharding import PartitionSpec as P

HEADS = 16
HD = 64


norm_eps = 1e-06
masked_score = -2e30
start_score = -1e30


def rms_scale(features, scale_gain):
    return (
        features
        * lax.rsqrt(jnp.mean(features * features, axis=-1, keepdims=True) + norm_eps)
        * scale_gain
    )


def rope_angles(positions, head_size):
    half_size = head_size // 2
    frequency = 10000.0 ** (-(jnp.arange(half_size, dtype=jnp.float32) * 2.0) / head_size)
    angles = positions.astype(jnp.float32)[:, None] * frequency[None, :]
    return jnp.concatenate([angles, angles], axis=-1)


def rotate(features, angles):
    half_size = features.shape[-1] // 2
    turned = jnp.concatenate([-features[..., half_size:], features[..., :half_size]], axis=-1)
    return features * jnp.cos(angles)[:, None, :] + turned * jnp.sin(angles)[:, None, :]


def block_size(shard_rows):
    size_guess = shard_rows * max(1, 640 // shard_rows)
    return size_guess


def masked_scores(queries, keys_part, query_index, query_start, key_index, key_start, score_scale):
    scores = (
        jnp.einsum("qhd,khd->hqk", queries, keys_part, preferred_element_type=jnp.float32)
        * score_scale
    )
    allowed = (query_start[:, None] == key_start[None, :]) & (
        key_index[None, :] <= query_index[:, None]
    )
    return jnp.where(allowed[None], scores, masked_score)


def per_device(
    tokens,
    first_values,
    gain_attn,
    w_query,
    w_key,
    w_value,
    w_out,
    gain_ffn,
    w_gate,
    w_up,
    w_down,
    segment_start,
    cotangent,
):
    tok_rows, model_width = tokens.shape
    score_scale = HD ** (-0.5)
    own_weights = (gain_attn, w_query, w_key, w_value, w_out, gain_ffn, w_gate, w_up, w_down)
    full_weights = (
        lax.all_gather(own_weights[0], ("seq", "ctx"), axis=0, tiled=True),
        lax.all_gather(own_weights[1], ("seq", "ctx"), axis=0, tiled=True),
        lax.all_gather(own_weights[2], ("seq", "ctx"), axis=0, tiled=True),
        lax.all_gather(own_weights[3], ("seq", "ctx"), axis=0, tiled=True),
        lax.all_gather(own_weights[4], ("seq", "ctx"), axis=0, tiled=True),
        lax.all_gather(own_weights[5], ("seq", "ctx"), axis=0, tiled=True),
        lax.all_gather(own_weights[6], ("seq", "ctx"), axis=0, tiled=True),
        lax.all_gather(own_weights[7], ("seq", "ctx"), axis=0, tiled=True),
        lax.all_gather(own_weights[8], ("seq", "ctx"), axis=0, tiled=True),
    )
    all_starts = lax.all_gather(segment_start, "ctx", axis=0, tiled=True)
    own_index = lax.axis_index("ctx") * tok_rows + jnp.arange(tok_rows, dtype=jnp.int32)
    angles = rope_angles(own_index - segment_start, HD)
    (
        gain_one,
        query_weight,
        key_weight,
        value_weight,
        out_weight,
        gain_two,
        gate_weight,
        up_weight,
        down_weight,
    ) = full_weights
    token_float = tokens.astype(jnp.float32)
    normed = rms_scale(token_float, gain_one.astype(jnp.float32)).astype(jnp.bfloat16)
    query_raw = jnp.dot(normed, query_weight, preferred_element_type=jnp.float32).reshape(
        tok_rows, HEADS, HD
    )
    key_raw = jnp.dot(normed, key_weight, preferred_element_type=jnp.float32).reshape(
        tok_rows, HEADS, HD
    )
    queries = rotate(query_raw, angles).astype(jnp.bfloat16)
    keys_rot = rotate(key_raw, angles).astype(jnp.bfloat16)
    values = (
        0.5 * jnp.dot(normed, value_weight, preferred_element_type=jnp.float32)
        + 0.5 * first_values.astype(jnp.float32)
    ).astype(jnp.bfloat16)
    values_heads = values.reshape(tok_rows, HEADS, HD)
    keys_flat = keys_rot.reshape(tok_rows, model_width)
    forward_init = (
        jnp.full((HEADS, tok_rows), start_score, jnp.float32),
        jnp.zeros((HEADS, tok_rows), jnp.float32),
        jnp.zeros((HEADS, tok_rows, HD), jnp.float32),
    )
    running = forward_init
    key_piece = lax.all_gather(keys_flat, "ctx", axis=0, tiled=True)
    value_piece = lax.all_gather(values, "ctx", axis=0, tiled=True)
    piece_rows = key_piece.shape[0]
    size_now = block_size(tok_rows)
    block_count = piece_rows // size_now
    key_blocks = key_piece.reshape(block_count, size_now, HEADS, HD)
    value_blocks = value_piece.reshape(block_count, size_now, HEADS, HD)
    block_starts = jnp.arange(block_count, dtype=jnp.int32) * size_now

    def forward_one_block(partial_value, inputs):
        key_block, value_block, block_start = inputs
        key_index = block_start + jnp.arange(size_now, dtype=jnp.int32)
        key_start = lax.dynamic_slice_in_dim(all_starts, block_start, size_now)
        run_max, run_sum, accum_out = partial_value
        scores = masked_scores(
            queries, key_block, own_index, segment_start, key_index, key_start, score_scale
        )
        new_max = jnp.maximum(run_max, jnp.max(scores, axis=-1))
        weights = jnp.exp(scores - new_max[..., None])
        factor = jnp.exp(run_max - new_max)
        new_sum = run_sum * factor + jnp.sum(weights, axis=-1)
        new_accum = accum_out * factor[..., None] + jnp.einsum(
            "hqk,khd->hqd",
            weights.astype(jnp.bfloat16),
            value_block,
            preferred_element_type=jnp.float32,
        )
        partial_value = (new_max, new_sum, new_accum)
        return (partial_value, None)

    running, _ = lax.scan(forward_one_block, running, (key_blocks, value_blocks, block_starts))
    run_max, run_sum, accum_out = running
    attn_heads = accum_out / run_sum[..., None]
    log_total = run_max + jnp.log(run_sum)
    attn_low = attn_heads.transpose(1, 0, 2).reshape(tok_rows, model_width).astype(jnp.bfloat16)
    resid = token_float + jnp.dot(attn_low, out_weight, preferred_element_type=jnp.float32)
    normed_two = rms_scale(resid, gain_two.astype(jnp.float32)).astype(jnp.bfloat16)
    gate = jnp.dot(normed_two, gate_weight, preferred_element_type=jnp.float32)
    up_proj = jnp.dot(normed_two, up_weight, preferred_element_type=jnp.float32)
    hidden = (jax.nn.silu(gate) * up_proj).astype(jnp.bfloat16)
    block_out = (resid + jnp.dot(hidden, down_weight, preferred_element_type=jnp.float32)).astype(
        jnp.bfloat16
    )
    grad_down = jnp.einsum("tf,td->fd", hidden, cotangent, preferred_element_type=jnp.float32)
    d_hidden = jnp.einsum("td,fd->tf", cotangent, down_weight, preferred_element_type=jnp.float32)
    silu_value, silu_back = jax.vjp(jax.nn.silu, gate)
    d_gate = silu_back(d_hidden * up_proj)[0].astype(jnp.bfloat16)
    d_up = (d_hidden * silu_value).astype(jnp.bfloat16)
    grad_gate = jnp.einsum("td,tf->df", normed_two, d_gate, preferred_element_type=jnp.float32)
    grad_up = jnp.einsum("td,tf->df", normed_two, d_up, preferred_element_type=jnp.float32)
    d_normed_two = jnp.einsum(
        "tf,df->td", d_gate, gate_weight, preferred_element_type=jnp.float32
    ) + jnp.einsum("tf,df->td", d_up, up_weight, preferred_element_type=jnp.float32)
    _, norm_two_back = jax.vjp(rms_scale, resid, gain_two.astype(jnp.float32))
    resid_part, grad_gain_two = norm_two_back(d_normed_two)
    d_resid = cotangent.astype(jnp.float32) + resid_part
    d_branch = d_resid.astype(jnp.bfloat16)
    grad_out = jnp.einsum("td,te->de", attn_low, d_branch, preferred_element_type=jnp.float32)
    d_attn = jnp.einsum(
        "te,de->td", d_branch, out_weight, preferred_element_type=jnp.float32
    ).astype(jnp.bfloat16)
    d_attn_heads = d_attn.reshape(tok_rows, HEADS, HD)
    delta_heads = jnp.sum(d_attn_heads.astype(jnp.float32).transpose(1, 0, 2) * attn_heads, axis=-1)
    all_log_total, all_delta = (
        lax.all_gather(log_total.T.astype(jnp.bfloat16), "ctx", axis=0, tiled=True).astype(
            jnp.float32
        ),
        lax.all_gather(delta_heads.T.astype(jnp.bfloat16), "ctx", axis=0, tiled=True).astype(
            jnp.float32
        ),
    )
    d_query_sum = jnp.zeros((tok_rows, HEADS, HD), jnp.float32)
    key_piece = lax.all_gather(keys_flat, "ctx", axis=0, tiled=True)
    value_piece = lax.all_gather(values, "ctx", axis=0, tiled=True)
    piece_rows = key_piece.shape[0]
    query_size_now = block_size(tok_rows)
    block_count = piece_rows // query_size_now
    key_blocks = key_piece.reshape(block_count, query_size_now, HEADS, HD)
    value_blocks = value_piece.reshape(block_count, query_size_now, HEADS, HD)
    block_starts = jnp.arange(block_count, dtype=jnp.int32) * query_size_now

    def query_one_block(partial_value, inputs):
        key_block, value_block, block_start = inputs
        key_index = block_start + jnp.arange(query_size_now, dtype=jnp.int32)
        key_start = lax.dynamic_slice_in_dim(all_starts, block_start, query_size_now)
        scores = masked_scores(
            queries, key_block, own_index, segment_start, key_index, key_start, score_scale
        )
        probability = jnp.exp(scores - log_total[..., None])
        d_prob = jnp.einsum(
            "qhd,khd->hqk", d_attn_heads, value_block, preferred_element_type=jnp.float32
        )
        d_score = (probability * (d_prob - delta_heads[..., None])).astype(jnp.bfloat16)
        partial_value = (
            partial_value
            + jnp.einsum("hqk,khd->qhd", d_score, key_block, preferred_element_type=jnp.float32)
            * score_scale
        )
        return (partial_value, None)

    d_query_sum, _ = lax.scan(
        query_one_block, d_query_sum, (key_blocks, value_blocks, block_starts)
    )
    queries_flat = queries.reshape(tok_rows, model_width)
    key_init = (
        jnp.zeros((tok_rows, HEADS, HD), jnp.float32),
        jnp.zeros((tok_rows, HEADS, HD), jnp.float32),
    )
    sums_now = key_init
    query_piece = lax.all_gather(queries_flat, "ctx", axis=0, tiled=True)
    grad_piece = lax.all_gather(d_attn, "ctx", axis=0, tiled=True)
    piece_rows = query_piece.shape[0]
    key_size_now = block_size(tok_rows)
    block_count = piece_rows // key_size_now
    query_blocks = query_piece.reshape(block_count, key_size_now, HEADS, HD)
    grad_blocks = grad_piece.reshape(block_count, key_size_now, HEADS, HD)
    block_starts = jnp.arange(block_count, dtype=jnp.int32) * key_size_now

    def key_one_block(partial_value, inputs):
        query_block, grad_block, block_start = inputs
        query_index = block_start + jnp.arange(key_size_now, dtype=jnp.int32)
        query_start = lax.dynamic_slice_in_dim(all_starts, block_start, key_size_now)
        block_total = lax.dynamic_slice_in_dim(all_log_total, block_start, key_size_now).T
        block_delta = lax.dynamic_slice_in_dim(all_delta, block_start, key_size_now).T
        d_key_sum, d_value_sum = partial_value
        scores = masked_scores(
            query_block, keys_rot, query_index, query_start, own_index, segment_start, score_scale
        )
        probability = jnp.exp(scores - block_total[..., None])
        d_prob = jnp.einsum(
            "qhd,khd->hqk", grad_block, values_heads, preferred_element_type=jnp.float32
        )
        d_score = (probability * (d_prob - block_delta[..., None])).astype(jnp.bfloat16)
        d_value_sum = d_value_sum + jnp.einsum(
            "hqk,qhd->khd",
            probability.astype(jnp.bfloat16),
            grad_block,
            preferred_element_type=jnp.float32,
        )
        d_key_sum = (
            d_key_sum
            + jnp.einsum("hqk,qhd->khd", d_score, query_block, preferred_element_type=jnp.float32)
            * score_scale
        )
        partial_value = (d_key_sum, d_value_sum)
        return (partial_value, None)

    sums_now, _ = lax.scan(key_one_block, sums_now, (query_blocks, grad_blocks, block_starts))
    d_key_rot, d_values = sums_now

    def rotate_here(features):
        return rotate(features, angles)

    _, rotate_back = jax.vjp(rotate_here, query_raw)
    d_query = (
        rotate_back(d_query_sum.astype(jnp.bfloat16).astype(jnp.float32))[0]
        .astype(jnp.bfloat16)
        .reshape(tok_rows, model_width)
    )
    d_key = (
        rotate_back(d_key_rot.astype(jnp.bfloat16).astype(jnp.float32))[0]
        .astype(jnp.bfloat16)
        .reshape(tok_rows, model_width)
    )
    d_values_low = d_values.astype(jnp.bfloat16).reshape(tok_rows, model_width)
    grad_first = (0.5 * d_values_low.astype(jnp.float32)).astype(jnp.bfloat16)
    grad_query = jnp.einsum("td,te->de", normed, d_query, preferred_element_type=jnp.float32)
    grad_key = jnp.einsum("td,te->de", normed, d_key, preferred_element_type=jnp.float32)
    grad_value = jnp.einsum("td,te->de", normed, grad_first, preferred_element_type=jnp.float32)
    d_normed = jnp.einsum("te,de->td", d_query, query_weight, preferred_element_type=jnp.float32)
    d_normed = d_normed + jnp.einsum(
        "te,de->td", d_key, key_weight, preferred_element_type=jnp.float32
    )
    d_normed = d_normed + jnp.einsum(
        "te,de->td", grad_first, value_weight, preferred_element_type=jnp.float32
    )
    _, norm_one_back = jax.vjp(rms_scale, token_float, gain_one.astype(jnp.float32))
    token_part, grad_gain_one = norm_one_back(d_normed)
    grad_tokens = (d_resid + token_part).astype(jnp.bfloat16)
    reduced = (
        lax.psum_scatter(grad_gain_one, ("seq", "ctx"), scatter_dimension=0, tiled=True),
        lax.psum_scatter(grad_query, ("seq", "ctx"), scatter_dimension=0, tiled=True),
        lax.psum_scatter(grad_key, ("seq", "ctx"), scatter_dimension=0, tiled=True),
        lax.psum_scatter(grad_value, ("seq", "ctx"), scatter_dimension=0, tiled=True),
        lax.psum_scatter(grad_out, ("seq", "ctx"), scatter_dimension=0, tiled=True),
        lax.psum_scatter(grad_gain_two, ("seq", "ctx"), scatter_dimension=0, tiled=True),
        lax.psum_scatter(grad_gate, ("seq", "ctx"), scatter_dimension=0, tiled=True),
        lax.psum_scatter(grad_up, ("seq", "ctx"), scatter_dimension=0, tiled=True),
        lax.psum_scatter(grad_down, ("seq", "ctx"), scatter_dimension=0, tiled=True),
    )
    return (
        block_out,
        grad_tokens,
        grad_first,
        reduced[0],
        reduced[1],
        reduced[2],
        reduced[3],
        reduced[4],
        reduced[5],
        reduced[6],
        reduced[7],
        reduced[8],
    )


BF = jnp.bfloat16
F32 = jnp.float32
MESH_ID = pl.DeviceIdType.MESH
QC = 768
GC = 1536
BLK = 256
ALL_Z = range(4)


def dot_nn(a, b):
    return lax.dot_general(a, b, (((1,), (0,)), ((), ())), preferred_element_type=F32)


def dot_nt(a, b):
    return lax.dot_general(a, b, (((1,), (1,)), ((), ())), preferred_element_type=F32)


def dot_tn(a, b):
    return lax.dot_general(a, b, (((0,), (0,)), ((), ())), preferred_element_type=F32)


N_SEND = 228
N_RECV = 202
VMEM_LIMIT = 64 * 2**20 - 2**18
DUE = (
    (7.4, 3.9, 7.3, 7.4), (11.9, 11.7, 11.7, 12.0), (8.8, 14.2, 13.0, 9.7),
    (20.8, 27.2, 17.5, 23.4), (34.9, 0.1, -9.8, 34.1), (25.4, 28.1, 21.9, 26.0),
    (40.3, 38.1, 32.4, 36.6), (48.5, 42.6, 35.7, 44.5), (45.2, 47.8, 34.6, 46.9),
    (14.5, 15.6, 16.3, 14.5), (10.4, 16.5, 9.7, 12.4), (23.1, 29.8, 22.4, 27.0),
    (32.0, 0.1, -6.8, 38.1), (57.0, 65.2, 60.2, 62.2), (61.7, 67.2, 61.5, 65.0),
    (66.1, 71.3, 62.2, 66.7), (69.3, 75.4, 63.6, 71.5), (68.4, 79.6, 68.2, 76.0),
    (77.0, 90.8, 72.4, 80.3), (81.5, -1.6, -7.1, 83.7), (87.1, -2.2, -5.7, 89.0),
    (93.9, 3.5, -2.1, 96.7), (23.0, 20.8, 15.4, 22.8), (30.9, 25.2, 29.5, 25.4),
    (87.5, 75.1, 84.1, 79.5), (86.6, 75.1, 84.1, 78.2), (138.0, 131.8, 133.0, 132.1),
    (140.9, 134.8, 137.4, 135.7), (57.7, 48.2, 42.4, 45.4), (64.8, 54.5, 47.9, 54.5),
    (64.0, 57.5, 56.9, 54.2), (71.7, 62.2, 62.8, 63.8), (126.9, 122.2, 121.7, 123.1),
    (127.5, 122.5, 122.0, 121.3), (127.8, 123.5, 124.4, 124.4), (129.3, 126.7, 128.7, 128.1),
    (121.0, -0.6, 0.4, -1.4), (-0.6, 131.6, 0.4, 0.8), (-3.0, 0.0, 135.0, 15.9),
    (-2.4, 0.0, -11.0, 138.6), (131.4, -4.5, -11.2, -0.2), (-3.2, 129.0, -11.8, -0.8),
    (-3.9, -1.5, 93.2, -1.5), (-31.7, -8.3, -8.3, 109.9), (111.3, -0.0, 2.6, 2.6),
    (4.1, 135.9, 12.0, 30.3), (-5.9, -1.2, 139.8, -1.2), (-22.8, -11.0, -35.4, 113.8),
    (121.2, 0.2, 0.2, 0.2), (-8.6, 141.6, 0.0, 0.0), (0.3, 0.6, 135.7, 0.2),
    (2.4, 0.3, 0.3, 129.0), (133.3, 130.6, 133.6, 132.5), (137.0, 134.1, 138.5, 138.2),
    (141.3, 140.0, 143.6, 141.2), (145.5, 143.0, 145.6, 144.5), (136.9, 0.0, 0.0, 22.1),
    (-3.0, 143.9, -0.2, 21.9), (-1.3, 0.0, 150.1, -1.8), (-1.3, 3.4, 0.0, 165.7),
    (149.7, 0.0, 1.1, 9.2), (0.0, 145.9, 0.0, 0.0), (0.0, 0.0, 142.5, -1.9),
    (0.0, -11.1, 0.0, 131.4), (135.9, -33.7, -6.1, -10.3), (0.0, 149.1, -4.7, -1.9),
    (42.9, 37.3, 197.8, 42.1), (0.0, -4.8, 0.0, 141.5), (145.5, -0.5, -11.4, -0.5),
    (0.5, 165.0, 0.3, 0.3), (-6.5, 2.9, 158.3, 0.3), (-32.2, -25.4, -25.5, 120.3),
    (151.0, 154.7, 148.8, 148.6), (161.6, 155.2, 157.7, 158.7), (155.8, 159.0, 158.8, 161.7),
    (162.6, 160.3, 165.3, 163.3), (147.6, -1.9, -1.9, -1.3), (-3.0, 164.7, -0.3, 1.1),
    (-4.9, -0.3, 171.0, 1.1), (-0.2, -0.2, 1.7, 178.4), (179.0, -0.7, 1.2, -0.7),
    (0.8, 176.5, 11.4, 0.8), (-10.9, -7.4, 160.6, -7.4), (0.8, 0.8, 1.8, 154.9),
    (156.0, 1.9, -1.4, -3.6), (-0.5, 174.8, -18.4, 0.8), (-6.1, -4.8, 178.6, -4.8),
    (-7.4, 0.8, 0.8, 164.4), (157.7, 1.3, 0.8, 3.4), (-8.2, 184.6, 0.0, 0.0),
    (0.6, -2.7, 176.8, -4.6), (-1.9, -0.6, -0.6, 164.5), (163.7, 164.2, 164.3, 164.6),
    (163.0, 164.9, 163.4, 164.6), (167.2, 166.7, 165.1, 169.2), (177.5, 172.0, 174.5, 177.5),
    (185.7, 2.2, 2.2, 2.2), (6.1, 189.7, -0.6, -0.6), (20.4, 13.4, 199.5, 13.4),
    (4.9, -0.4, -1.0, 178.1), (174.1, 172.0, 169.4, 171.2), (177.1, 172.3, 174.6, 173.2),
    (174.7, 172.2, 170.5, 169.9), (178.3, 167.3, 175.5, 177.5), (171.3, 1.2, 1.2, 1.7),
    (18.2, 183.3, -5.8, -5.8), (29.0, -5.9, 188.0, -5.8), (30.4, -5.5, -5.4, 189.7),
    (235.3, 2.5, 2.6, -2.8), (2.4, 194.0, -0.9, -3.7), (2.5, 0.0, 190.8, -22.0),
    (2.5, 0.0, -3.8, 159.8), (161.8, -17.6, -15.5, -29.3), (-4.6, 189.2, -0.1, -3.8),
    (7.3, 2.7, 204.9, 1.1), (4.4, -1.7, 3.1, 172.3), (184.9, 0.0, 5.9, -1.6),
    (6.0, 203.8, 7.3, -2.4), (0.1, -16.7, 200.8, -3.8), (2.8, 2.8, 8.7, 176.8),
    (189.5, 180.6, 181.3, 180.0), (178.6, 171.3, 170.1, 170.8), (188.9, 182.8, 180.4, 182.1),
    (190.8, 186.4, 180.5, 182.3), (189.4, 2.3, 22.4, -3.5), (0.2, 197.1, -2.8, -4.1),
    (-1.6, -1.6, 203.2, -3.8), (5.9, 5.9, 5.9, 211.5), (213.1, 10.2, 24.0, 13.9),
    (25.6, 227.2, 23.1, 11.7), (-1.7, -1.7, 197.8, -13.1), (5.4, 2.7, -5.1, 171.0),
    (189.2, -0.0, 8.4, -11.1), (-0.2, 202.5, -0.2, -11.1), (-2.2, -0.5, 206.1, -11.6),
    (-12.8, 19.4, -11.3, 162.0), (195.4, 4.9, -13.2, -22.2), (-2.0, 227.3, -7.8, -1.1),
    (-2.0, 12.2, 207.1, -1.1), (-11.1, -15.8, -11.4, 176.2),
)
LOOK = (
    (4.2, -4.7, -5.6, 7.3), (11.6, 11.7, 11.6, 11.5), (-5.0, 6.6, 6.5, 6.4),
    (14.0, 14.6, 7.4, 15.6), (21.6, 13.4, 13.3, 18.3), (15.5, 15.9, 16.0, 15.4),
    (18.6, 6.4, 12.4, 11.9), (19.3, 12.2, 17.8, 10.9), (37.7, 33.4, 33.0, 36.9),
    (37.4, 33.7, 34.5, 37.1), (48.5, 42.8, 49.7, 41.6), (52.4, 46.4, 53.8, 45.2),
    (55.9, 50.8, 57.5, 49.2), (60.5, 54.8, 61.7, 56.6), (58.7, 58.6, 64.8, 60.9),
    (74.6, 69.7, 77.0, 67.9), (59.0, 54.2, 59.3, 57.3), (68.8, 69.0, 70.2, 62.5),
    (96.9, 103.8, 95.6, 95.4), (106.4, 106.2, 107.0, 97.8), (114.3, 124.2, 124.9, 117.0),
    (123.4, 120.6, 121.3, 118.2), (130.0, 119.3, 124.9, 122.9), (114.7, 128.8, 129.4, 127.5),
    (131.9, 132.6, 130.3, 127.5), (140.0, 132.5, 131.8, 130.8), (148.4, 145.5, 137.3, 144.6),
    (132.9, 134.4, 124.2, 127.5), (148.3, 142.7, 144.3, 135.0), (143.8, 142.3, 143.9, 140.3),
    (146.3, 145.1, 142.6, 136.5), (160.5, 149.4, 151.8, 148.6), (163.8, 153.6, 152.8, 151.7),
    (168.9, 157.2, 159.8, 163.9), (176.2, 165.0, 167.3, 162.9), (177.5, 166.3, 169.4, 172.6),
    (185.2, 173.2, 176.5, 171.9), (184.9, 177.6, 176.9, 176.0), (198.3, 180.4, 187.4, 175.9),
    (194.9, 180.5, 186.0, 179.6), (202.5, 190.4, 191.3, 186.8), (204.0, 186.4, 196.2, 191.8),
    (204.9, 180.0, 197.2, 192.8), (194.0, 195.5, 206.1, 208.7),
)


SCRATCH = dict(
    TOK=((256, 1024), BF),
    STT=((4, 8, 128), F32),
    ST=((1024, 128), F32),
    COS=((1024, 128), F32),
    SIN=((1024, 128), F32),
    FV=((1024, 256), BF),
    COT=((1024, 1024), BF),
    N1=((1024, 1024), BF),
    N2=((1024, 1024), BF),
    DB=((1024, 1024), BF),
    GAZ=((4, 16, 128), F32),
    GAS=((2, 16, 128), F32),
    GAJ=((4, 16, 128), F32),
    RAW=((3, 32, 1024), BF),
    RAWG=((2, 32, 2816), BF),
    RAWD=((88, 1024), BF),
    SYD=((4, 96, 1024), BF),
    GV=((8, 1024), F32),
    WA=((2, 4, 4, 32, QC), BF),
    WO=((2, 4, 32, 1024), BF),
    WG=((2, 4, 4, 32, GC), BF),
    WD=((2, 4, 96, 1024), BF),
    QS=((1024, 256), BF),
    KR=((1024, 256), BF),
    V=((1024, 256), BF),
    O=((1024, 256), BF),
    DA=((1024, 256), BF),
    P0=((4, 256, 256), BF),
    P1=((4, 256, 512), BF),
    P2=((4, 256, 768), BF),
    P3=((4, 256, 1024), BF),
    DQ=((1024, 256), BF),
    DK=((1024, 256), F32),
    DV=((1024, 256), F32),
    DQKV=((1024, QC), BF),
    H=((1024, 768), BF),
    DGU=((1024, GC), BF),
    RES=((256, 1024), F32),
    DRES=((256, 1024), F32),
    SSA=((2, 256, 1024), BF),
    SRA=((2, 256, 1024), BF),
    XSA=((256, 1024), BF),
    XRA=((256, 1024), BF),
    SSB=((2, 256, 1024), BF),
    SRB=((2, 256, 1024), BF),
    XSB=((256, 1024), BF),
    XRB=((256, 1024), BF),
    FF=((256, 1024), F32),
    OUT=((256, 1024), BF),
    GQ=((4, 4, 32, QC), F32),
    GO=((4, 32, 1024), F32),
    GG=((4, 4, 32, GC), F32),
    GD=((4, 96, 1024), F32),
    RYQ=((4, 4, 32, QC), BF),
    RYO=((4, 32, 1024), BF),
    RYG=((4, 4, 32, GC), BF),
    RYD=((4, 96, 1024), BF),
    ZQ=((5, 4, 32, QC), BF),
    ZO=((5, 32, 1024), BF),
    ZG=((5, 4, 32, GC), BF),
    ZD=((5, 96, 1024), BF),
    GGS=((16, 128), F32),
    GGR=((3, 16, 128), F32),
    GGY=((16, 128), F32),
    GGT=((16, 128), F32),
    GGZ=((4, 16, 128), F32),
)


def slot_window(c):
    return 352 * c // 128 * 128, (352 * c + 352 + 127) // 128 * 128


def slot_map(c):
    lo, hi = slot_window(c)
    unit = lax.broadcasted_iota(jnp.int32, (hi - lo, 384), 0) + (lo - 352 * c)
    slot = lax.broadcasted_iota(jnp.int32, (hi - lo, 384), 1)
    block = (slot >= 96).astype(jnp.int32) + (slot >= 192).astype(jnp.int32)
    block = block + (slot >= 288).astype(jnp.int32)
    within = slot - 96 * block
    return ((unit == 88 * block + within) & (within < 88)).astype(F32).astype(BF)


def finish_kernel(*refs):
    (block, gtok, gfv, gq, gg, go, gd, gain) = refs[:8]
    (o_block, o_gtok, o_gfv, o_ga, o_q, o_k, o_v, o_o, o_gf, o_g, o_u, o_d) = refs[8:]
    o_block[...] = block[...]
    o_gtok[...] = gtok[...]
    o_gfv[...] = gfv[...]
    o_o[...] = go[...]
    o_d[...] = gd[0:88, :]
    for t, out in enumerate((o_q, o_k, o_v)):
        for h in range(2):
            for c in range(4):
                part = gq[c, :, 384 * h + 128 * t : 384 * h + 128 * t + 128]
                out[:, 128 * (c + 4 * h) : 128 * (c + 4 * h) + 128] = part.astype(F32)
    o_g[...] = jnp.zeros((32, 2816), F32)
    o_u[...] = jnp.zeros((32, 2816), F32)
    for c in range(4):
        lo, hi = slot_window(c)
        place = slot_map(c)
        parts = [gg[c, :, 384 * n : 384 * n + 384] for n in range(4)]
        back = dot_nt(jnp.concatenate(parts, axis=0), place)
        for t, out in enumerate((o_g, o_u)):
            for h in range(2):
                n = 2 * t + h
                out[:, 1408 * h + lo : 1408 * h + hi] += back[32 * n : 32 * n + 32, :]
    d = lax.axis_index("seq") * 4 + lax.axis_index("ctx")
    line = lax.broadcasted_iota(jnp.int32, (8, 128), 0) == d // 4
    for r, out in ((0, o_ga), (8, o_gf)):
        own = jnp.sum(jnp.where(line, gain[r : r + 8, :], 0.0), axis=0, keepdims=True)
        own = pltpu.roll(jnp.broadcast_to(own, (8, 128)), (128 - 32 * (d % 4)) % 128, 1)
        out[...] = own[0:1, 0:32]


class Step(tuple):
    def __lt__(self, other):
        return self[:2] < other[:2]


def layer_kernel(*refs):
    (tok, fv, cot, small, wq, wk, wv, wg, wu, wo, wdn) = refs[:11]
    (o_block, o_gtok, o_gfv, o_gq, o_gg, o_go, o_gd, o_gain) = refs[11:19]
    R = types.SimpleNamespace(**dict(zip(SCRATCH, refs[19:])))
    ssem, rsem, lsem = refs[19 + len(SCRATCH) :]
    gt, stt = small.at[0:16], small.at[16:24]
    sa, sg, wd = R.DQKV, R.DGU, R.DB.at[768:864]

    def pack(c):
        return slice(32 * c, 32 * c + 32)

    raw = [R.RAW.at[0], R.RAW.at[1], R.RAW.at[2], R.RAWG.at[0], R.RAWG.at[1], R.RAWD]
    fetch = [
        pltpu.make_async_copy(src, dst, lsem.at[14 + n])
        for n, (src, dst) in enumerate(zip((wq, wk, wv, wg, wu, wdn), raw))
    ]
    for f in fetch:
        f.start()
    wq, wk, wv, wg, wu, wdn = raw

    def prep():
        for f in fetch:
            f.wait()
        for t, w in enumerate((wq, wk, wv)):
            for h in range(2):
                for c in range(4):
                    lanes = pl.ds(128 * (c + 4 * h), 128)
                    sa[pack(c), 384 * h + 128 * t : 384 * h + 128 * t + 128] = w[:, lanes]
        for c in range(4):
            lo, hi = slot_window(c)
            place = slot_map(c)
            parts = [
                w[:, 1408 * h + lo : 1408 * h + hi] for w in (wg, wu) for h in range(2)
            ]
            part = dot_nn(jnp.concatenate(parts, axis=0), place).astype(BF)
            for n in range(4):
                sg[pack(c), 384 * n : 384 * n + 384] = part[32 * n : 32 * n + 32, :]
        wd[0:88, :] = wdn[...]
        wd[88:96, :] = jnp.zeros((8, 1024), BF)

    s = lax.axis_index("seq")
    z = lax.axis_index("ctx")
    y = s // 4
    j = s % 4
    x = j // 2
    k = j % 2
    ny = 1 - y
    sib = (4 * y + 2 * x + (1 - k), z)
    xp = (4 * y + 2 * (1 - x) + k, z)
    yp = (4 * ny + j, z)
    up_z, dn_z = (s, z + 1), (s, z - 1)
    column = (z + k) % 2
    crossing = x != column
    direct = x == column
    jp = 2 * (1 - x) + k

    def host(jj):
        return (4 * y + 2 * column + z // 2, jj)

    home = (4 * y + z, 2 * k + (x + z) % 2)
    at_home = (home[0] == s) & (home[1] == z)
    away = host(j)
    away_self = (away[0] == s) & (away[1] == z)
    b_me = 2 * k + (x + z) % 2
    b_x = 2 * k + (1 - x + z) % 2
    b_s = 2 * (1 - k) + (x + z) % 2
    b_xs = 2 * (1 - k) + (1 - x + z) % 2

    counters = [0, 0, 0]
    pend = []
    tasks = []
    made = [0, 0]

    def ids(n):
        made[0] += n
        return made[0] - n

    on_z = {q: z == q for q in ALL_Z}
    turn_of = [None]

    def guard():
        return None if turn_of[0] is None else on_z[turn_of[0]]

    def place():
        return z if turn_of[0] is None else turn_of[0]

    def later(i, fn, of=None):
        for q in ALL_Z if turn_of[0] is None else turn_of:
            tasks.append(Step((DUE[i][q], i, fn, of, q)))

    def due(q):
        return min([e for e in tasks if e[4] == q], default=None)

    def take(step):
        tasks.remove(step)
        turn_of[0] = step[4]
        step[2]()
        turn_of[0] = None

    def look():
        for q in ALL_Z:
            step = due(q)
            while step is not None and step[0] <= LOOK[made[1]][q]:
                take(step)
                step = due(q)
        made[1] += 1

    def flush(of=None):
        for q in ALL_Z:
            while any((of is None or e[3] is of) and e[4] == q for e in tasks):
                take(due(q))

    def snd(n=1):
        counters[0] += n
        assert counters[0] <= N_SEND
        return counters[0] - n

    def rcv(n=1):
        counters[2] += n
        assert counters[2] <= N_RECV
        return counters[2] - n

    def rows(b):
        return pl.ds(pl.multiple_of(b * BLK, BLK), BLK)

    def half_rows(b, h):
        return pl.ds(pl.multiple_of(b * BLK + 128 * h, 128), 128)

    def came(dst, r):
        return rc(dst, dst, 0, sib, r).wait_recv

    def rc(src, dst, i, dev, r):
        return pltpu.make_async_remote_copy(
            src_ref=src,
            dst_ref=dst,
            send_sem=ssem.at[i],
            recv_sem=rsem.at[r],
            device_id=dev,
            device_id_type=MESH_ID,
        )

    def both(p, q):
        if p is None or q is None or isinstance(p, bool) or isinstance(q, bool):
            if p is False or q is False:
                return False
            return p if q is None or q is True else q
        return p & q

    def when(cond, fn):
        cond = both(guard(), cond)
        if cond is None or cond is True:
            fn()
        elif cond is not False:
            pl.when(cond)(fn)

    def start(desc, cond=None):
        when(cond, desc.start)
        cond = both(guard(), cond)
        if cond is not False:
            pend.append((cond, desc))

    def local(src, dst):
        d = pltpu.make_async_copy(src, dst, lsem.at[counters[1]])
        counters[1] += 1
        d.start()
        return d

    def route(src, dst, i, self_cond, dev, r, cond=None):
        when(both(cond, self_cond), pltpu.make_async_copy(src, dst, rsem.at[r]).start)
        start(rc(src, dst, i, dev, r), both(cond, jnp.logical_not(self_cond)))

    def arrive(like_src, dst, r, self_cond):
        when(self_cond, pltpu.make_async_copy(like_src, dst, rsem.at[r]).wait)
        when(jnp.logical_not(self_cond), came(dst, r))

    def group_dev(c, jj):
        return (4 * y + c, jj)

    barrier = pltpu.get_barrier_semaphore()
    me = j * 4 + z
    for i in range(1, 16):
        t = (me + i) % 16
        pl.semaphore_signal(
            barrier, inc=1, device_id=(4 * y + t // 4, t % 4), device_id_type=MESH_ID
        )
    pl.semaphore_signal(barrier, inc=1, device_id=yp, device_id_type=MESH_ID)
    prep()
    pl.semaphore_wait(barrier, 16)

    i_gz, i_gy, i_gj = snd(4), snd(), snd(4)
    r_gz, r_gy, r_gj = rcv(4), rcv(), rcv(4)
    loc_gt = local(gt, R.GAZ.at[z])
    for c in range(4):
        start(rc(gt, R.GAZ.at[z], i_gz + c, (s, c), r_gz + z), z != c)

    class Move:
        def __init__(self, src, stage, pieces, arrivals):
            self.src, self.stage, self.pieces, self.arrivals = src, stage, pieces, arrivals
            n = len(pieces(j))
            self.ix, self.io, self.ir = snd(2), snd(n), snd(n)
            self.rx = rcv(2)

        def cross(self):
            for h in range(2):
                cut = pl.ds(128 * h, 128)
                start(rc(self.src.at[cut], self.stage.at[cut], self.ix + h, xp, self.rx + h), crossing)

        def own(self):
            for n, (cut, dst, self_cond, dev, r) in enumerate(self.pieces(j)):
                route(self.src.at[cut], dst, self.io + n, self_cond, dev, r, direct)

        def relay(self, h):
            pieces = self.pieces(jp)
            part = self.stage.at[pl.ds(128 * h, 128)]
            when(direct, came(part, self.rx + h))
            for n, (cut, dst, self_cond, dev, r) in enumerate(pieces):
                if (n == h) if len(pieces) == 2 else h == 1:
                    route(self.stage.at[cut], dst, self.ir + n, self_cond, dev, r, direct)

        def wait(self, part=None):
            for n, (like, dst, r, self_cond) in enumerate(self.arrivals()):
                if part is None or n == part:
                    arrive(like, dst, r, self_cond)

    last_hop_self = (z % 2 == k) & (b_me == z)

    def block_pieces(dst_at, base):
        def pieces(jj):
            dev = host(jj)
            self_cond = (dev[0] == s) & (dev[1] == z)
            return [
                (pl.ds(128 * h, 128), dst_at(z, h), self_cond, dev, base + h) for h in range(2)
            ]

        return pieces

    def block_arrivals(src, dst_at, base):
        return lambda: [
            (src.at[pl.ds(128 * h, 128)], dst_at(b_me, h), base + h, last_hop_self)
            for h in range(2)
        ]

    def tok_at(b, h):
        return R.TOK.at[pl.ds(128 * h, 128)]

    def cot_at(b, h):
        return R.COT.at[half_rows(b, h)]

    def fv_at(b, h):
        return R.FV.at[rows(b), pl.ds(128 * h, 128)]

    i_tok, i_cot, i_fv, i_st = rcv(2), rcv(2), rcv(8), rcv(4)
    s_st = snd(4)

    def fv_pieces(jj):
        out = []
        for c in range(4):
            dev = group_dev(c, jj)
            self_cond = (dev[0] == s) & (dev[1] == z)
            for h in range(2):
                cut = (slice(None), pl.ds(128 * (c + 4 * h), 128))
                out.append((cut, fv_at(z, h), self_cond, dev, i_fv + 2 * z + h))
        return out

    def fv_arrivals():
        out = []
        for b in range(4):
            self_cond = (z % 2 == k) & (z == b) & (x == (b + k) % 2)
            for h in range(2):
                out.append((fv.at[:, pl.ds(128 * h, 128)], fv_at(b, h), i_fv + 2 * b + h, self_cond))
        return out

    m_tok = Move(tok, R.DB.at[0:256], block_pieces(tok_at, i_tok), block_arrivals(tok, tok_at, i_tok))
    m_cot = Move(cot, R.DB.at[512:768], block_pieces(cot_at, i_cot), block_arrivals(cot, cot_at, i_cot))
    m_fv = Move(fv, R.DB.at[256:512], fv_pieces, fv_arrivals)

    m_tok.own()
    i_sa, i_sg, r_sa, r_sg = snd(4), snd(4), rcv(4), rcv(4)
    own_pack = pl.ds(pl.multiple_of(32 * j, 32), 32)
    loc_sa = local(sa.at[own_pack], R.WA.at[y, j, z])
    loc_wo = local(wo, R.WO.at[y, z])
    for c in range(4):
        start(rc(sa.at[pack(c)], R.WA.at[y, j, z], i_sa + c, group_dev(c, z), r_sa + j), j != c)
    m_tok.cross()
    loc_wd = local(wd, R.WD.at[y, z])
    loc_sg = local(sg.at[own_pack], R.WG.at[y, j, z])

    def wait_group(base, dst_of):
        for c in range(4):
            when(j != c, came(dst_of(c), base + c))

    class Gather:
        def __init__(self, piece):
            self.piece = piece
            self.iz, self.iy, self.rz, self.ry = snd(8), snd(4), rcv(4), rcv(4)

        def sources(self, step):
            at = place()
            below, above = at - step, at + step
            out = []
            for src, sem, target, here, on in (
                (below, self.iz, up_z, below >= 0, at < 3),
                (above, self.iz + 4, dn_z, above <= 3, at > 0),
            ):
                if here is not False:
                    out.append((src, sem, target, here, on))
            return out

        def send_z(self, step, cond=None):
            for src, sem, target, here, on in self.sources(step):
                p = self.piece(y, src)
                start(rc(p, p, sem + src, target, self.rz + src), both(cond, both(here, on)))

        def send_y(self, step):
            for src, _, _, here, _ in self.sources(step)[: 1 if step == 0 else 2]:
                p = self.piece(y, src)
                start(rc(p, p, self.iy + src, yp, self.ry + src), here)

        def recv(self, step):
            for src, _, _, here, _ in self.sources(step):
                when(here, came(self.piece(y, src), self.rz + src))

        def pass_on(self, step):
            self.recv(step)
            if step < 3:
                self.send_z(step)
            self.send_y(step)

        def finish(self):
            for zz in range(4):
                came(self.piece(ny, zz), self.ry + zz)()

    g_a = Gather(lambda yy, zz: R.WA.at[yy, :, zz])
    g_o = Gather(lambda yy, zz: R.WO.at[yy, zz])
    g_d = Gather(lambda yy, zz: R.WD.at[yy, zz])
    g_g0 = Gather(lambda yy, zz: R.WG.at[yy, 0:2, zz])
    g_g1 = Gather(lambda yy, zz: R.WG.at[yy, 2:4, zz])

    loc_gt.wait()
    for c in range(4):
        when(z != c, came(R.GAZ.at[c], r_gz + c))
    R.GAS[0] = R.GAZ[0] + R.GAZ[1] + R.GAZ[2] + R.GAZ[3]
    start(rc(R.GAS.at[0], R.GAS.at[1], i_gy, yp, r_gy))

    wait_group(r_sa, lambda c: R.WA.at[y, c, z])
    loc_sa.wait()
    loc_wo.wait()
    g_a.send_z(0)
    g_a.send_y(0)
    g_o.send_z(0)
    g_o.send_y(0)
    t_tok, t_a, t_move, t_o, t_ffn = ids(2), ids(3), ids(5), ids(3), ids(9)
    t_n1, t_n2, t_db, t_cot = ids(2), ids(2), ids(2), ids(4)
    later(t_tok, lambda: m_tok.relay(0), m_tok)
    later(t_tok + 1, lambda: m_tok.relay(1), m_tok)
    def pass_a(step):
        g_a.pass_on(step)
        later(t_o + step - 1, lambda: g_o.pass_on(step), g_o)
        if step == 1:
            later(t_a + 1, lambda: pass_a(2), g_a)
        if step == 2:
            later(t_a + 2, lambda: pass_a(3), g_a)
            later(t_move, first_move, m_fv)

    later(t_a, lambda: pass_a(1), g_a)

    came(R.GAS.at[1], r_gy)()
    R.GAJ[j] = R.GAS[0] + R.GAS[1]
    for c in range(4):
        start(rc(R.GAJ.at[j], R.GAJ.at[j], i_gj + c, group_dev(c, z), r_gj + j), j != c)
    first_packed = len(pend)
    for c in range(4):
        start(rc(sg.at[pack(c)], R.WG.at[y, j, z], i_sg + c, group_dev(c, z), r_sg + j), j != c)
    packed = pend[first_packed:]
    del pend[first_packed:]
    look()
    for c in range(4):
        self_c = (j == z) & (j == c)
        route(stt, R.STT.at[z], s_st + c, self_c, group_dev(c, j), i_st + z)
    loc_wd.wait()
    g_d.send_y(0)

    def own_shard():
        wait_group(r_sg, lambda c: R.WG.at[y, c, z])
        when(None, loc_sg.wait)
        g_g0.send_y(0)

    def first_move():
        m_fv.own()
        later(t_move + 1, second_move, m_fv)

    def second_move():
        m_fv.relay(0)
        m_fv.relay(1)
        m_cot.own()
        later(t_move + 2, lambda: third_move(0))

    def third_move(h):
        m_cot.relay(h)
        if h == 0:
            later(t_move + 3, lambda: third_move(1))
        else:
            for g in (g_d, g_g0, g_g1):
                g.send_z(0, direct)
            g_g1.send_y(0)
            for n in range(3):
                later(t_ffn + n, lambda n=n: pass_ffn(1, n))

    def pass_ffn(step, n):
        (g_d, g_g0, g_g1)[n].pass_on(step)
        if step < 3:
            later(t_ffn + 3 * step + n, lambda: pass_ffn(step + 1, n))

    later(t_move + 4, own_shard, m_tok)
    look()
    wait_group(r_gj, lambda c: R.GAJ.at[c])
    gains = R.GAJ[0] + R.GAJ[1] + R.GAJ[2] + R.GAJ[3]
    for r in range(8):
        R.GV[0:1, 128 * r : 128 * r + 128] = gains[r : r + 1, :]
        R.GV[1:2, 128 * r : 128 * r + 128] = gains[8 + r : 9 + r, :]
    look()

    class Share:
        def __init__(self, buf):
            self.buf = buf
            self.i, self.r = snd(6), rcv(6)

        def piece(self, b, h):
            return self.buf.at[half_rows(b, h)]

        def send(self, h):
            p = self.piece(b_me, h)
            start(rc(p, p, self.i + h, xp, self.r + h))
            start(rc(p, p, self.i + 2 + h, sib, self.r + 2 + h))

        def forward(self, h):
            p = self.piece(b_x, h)
            when(None, came(p, self.r + h))
            start(rc(p, p, self.i + 4 + h, sib, self.r + 4 + h))

        def near(self):
            for h in range(2):
                came(self.piece(b_s, h), self.r + 2 + h)()

        def far(self):
            for h in range(2):
                came(self.piece(b_xs, h), self.r + 4 + h)()

        def finish(self):
            self.near()
            self.far()

    sh1, sh2, sh3, sh_cot = Share(R.N1), Share(R.N2), Share(R.DB), Share(R.COT)

    def send_cot(h):
        m_cot.wait(h)
        sh_cot.send(h)
        if h == 0:
            later(t_cot + 1, lambda: send_cot(1))

    for h in range(2):
        flush(m_tok)
        look()
        m_tok.wait(h)
        xs = R.TOK[128 * h : 128 * h + 128, :].astype(F32)
        rs1 = lax.rsqrt(jnp.mean(xs * xs, axis=-1, keepdims=True) + norm_eps)
        R.N1[half_rows(b_me, h), :] = (xs * rs1 * R.GV[0:1, :]).astype(BF)
        sh1.send(h)
        later(t_n1 + h, lambda h=h: sh1.forward(h), sh1)
        look()
    m_fv.cross()
    m_cot.cross()
    later(t_cot, lambda: send_cot(0))
    look()
    for c in range(4):
        arrive(stt, R.STT.at[c], i_st + c, (j == z) & (c == z))
    for b in range(4):
        for r in range(2):
            row = R.STT[b, r : r + 1, :]
            R.ST[256 * b + 128 * r : 256 * b + 128 * r + 128, :] = jnp.transpose(
                jnp.broadcast_to(row, (128, 128))
            )
    lane = lax.broadcasted_iota(jnp.int32, (1, 128), 1)
    low_half = (lane % 64) < 32
    freq = jnp.exp((lane % 32).astype(F32) * (-2.0 / HD * 9.210340371976184))

    def angle_body(b, c):
        pos = (lax.broadcasted_iota(jnp.int32, (BLK, 128), 0) + b * BLK).astype(F32)
        ang = (pos - R.ST[rows(b), :]) * freq
        R.COS[rows(b), :] = jnp.cos(ang)
        R.SIN[rows(b), :] = jnp.sin(ang) * jnp.where(low_half, -1.0, 1.0)
        return c

    lax.fori_loop(0, 4, angle_body, 0)

    def turn(v):
        return jnp.where(low_half, pltpu.roll(v, 96, 1), pltpu.roll(v, 32, 1))

    flush(g_a)
    look()
    g_a.finish()
    flush(sh1)
    look()
    sh1.finish()
    flush(m_fv)
    look()
    m_fv.wait()
    for g in (g_d, g_g0, g_g1):
        g.send_z(0, crossing)

    def qkv_body(b, c):
        raw = dot_nn(R.N1[rows(b), :], R.WA[...].reshape(1024, QC))
        cs, sn = R.COS[rows(b), :], R.SIN[rows(b), :]
        for t in range(2):
            sl = slice(128 * t, 128 * t + 128)
            q = raw[:, 384 * t : 384 * t + 128]
            R.QS[rows(b), sl] = ((q * cs + turn(q) * sn).astype(BF).astype(F32) * 0.125).astype(BF)
            kk = raw[:, 384 * t + 128 : 384 * t + 256]
            R.KR[rows(b), sl] = (kk * cs + turn(kk) * sn).astype(BF)
            v = raw[:, 384 * t + 256 : 384 * t + 384]
            R.V[rows(b), sl] = (0.5 * v + 0.5 * R.FV[rows(b), sl].astype(F32)).astype(BF)
        return c

    lax.fori_loop(0, 4, qkv_body, 0)
    look()

    PB = [R.P0, R.P1, R.P2, R.P3]

    def head_parts(h):
        pair = pl.ds(pl.multiple_of((h // 2) * 128, 128), 128)
        mine = ((lane // 64) == (h % 2)).astype(F32)
        return pair, mine.astype(BF), mine

    def attn_body(h, c):
        pair, low_mine, mine = head_parts(h)
        for i in range(4):
            n = BLK * (i + 1)
            q = R.QS[BLK * i : n, pair] * low_mine
            sc = dot_nt(q, R.KR[0:n, pair])
            col = lax.broadcasted_iota(jnp.int32, (BLK, n), 1)
            row = lax.broadcasted_iota(jnp.int32, (BLK, n), 0) + BLK * i
            first = R.ST[BLK * i : n, 0:1].astype(jnp.int32)
            sc = jnp.where((col >= first) & (col <= row), sc, masked_score)
            top = jnp.max(sc, axis=-1, keepdims=True)
            e = jnp.exp(sc - top)
            p = (e * (1.0 / jnp.sum(e, axis=-1, keepdims=True))).astype(BF)
            PB[i][h] = p
            o = dot_nn(p, R.V[0:n, pair]) * mine
            R.O[BLK * i : n, pair] += o.astype(BF)
        return c

    R.O[...] = jnp.zeros((1024, 256), BF)
    lax.fori_loop(0, 2, attn_body, 0)
    look()
    lax.fori_loop(2, 4, attn_body, 0)
    look()

    class GroupSum:
        def __init__(self, bufs):
            self.ss, self.sr, self.xs, self.xr = bufs
            self.i, self.r = snd(4), rcv(4)

        def run(self, fn):
            self.ss[0] = fn(b_xs).astype(BF)
            d0 = rc(self.ss.at[0], self.sr.at[0], self.i, sib, self.r)
            d0.start()
            self.ss[1] = fn(b_s).astype(BF)
            d1 = rc(self.ss.at[1], self.sr.at[1], self.i + 1, sib, self.r + 1)
            d1.start()
            look()
            d0.wait_recv()
            self.xs[...] = (fn(b_x) + self.sr[0].astype(F32)).astype(BF)
            d2 = []
            for h in range(2):
                cut = pl.ds(128 * h, 128)
                d2.append(rc(self.xs.at[cut], self.xr.at[cut], self.i + 2 + h, xp, self.r + 2 + h))
                d2[h].start()
            R.FF[...] = fn(b_me)
            look()
            d1.wait_recv()
            R.FF[...] += self.sr[1].astype(F32)
            self.descs = (d0, d1, *d2)

        def result(self, h):
            look()
            self.descs[2 + h].wait_recv()
            cut = slice(128 * h, 128 * h + 128)
            return R.FF[cut, :] + self.xr[cut, :].astype(F32)

        def end(self):
            for d in self.descs:
                d.wait_send()

    set_a = (R.SSA, R.SRA, R.XSA, R.XRA)
    set_b = (R.SSB, R.SRB, R.XSB, R.XRB)
    flush(g_o)
    look()
    g_o.finish()
    sum_attn = GroupSum(set_a)
    sum_attn.run(lambda b: dot_nn(R.O[rows(b), :], R.WO[...].reshape(256, 1024)))
    for h in range(2):
        cut = slice(128 * h, 128 * h + 128)
        res = R.TOK[cut, :].astype(F32) + sum_attn.result(h)
        R.RES[cut, :] = res
        rs2 = lax.rsqrt(jnp.mean(res * res, axis=-1, keepdims=True) + norm_eps)
        R.N2[half_rows(b_me, h), :] = (res * rs2 * R.GV[1:2, :]).astype(BF)
        sh2.send(h)
    sum_attn.end()
    flush()
    sh_cot.forward(0)
    sh_cot.forward(1)
    for g in (g_d, g_g0, g_g1):
        g.finish()

    def ffn_body(b, c):
        gu = dot_nn(R.N2[rows(b), :], R.WG[...].reshape(1024, GC))
        gate, up = gu[:, :768], gu[:, 768:]
        sig = 1.0 / (1.0 + jnp.exp(-gate))
        silu = gate * sig
        R.H[rows(b), :] = (silu * up).astype(BF)
        dh = dot_nt(R.COT[rows(b), :], R.WD[...].reshape(768, 1024))
        R.DGU[rows(b), 0:768] = (dh * up * (sig * (1.0 + gate * (1.0 - sig)))).astype(BF)
        R.DGU[rows(b), 768:1536] = (dh * silu).astype(BF)
        return c

    for cond, desc in packed:
        when(cond, desc.wait_send)
    ffn_body(b_me, 0)
    sh2.near()
    sh_cot.near()
    ffn_body(b_s, 0)
    sh2.forward(0)
    sh2.forward(1)
    ffn_body(b_x, 0)
    sh2.far()
    sh_cot.far()
    ffn_body(b_xs, 0)
    for cond, desc in pend:
        when(cond, desc.wait_send)
    pend.clear()

    class Reduce:
        def __init__(self, g, sy, ry, zr, cs):
            self.g, self.sy, self.ry, self.zr = g, sy, ry, zr
            self.cs = cs
            self.iy, self.iz, self.r, self.rz = snd(4), snd(4), rcv(4), rcv(5)

        def cut(self, ref, o):
            if self.cs is None:
                return ref.at[o]
            return ref.at[self.cs[0] : self.cs[1], o]

        def zslot(self, o):
            if self.cs is None:
                return self.zr.at[o]
            return self.zr.at[o, self.cs[0] : self.cs[1]]

        def chunks(self):
            return [None] if self.cs is None else range(*self.cs)

        def chunk(self, o, c):
            return self.zr.at[o] if c is None else self.zr.at[o, c]

        def term(self, o, c):
            at = o if c is None else (c, o)
            return self.g[at] + self.ry[at].astype(F32)

        def send_y(self):
            for o in (3, 0, 2, 1):
                start(rc(self.cut(self.sy, o), self.cut(self.ry, o), self.iy + o, yp, self.r + o))

        def recv_y(self, o):
            when(None, came(self.cut(self.ry, o), self.r + o))

        def hop(self, o, upward, zz):
            if upward:
                head, target, slot_out = zz == 0, up_z, o
            else:
                head, target = zz == 3, dn_z
                slot_out = 4 if zz - 1 == o else o
            d = rc(self.zslot(o), self.zslot(slot_out), self.iz + o, target, self.rz + slot_out)

            def go():
                if not head:
                    came(self.zslot(o), self.rz + o)()
                for c in self.chunks():
                    p = self.chunk(o, c)
                    val = self.term(o, c)
                    if not head:
                        val = val + p[...].astype(F32)
                    p[...] = val.astype(BF)
                d.start()

            pl.when(z == zz)(go)
            pend.append((z == zz, d))

        def last(self, zz, put):
            def go():
                if zz > 0:
                    came(self.zslot(zz), self.rz + zz)()
                if zz < 3:
                    came(self.zslot(4), self.rz + 4)()
                for c in self.chunks():
                    val = self.term(zz, c)
                    if zz > 0:
                        val = val + self.chunk(zz, c)[...].astype(F32)
                    if zz < 3:
                        val = val + self.chunk(4, c)[...].astype(F32)
                    put(c, val)

            pl.when(z == zz)(go)

        def schedule(self, put):
            t = ids(20)

            def take_y(n):
                o = (3, 0, 2, 1)[n]
                self.recv_y(o)
                zz = turn_of[0]
                later(t + 4 + 4 * n + zz, lambda: step(o, zz), self)
                if n < 3:
                    later(t + n + 1, lambda: take_y(n + 1), self)

            def step(o, zz):
                if zz == o:
                    self.last(o, put)
                else:
                    self.hop(o, zz < o, zz)

            later(t, lambda: take_y(0), self)

    class Direct(Reduce):
        def send_term(self, o):
            d = rc(self.cut(self.ry, o), self.zslot(z), self.iz + o, (s, o), self.rz + z)

            def go():
                for c in self.chunks():
                    p = self.ry.at[o] if c is None else self.ry.at[c, o]
                    p[...] = self.term(o, c).astype(BF)
                d.start()

            if place() != o:
                when(None, go)
                pend.append((guard(), d))

        def gather(self, zz, put):
            def go():
                for o in range(4):
                    if o != zz:
                        came(self.zslot(o), self.rz + o)()
                for c in self.chunks():
                    val = self.term(zz, c)
                    for o in range(4):
                        if o != zz:
                            val = val + self.chunk(o, c)[...].astype(F32)
                    put(c, val)

            pl.when(z == zz)(go)

        def schedule(self, put):
            t = ids(8)

            def take_y(n):
                o = (3, 0, 2, 1)[n]
                self.recv_y(o)
                self.send_term(o)
                if n < 3:
                    later(t + n + 1, lambda: take_y(n + 1), self)
                else:
                    zz = turn_of[0]
                    later(t + 4 + zz, lambda: self.gather(zz, put), self)

            later(t, lambda: take_y(0), self)

    def half(yy, width):
        return pl.ds(pl.multiple_of(yy * width, width), width)

    def grad_cols(left, right, g, sy, yy, m, keep):
        width = right.shape[1]
        a = left[:, pl.ds(pl.multiple_of(yy * 512 + 256 * m, 256), 256)]
        val = dot_tn(a, right[...]).reshape(2, 4, 32, width)
        if keep:
            g[2 * m : 2 * m + 2] = val
        else:
            sy[2 * m : 2 * m + 2] = val.astype(BF)

    def grad_rows(left, right, g, sy, yy, per, keep):
        a = left[:, half(yy, 4 * per)]
        val = dot_tn(a, right[...]).reshape(4, per, 1024)
        if keep:
            g[...] = val
        else:
            sy[...] = val.astype(BF)

    red_d = Reduce(R.GD, R.SYD, R.RYD, R.ZD, None)
    red_g0 = Reduce(R.GG, R.WG.at[0], R.RYG, R.ZG, (0, 2))
    red_g1 = Reduce(R.GG, R.WG.at[0], R.RYG, R.ZG, (2, 4))
    red_o = Direct(R.GO, R.WO.at[0], R.RYO, R.ZO, None)

    def put_rows(ref):
        def put(c, val):
            ref[...] = val

        return put

    def put_cols(ref):
        def put(c, val):
            ref[c, 0] = val

        return put

    grad_rows(R.H, R.COT, None, R.SYD, ny, 96, False)
    red_d.send_y()
    sum_dn2 = GroupSum(set_a)
    sum_dn2.run(lambda b: dot_nt(R.DGU[rows(b), :], R.WG[...].reshape(1024, GC)))
    for m, red in ((0, red_g0), (1, red_g1)):
        grad_cols(R.N2, R.DGU, None, R.WG.at[0], ny, m, False)
        red.send_y()
    grad_rows(R.H, R.COT, R.GD, None, y, 96, True)
    red_d.schedule(put_rows(R.GD.at[0]))
    look()
    for m in range(2):
        grad_cols(R.N2, R.DGU, R.GG, None, y, m, True)
    red_g0.schedule(put_cols(R.GG))
    red_g1.schedule(put_cols(R.GG))

    R.GGS[...] = jnp.zeros((16, 128), F32)

    def add_gain(first, row):
        for r in range(8):
            R.GGS[first + r : first + r + 1, :] += row[:, 128 * r : 128 * r + 128]

    for h in range(2):
        cut = slice(128 * h, 128 * h + 128)
        dn2 = sum_dn2.result(h)
        res = R.RES[cut, :]
        rs2 = lax.rsqrt(jnp.mean(res * res, axis=-1, keepdims=True) + norm_eps)
        xh = res * rs2
        gd = dn2 * R.GV[1:2, :]
        add_gain(8, jnp.sum(dn2 * xh, axis=0, keepdims=True))
        dres = R.COT[half_rows(b_me, h), :].astype(F32) + rs2 * (
            gd - xh * jnp.mean(gd * xh, axis=-1, keepdims=True)
        )
        R.DRES[cut, :] = dres
        R.DB[half_rows(b_me, h), :] = dres.astype(BF)
        sh3.send(h)
        later(t_db + h, lambda h=h: sh3.forward(h), sh3)
    sum_dn2.end()
    look()
    sum_out = GroupSum(set_b)
    sum_out.run(lambda b: dot_nn(R.H[rows(b), :], R.WD[...].reshape(768, 1024)))
    look()
    flush(sh3)
    look()
    sh3.finish()

    def da_body(b, c):
        R.DA[rows(b), :] = dot_nt(R.DB[rows(b), :], R.WO[...].reshape(256, 1024)).astype(BF)
        return c

    lax.fori_loop(0, 4, da_body, 0)
    grad_rows(R.O, R.DB, None, R.WO.at[0], ny, 32, False)
    red_o.send_y()
    grad_rows(R.O, R.DB, R.GO, None, y, 32, True)
    red_o.schedule(put_rows(R.GO.at[0]))
    look()
    i_out, r_out = snd(2), rcv(2)
    for h in range(2):
        cut = slice(128 * h, 128 * h + 128)
        R.OUT[cut, :] = (R.RES[cut, :] + sum_out.result(h)).astype(BF)
        part = pl.ds(128 * h, 128)
        route(R.OUT.at[part], o_block.at[part], i_out + h, at_home, home, r_out + h)
    sum_out.end()
    R.DK[...] = jnp.zeros((1024, 256), F32)
    R.DV[...] = jnp.zeros((1024, 256), F32)

    def back_body(h, c):
        pair, low_mine, mine = head_parts(h)
        for i in range(4):
            n = BLK * (i + 1)
            do = R.DA[BLK * i : n, pair] * low_mine
            q = R.QS[BLK * i : n, pair] * low_mine
            dp = dot_nt(do, R.V[0:n, pair])
            pb = PB[i][h]
            p = pb.astype(F32)
            delta = jnp.sum(p * dp, axis=-1, keepdims=True)
            ds = (p * (dp - delta)).astype(BF)
            dq = dot_nn(ds, R.KR[0:n, pair]) * (0.125 * mine)
            R.DQ[BLK * i : n, pair] += dq.astype(BF)
            R.DK[0:n, pair] += dot_tn(ds, q)
            R.DV[0:n, pair] += dot_tn(pb, do)
        return c

    def pair_lanes(p):
        return pl.ds(384 * p, 384)

    def grad_pair(p, sy, yy, keep):
        for m in range(2):
            a = R.N1[:, pl.ds(pl.multiple_of(yy * 512 + 256 * m, 256), 256)]
            val = dot_tn(a, R.DQKV[:, pair_lanes(p)]).reshape(2, 4, 32, 384)
            if keep:
                R.GQ[2 * m : 2 * m + 2, :, :, pair_lanes(p)] = val
            else:
                sy[2 * m : 2 * m + 2] = val.astype(BF)

    red_q, i_gf, r_gf = [], snd(8), rcv(8)
    for p in range(2):
        sy = R.WG.at[1, :, :, :, pair_lanes(p)]
        cut = [r.at[:, :, :, pair_lanes(p)] for r in (R.GQ, R.RYQ, R.ZQ)]
        red_q.append(Reduce(cut[0], sy, cut[1], cut[2], (0, 4)))
    R.DQ[...] = jnp.zeros((1024, 256), BF)
    for p in range(2):
        for h in (2 * p, 2 * p + 1):
            lax.fori_loop(h, h + 1, back_body, 0)
            look()

        def dqkv_body(b, c):
            cs, sn = R.COS[rows(b), :], R.SIN[rows(b), :]
            sl = slice(128 * p, 128 * p + 128)
            u = R.DQ[rows(b), sl].astype(F32)
            R.DQKV[rows(b), 384 * p : 384 * p + 128] = (u * cs - turn(u) * sn).astype(BF)
            u = R.DK[rows(b), sl].astype(BF).astype(F32)
            R.DQKV[rows(b), 384 * p + 128 : 384 * p + 256] = (u * cs - turn(u) * sn).astype(BF)
            R.DQKV[rows(b), 384 * p + 256 : 384 * p + 384] = (
                0.5 * R.DV[rows(b), sl].astype(BF).astype(F32)
            ).astype(BF)
            return c

        lax.fori_loop(0, 4, dqkv_body, 0)
        grad_pair(p, red_q[p].sy, ny, False)
        red_q[p].send_y()
        for b in range(4):
            self_b = (j == z) & (z == b)
            src = R.DQKV.at[pl.ds(256 * b, 256), pl.ds(384 * p + 256, 128)]
            dst = o_gfv.at[:, pl.ds(pl.multiple_of(128 * (j + 4 * p), 128), 128)]
            route(src, dst, i_gf + 2 * b + p, self_b, (4 * y + z, b), r_gf + 2 * j + p)
        if p == 0:
            grad_pair(p, None, y, True)
            red_q[p].schedule(put_cols(red_q[p].g))
    sum_dn1 = GroupSum(set_a)
    sum_dn1.run(lambda b: dot_nt(R.DQKV[rows(b), :], R.WA[...].reshape(1024, QC)))
    grad_pair(1, None, y, True)
    red_q[1].schedule(put_cols(red_q[1].g))
    look()

    i_gtok, r_gtok = snd(2), rcv(2)
    for h in range(2):
        cut = slice(128 * h, 128 * h + 128)
        dn1 = sum_dn1.result(h)
        xs = R.TOK[cut, :].astype(F32)
        rs1 = lax.rsqrt(jnp.mean(xs * xs, axis=-1, keepdims=True) + norm_eps)
        xh = xs * rs1
        gd = dn1 * R.GV[0:1, :]
        add_gain(0, jnp.sum(dn1 * xh, axis=0, keepdims=True))
        R.XSB[cut, :] = (
            R.DRES[cut, :] + rs1 * (gd - xh * jnp.mean(gd * xh, axis=-1, keepdims=True))
        ).astype(BF)
        part = pl.ds(128 * h, 128)
        route(R.XSB.at[part], o_gtok.at[part], i_gtok + h, at_home, home, r_gtok + h)
    sum_dn1.end()

    i_ggg, i_ggy, i_ggz = snd(4), snd(), snd(4)
    r_ggg, r_ggy, r_ggz = rcv(4), rcv(), rcv(4)
    for c in range(4):
        start(
            rc(R.GGS, R.GGR.at[(j - c - 1) % 4], i_ggg + c, group_dev(c, z), r_ggg + j), j != c
        )
    look()
    for c in range(4):
        when(j != c, came(R.GGR.at[(c - j - 1) % 4], r_ggg + c))
    R.GGT[...] = R.GGS[...] + R.GGR[0] + R.GGR[1] + R.GGR[2]
    start(rc(R.GGT, R.GGY, i_ggy, yp, r_ggy))
    look()
    came(R.GGY, r_ggy)()
    R.GGZ[z] = R.GGT[...] + R.GGY[...]
    for c in range(4):
        start(rc(R.GGZ.at[z], R.GGZ.at[z], i_ggz + c, (s, c), r_ggz + z), z != c)

    i_rg, i_rq, r_rg, r_rq = snd(4), snd(4), rcv(4), rcv(4)
    outs = []

    def hand_back(g, send, out, base, r):
        for c in range(4):
            send[c] = g[c, 0].astype(BF)
            start(rc(send.at[c], out.at[j], base + c, group_dev(c, z), r + j), j != c)
        outs.append(local(send.at[j], out.at[j]))

    look()
    for red in (red_d, red_g0, red_g1):
        flush(red)
    hand_back(R.GG, R.RYG.at[0], o_gg, i_rg, r_rg)
    outs.append(local(R.GD.at[0], o_gd))
    flush()
    hand_back(R.GQ, R.RYQ.at[0], o_gq, i_rq, r_rq)
    outs.append(local(R.GO.at[0], o_go))
    for c in range(4):
        when(z != c, came(R.GGZ.at[c], r_ggz + c))
    R.GGY[...] = R.GGZ[0] + R.GGZ[1] + R.GGZ[2] + R.GGZ[3]
    outs.append(local(R.GGY, o_gain))

    for h in range(2):
        part = pl.ds(128 * h, 128)
        arrive(R.OUT.at[part], o_block.at[part], r_out + h, away_self)
        arrive(R.XSB.at[part], o_gtok.at[part], r_gtok + h, away_self)
    for c in range(4):
        self_c = (j == z) & (j == c)
        for h in range(2):
            src = R.DQKV.at[pl.ds(256 * z, 256), pl.ds(384 * h + 256, 128)]
            dst = o_gfv.at[:, pl.ds(pl.multiple_of(128 * (c + 4 * h), 128), 128)]
            arrive(src, dst, r_gf + 2 * c + h, self_c)
    wait_group(r_rg, lambda c: o_gg.at[c])
    wait_group(r_rq, lambda c: o_gq.at[c])
    for d in outs:
        d.wait()
    for cond, desc in pend:
        when(cond, desc.wait_send)


def fast_device(
    tokens,
    first_values,
    gain_attn,
    w_query,
    w_key,
    w_value,
    w_out,
    gain_ffn,
    w_gate,
    w_up,
    w_down,
    segment_start,
    cotangent,
):
    d = lax.axis_index("seq") * 4 + lax.axis_index("ctx")
    mine = jnp.arange(1024, dtype=jnp.int32) // 32 == d

    def spot(g):
        return jnp.where(mine, jnp.tile(g.astype(F32), 32), 0.0).reshape(8, 128)

    starts = jnp.pad(segment_start.astype(F32).reshape(2, 128), ((0, 6), (0, 0)))
    small = jnp.concatenate([spot(gain_attn), spot(gain_ffn), starts])
    hbm = pl.BlockSpec(memory_space=pl.ANY)
    vmem = pl.BlockSpec(memory_space=pltpu.VMEM)
    outs = pl.pallas_call(
        layer_kernel,
        name="layer",
        out_shape=[
            jax.ShapeDtypeStruct((256, 1024), BF),
            jax.ShapeDtypeStruct((256, 1024), BF),
            jax.ShapeDtypeStruct((256, 1024), BF),
            jax.ShapeDtypeStruct((4, 32, QC), BF),
            jax.ShapeDtypeStruct((4, 32, GC), BF),
            jax.ShapeDtypeStruct((32, 1024), F32),
            jax.ShapeDtypeStruct((96, 1024), F32),
            jax.ShapeDtypeStruct((16, 128), F32),
        ],
        in_specs=[hbm] * 11,
        out_specs=[hbm] * 8,
        scratch_shapes=[pltpu.VMEM(shape, dtype) for shape, dtype in SCRATCH.values()]
        + [
            pltpu.SemaphoreType.DMA((N_SEND,)),
            pltpu.SemaphoreType.DMA((N_RECV,)),
            pltpu.SemaphoreType.DMA((20,)),
        ],
        compiler_params=pltpu.CompilerParams(
            collective_id=0, has_side_effects=True, vmem_limit_bytes=VMEM_LIMIT
        ),
    )(
        tokens,
        first_values,
        cotangent,
        small,
        w_query,
        w_key,
        w_value,
        w_gate,
        w_up,
        w_out,
        w_down,
    )
    res = pl.pallas_call(
        finish_kernel,
        name="finish",
        out_shape=[
            jax.ShapeDtypeStruct((256, 1024), BF),
            jax.ShapeDtypeStruct((256, 1024), BF),
            jax.ShapeDtypeStruct((256, 1024), BF),
            jax.ShapeDtypeStruct((1, 32), F32),
            jax.ShapeDtypeStruct((32, 1024), F32),
            jax.ShapeDtypeStruct((32, 1024), F32),
            jax.ShapeDtypeStruct((32, 1024), F32),
            jax.ShapeDtypeStruct((32, 1024), F32),
            jax.ShapeDtypeStruct((1, 32), F32),
            jax.ShapeDtypeStruct((32, 2816), F32),
            jax.ShapeDtypeStruct((32, 2816), F32),
            jax.ShapeDtypeStruct((88, 1024), F32),
        ],
        in_specs=[vmem] * 8,
        out_specs=[vmem] * 12,
        compiler_params=pltpu.CompilerParams(vmem_limit_bytes=64 * 2**20),
    )(*outs)
    return tuple(r.reshape(32) if n in (3, 8) else r for n, r in enumerate(res))


def solution(mesh):
    fits = mesh.shape["seq"] == 8 and mesh.shape["ctx"] == 4
    return jax.shard_map(
        fast_device if fits else per_device,
        mesh=mesh,
        in_specs=(
            P(("seq", "ctx"), None),
            P(("seq", "ctx"), None),
            P(("seq", "ctx")),
            P(("seq", "ctx"), None),
            P(("seq", "ctx"), None),
            P(("seq", "ctx"), None),
            P(("seq", "ctx"), None),
            P(("seq", "ctx")),
            P(("seq", "ctx"), None),
            P(("seq", "ctx"), None),
            P(("seq", "ctx"), None),
            P(("seq", "ctx")),
            P(("seq", "ctx"), None),
        ),
        out_specs=(
            P(("seq", "ctx"), None),
            P(("seq", "ctx"), None),
            P(("seq", "ctx"), None),
            P(("seq", "ctx")),
            P(("seq", "ctx"), None),
            P(("seq", "ctx"), None),
            P(("seq", "ctx"), None),
            P(("seq", "ctx"), None),
            P(("seq", "ctx")),
            P(("seq", "ctx"), None),
            P(("seq", "ctx"), None),
            P(("seq", "ctx"), None),
        ),
        check_vma=False,
    )
```
